32 devices in a mesh: parts: 2 (over x), seq: 16 (over z, y, core).
Axes of the slice: x: 2, y: 2, z: 4, core: 2. Of those that a mesh axis runs over, the one named last changes fastest.
Arguments:
- x_state: bfloat16 [32, 64, 384], P(('parts', 'seq')), parts along dimension 0, may hold values from -6 to 6
- noise_field: bfloat16 [32, 64, 384], P(('parts', 'seq')), parts along dimension 0, may hold values from -6 to 6
- rotations: float32 [9, 32, 64], P(None, ('parts', 'seq')), parts along dimension 1, may hold values from -1 to 1, as said below
- translations: float32 [3, 32, 64], P(None, ('parts', 'seq')), parts along dimension 1, may hold values from -15 to 15
- residue_types: int32 [128], P('parts'), parts along dimension 0, may hold values from 0 to 20
- pocket_mask: int32 [128], P('parts'), parts along dimension 0, may hold values 0 or 1
- type_table: bfloat16 [21, 384], replicated, may hold values from -3 to 3
- null_embed: bfloat16 [384], replicated, may hold values from -3 to 3
- spatial_gain: float32 [384], replicated, may hold values from 0.25 to 1.75
- spatial_proj: bfloat16 [384, 1152], replicated, may hold values from -0.3125 to 0.3125
- spatial_points: bfloat16 [384, 288], replicated, may hold values from -0.3125 to 0.3125
- spatial_gamma: float32 [12], replicated, may hold values from 0.2 to 2
- spatial_out: bfloat16 [384, 384], replicated, may hold values from -0.3125 to 0.3125
- temporal_gain: float32 [384], replicated, may hold values from 0.25 to 1.75
- temporal_proj: bfloat16 [384, 1152], replicated, may hold values from -0.3125 to 0.3125
- temporal_out: bfloat16 [384, 384], replicated, may hold values from -0.3125 to 0.3125
- hidden_gain: float32 [384], replicated, may hold values from 0.25 to 1.75
- hidden_in: bfloat16 [384, 1536], replicated, may hold values from -0.3125 to 0.3125
- hidden_out: bfloat16 [1536, 384], replicated, may hold values from -0.15625 to 0.15625
- head_gain: float32 [384], replicated, may hold values from 0.25 to 1.75
- head_out: bfloat16 [384, 384], replicated, may hold values from -0.3125 to 0.3125
Outputs:
- x_next: bfloat16 [32, 64, 384], P(('parts', 'seq')), parts along dimension 0
- velocity: bfloat16 [32, 64, 384], P(('parts', 'seq')), parts along dimension 0
The draws below stay inside these ranges and needn't reach their ends.
There are 2 independent parts, one for each index of `parts`. The reference program is written for one: setup_inputs(seed, part) draws one part's arguments, and reference() takes and returns one part's arrays. A program takes and returns all parts, laid end to end along the dimension named above; an argument that names none is the same for every part. Nothing has to cross between parts.
Inputs may be any that keep to these rules, and one draw needn't show every extreme that they name: `rotations`: each column over the first dimension is a proper rotation matrix, row-major.
All inputs are finite; a program needn't handle non-finite values.
Results may differ from the reference program's by a relative error of at most 0.015.
Values may be sent and summed in bfloat16 or wider, within the bound.
No kernel may reach another device: no remote copies, remote signals or barrier semaphores. Data moves between devices by JAX's collectives and lax.ppermute only.
A program may use at most 64 MiB of HBM per device.

```python
import math
import jax
import jax.numpy as jnp
from jax import lax

WIDTH = 384
FEED_WIDTH = 1536
SHEADS = 12
THEADS = 6
POINTS = 4
TYPES = 21
FRAMES = 16
RESIDUES = 64


def draw_rotations(key, part):
    raw = jax.random.normal(key, (4, FRAMES, RESIDUES), jnp.float32)
    first = 1.0 + jnp.abs(raw[0])
    second = raw[1]
    third = raw[2]
    fourth = raw[3]
    length = jnp.sqrt(first * first + second * second + third * third + fourth * fourth)
    first = first / length
    second = second / length
    third = third / length
    fourth = fourth / length
    entries = [1.0 - 2.0 * (third * third + fourth * fourth), 2.0 * (second * third - first * fourth), 2.0 * (second * fourth + first * third), 2.0 * (second * third + first * fourth), 1.0 - 2.0 * (second * second + fourth * fourth), 2.0 * (third * fourth - first * second), 2.0 * (second * fourth - first * third), 2.0 * (third * fourth + first * second), 1.0 - 2.0 * (second * second + third * third)]
    return jnp.stack(entries)


def draw_translations(key, part):
    base = jax.random.normal(key, (3, FRAMES, RESIDUES), jnp.float32)
    values = 0.8 * base
    return jnp.clip(values, -15.0, 15.0)


def set_ends(values, key, smallest, largest):
    shape = values.shape
    place = [jax.random.randint(jax.random.fold_in(key, axis), (), 0, shape[axis]) for axis in range(len(shape))]
    values = values.at[tuple(place)].set(smallest)
    longest = shape.index(max(shape))
    place[longest] = (place[longest] + 1) % shape[longest]
    return values.at[tuple(place)].set(largest)


def block_levels(rng, shape, cuts, least, top_value):
    gain, own = 1.0, jax.random.fold_in(rng, 6)
    for dim, parts in cuts:
        heights = jnp.exp(jax.random.uniform(jax.random.fold_in(own, dim), (parts,), jnp.float32, least / len(cuts), top_value / len(cuts)))
        gain = gain * jnp.repeat(heights, shape[dim] // parts).reshape([-1 if axis == dim else 1 for axis in range(len(shape))])
    return gain


def noise(stream_key, shape, deviation, reach, shards=(), kind=jnp.bfloat16):
    array = jax.random.normal(stream_key, shape, jnp.float32) * deviation
    if len(shards) > 0:
        array = block_levels(stream_key, shape, shards, -0.22, 0.18) * array
    return jnp.clip(array, min=-reach, max=reach).astype(kind)


def setup_inputs(seed: int = 0, part: int = 0) -> dict:
    splits = jax.random.split(jax.random.key(seed), 22)
    part_splits = jax.random.split(jax.random.fold_in(splits[21], part), 22)
    return {
        "x_state": noise(part_splits[0], (FRAMES, RESIDUES, WIDTH), 1.0, 6.0, ((0, 16),)),
        "noise_field": noise(part_splits[1], (FRAMES, RESIDUES, WIDTH), 1.0, 6.0, ((0, 16),)),
        "rotations": draw_rotations(jax.random.fold_in(jax.random.fold_in(splits[21], part), 71), part),
        "translations": draw_translations(jax.random.fold_in(jax.random.fold_in(splits[21], part), 71), part),
        "residue_types": set_ends(jax.random.randint(part_splits[4], (RESIDUES,), 0, TYPES), jax.random.fold_in(part_splits[4], 1), 0, TYPES - 1).astype(jnp.int32),
        "pocket_mask": set_ends((jax.random.randint(part_splits[5], (RESIDUES,), 0, 4) < 3).astype(jnp.int32), jax.random.fold_in(part_splits[5], 1), 0, 1),
        "type_table": noise(splits[6], (TYPES, WIDTH), 0.5, 3.0),
        "null_embed": noise(splits[7], (WIDTH,), 0.5, 3.0),
        "spatial_gain": jnp.clip(1.0 + 0.15 * jax.random.normal(splits[8], (WIDTH,), jnp.float32), 0.25, 1.75),
        "spatial_proj": noise(splits[9], (WIDTH, 3 * WIDTH), WIDTH ** -0.5, 0.3125),
        "spatial_points": noise(splits[10], (WIDTH, 2 * SHEADS * POINTS * 3), WIDTH ** -0.5, 0.3125),
        "spatial_gamma": jnp.clip(jnp.exp(jax.random.uniform(splits[11], (SHEADS,), jnp.float32, math.log(0.2), math.log(2.0))), 0.2, 2.0),
        "spatial_out": noise(splits[12], (WIDTH, WIDTH), WIDTH ** -0.5, 0.3125),
        "temporal_gain": jnp.clip(1.0 + 0.15 * jax.random.normal(splits[13], (WIDTH,), jnp.float32), 0.25, 1.75),
        "temporal_proj": noise(splits[14], (WIDTH, 3 * WIDTH), WIDTH ** -0.5, 0.3125),
        "temporal_out": noise(splits[15], (WIDTH, WIDTH), WIDTH ** -0.5, 0.3125),
        "hidden_gain": jnp.clip(1.0 + 0.15 * jax.random.normal(splits[16], (WIDTH,), jnp.float32), 0.25, 1.75),
        "hidden_in": noise(splits[17], (WIDTH, FEED_WIDTH), WIDTH ** -0.5, 0.3125),
        "hidden_out": noise(splits[18], (FEED_WIDTH, WIDTH), FEED_WIDTH ** -0.5, 0.15625),
        "head_gain": jnp.clip(1.0 + 0.15 * jax.random.normal(splits[19], (WIDTH,), jnp.float32), 0.25, 1.75),
        "head_out": noise(splits[20], (WIDTH, WIDTH), WIDTH ** -0.5, 0.3125),
    }


WEIGHT_LOGIT = 0.7071067811865476
WEIGHT_POINT = 0.23570226039551584
GUIDE = 2.0
STEP_SIZE = 0.25
NOISE_SCALE = 0.2
EPSILON = 1e-05

def layer_norm(values, scale_gain):
    average = lax.optimization_barrier(jnp.mean(values, axis=-1, keepdims=True))
    centered = values - average
    spread = lax.optimization_barrier(jnp.mean(centered * centered, axis=-1, keepdims=True))
    return centered * lax.rsqrt(spread + EPSILON) * scale_gain

def softmax_rows(logits):
    row_max = lax.optimization_barrier(jnp.max(logits, axis=-1, keepdims=True))
    powers = jnp.exp(logits - row_max)
    return powers / lax.optimization_barrier(jnp.sum(powers, axis=-1, keepdims=True))

def branch_embed(residue_types, type_table, null_embed):
    count = type_table.shape[0]
    onehot = (residue_types[:, None] == jnp.arange(count, dtype=jnp.int32)[None, :]).astype(jnp.bfloat16)
    conditional = jnp.dot(onehot, type_table, preferred_element_type=jnp.float32)
    empty = jnp.broadcast_to(null_embed.astype(jnp.float32)[None, :], conditional.shape)
    return jnp.stack([conditional, empty])

def spatial_frame(state, rotation, translation, embedding, allowed, weights):
    spatial_gain, spatial_proj, spatial_points, spatial_gamma, spatial_out = weights
    branches, residues, model_width = embedding.shape
    head_count = spatial_gamma.shape[0]
    head_dim = model_width // head_count
    initial = state.astype(jnp.float32)[None] + embedding
    normed = layer_norm(initial, spatial_gain).astype(jnp.bfloat16).reshape(branches * residues, model_width)
    projected = jnp.dot(normed, spatial_proj, preferred_element_type=jnp.float32).astype(jnp.bfloat16)
    projected = projected.reshape(branches, residues, 3, head_count, head_dim).astype(jnp.float32)
    points = jnp.dot(normed, spatial_points, preferred_element_type=jnp.float32)
    points = points.reshape(branches, residues, 2, head_count, -1, 3)
    centred = translation - lax.optimization_barrier(jnp.mean(translation, axis=1, keepdims=True))
    turned = jnp.einsum('der,brshpe->bshpdr', rotation.reshape(3, 3, residues), points, precision=lax.Precision.HIGHEST)
    placed = turned + centred
    query_points = placed[:, 0].reshape(branches, head_count, -1, residues)
    key_points = placed[:, 1].reshape(branches, head_count, -1, residues)
    pairwise = jnp.einsum('bhcr,bhcs->bhrs', query_points, key_points, precision=lax.Precision.HIGHEST)
    query_norm = lax.optimization_barrier(jnp.sum(query_points * query_points, axis=2))
    key_norm = lax.optimization_barrier(jnp.sum(key_points * key_points, axis=2))
    distance = query_norm[..., :, None] + key_norm[..., None, :] - 2.0 * pairwise
    scalar = jnp.einsum('brhc,bshc->bhrs', projected[:, :, 0], projected[:, :, 1])
    logits = WEIGHT_LOGIT * scalar / jnp.sqrt(jnp.float32(head_dim)) - 0.5 * WEIGHT_LOGIT * WEIGHT_POINT * spatial_gamma[None, :, None, None] * distance
    logits = jnp.where(allowed[None, None], logits, -jnp.inf)
    attend = softmax_rows(logits).astype(jnp.bfloat16).astype(jnp.float32)
    context = jnp.einsum('bhrs,bshc->brhc', attend, projected[:, :, 2]).astype(jnp.bfloat16)
    update = jnp.dot(context.reshape(branches * residues, model_width), spatial_out, preferred_element_type=jnp.float32)
    return (initial + update.reshape(branches, residues, model_width)).astype(jnp.bfloat16)

def temporal_block(states, weights):
    temporal_gain, temporal_proj, temporal_out, hidden_gain, hidden_in, hidden_out = weights
    frames, branches, residues, model_width = states.shape
    head_dim = model_width // THEADS
    initial = states.astype(jnp.float32)
    normed = layer_norm(initial, temporal_gain).astype(jnp.bfloat16).reshape(-1, model_width)
    projected = jnp.dot(normed, temporal_proj, preferred_element_type=jnp.float32).astype(jnp.bfloat16)
    projected = projected.reshape(frames, branches, residues, 3, THEADS, head_dim).astype(jnp.float32)
    scores = jnp.einsum('qbrhc,kbrhc->brhqk', projected[:, :, :, 0], projected[:, :, :, 1]) / jnp.sqrt(jnp.float32(head_dim))
    attend = softmax_rows(scores).astype(jnp.bfloat16).astype(jnp.float32)
    context = jnp.einsum('brhqk,kbrhc->qbrhc', attend, projected[:, :, :, 2]).astype(jnp.bfloat16)
    after_time = initial + jnp.dot(context.reshape(-1, model_width), temporal_out, preferred_element_type=jnp.float32).reshape(states.shape)
    second = layer_norm(after_time, hidden_gain).astype(jnp.bfloat16).reshape(-1, model_width)
    feed_hidden = jax.nn.gelu(jnp.dot(second, hidden_in, preferred_element_type=jnp.float32)).astype(jnp.bfloat16)
    result = after_time + jnp.dot(feed_hidden, hidden_out, preferred_element_type=jnp.float32).reshape(states.shape)
    return result.astype(jnp.bfloat16)

def velocity_head(states, head_gain, head_out):
    model_width = states.shape[-1]
    normed = layer_norm(states.astype(jnp.float32), head_gain).astype(jnp.bfloat16).reshape(-1, model_width)
    branch_velocity = jnp.dot(normed, head_out, preferred_element_type=jnp.float32).reshape(states.shape)
    guided = branch_velocity[:, 1] + GUIDE * (branch_velocity[:, 0] - branch_velocity[:, 1])
    return guided.astype(jnp.bfloat16)

def reference(x_state, noise_field, rotations, translations, residue_types, pocket_mask, type_table, null_embed, spatial_gain, spatial_proj, spatial_points, spatial_gamma, spatial_out, temporal_gain, temporal_proj, temporal_out, hidden_gain, hidden_in, hidden_out, head_gain, head_out):
    embedding = branch_embed(residue_types, type_table, null_embed)
    residues = x_state.shape[1]
    allowed = (pocket_mask[None, :] == 1) | jnp.eye(residues, dtype=bool)
    spatial_weights = (spatial_gain, spatial_proj, spatial_points, spatial_gamma, spatial_out)
    time_weights = (temporal_gain, temporal_proj, temporal_out, hidden_gain, hidden_in, hidden_out)

    def one_frame(pieces):
        return spatial_frame(pieces[0], pieces[1], pieces[2], embedding, allowed, spatial_weights)
    spatial = lax.map(one_frame, (x_state, jnp.moveaxis(rotations, 1, 0), jnp.moveaxis(translations, 1, 0)))
    per_residue = jnp.moveaxis(spatial, 2, 0)

    def one_residue(column):
        return temporal_block(column[:, :, None, :], time_weights)[:, :, 0, :]
    mixed = jnp.moveaxis(lax.map(one_residue, per_residue), 0, 2)
    velocity = velocity_head(mixed, head_gain, head_out)
    x_next = (x_state.astype(jnp.float32) + STEP_SIZE * velocity.astype(jnp.float32) + NOISE_SCALE * noise_field.astype(jnp.float32)).astype(jnp.bfloat16)
    return (x_next, velocity)
```

```python
import functools
import math

import jax
import jax.numpy as jnp
from jax import lax
from jax.experimental import pallas as pl
from jax.experimental.pallas import tpu as pltpu
from jax.sharding import PartitionSpec as P

THEADS = 6
BRANCHES = 2

WEIGHT_LOGIT = 0.7071067811865476
WEIGHT_POINT = 0.23570226039551584
GUIDE = 2.0
STEP_SIZE = 0.25
NOISE_SCALE = 0.2
EPSILON = 1e-05

BF16 = jnp.bfloat16
F32 = jnp.float32
LANES = 128
NT = (((1,), (1,)), ((), ()))


def round_up(value, step):
    return -(-value // step) * step


def layer_norm(values, scale_gain):
    average = jnp.mean(values, axis=-1, keepdims=True)
    centered = values - average
    spread = jnp.mean(centered * centered, axis=-1, keepdims=True)
    return centered * lax.rsqrt(spread + EPSILON) * scale_gain


def matmul(left, right):
    return jnp.dot(left, right, preferred_element_type=F32)


def iota(shape, axis):
    return lax.broadcasted_iota(jnp.int32, shape, axis)


def softmax_down(logits, allowed):
    logits = jnp.where(allowed, logits, -jnp.inf)
    powers = jnp.exp(logits - jnp.max(logits, axis=0, keepdims=True))
    return (powers * (1.0 / jnp.sum(powers, axis=0, keepdims=True))).astype(BF16)


def spatial_kernel(
    groups,
    gamma_ref,
    x_ref,
    rotation_ref,
    translation_ref,
    types_ref,
    mask_ref,
    table_ref,
    null_ref,
    gain_ref,
    proj_ref,
    points_ref,
    spatial_out_ref,
    out_ref,
    columns_ref,
    wide_ref,
    rows_ref,
):
    frames, residues, width = x_ref.shape
    heads = gamma_ref.shape[0]
    head_dim = width // heads
    block_heads = LANES // head_dim
    all_points = points_ref.shape[1]
    half = all_points // 2
    per_head = half // heads
    points_wide = wide_ref.shape[1]
    feature = round_up(half + 2 * heads, LANES)
    share = residues // groups
    fold = max(residues, LANES)
    point_scale = 0.5 * WEIGHT_LOGIT * WEIGHT_POINT

    kinds = table_ref.shape[0]
    onehot = (iota((kinds, residues), 0) == types_ref[...]).astype(F32).T.astype(BF16)
    conditional = matmul(onehot, table_ref[...])
    empty = null_ref[...].astype(F32)

    lane = iota((1, points_wide), 1)
    component = lane % 3
    narrow = iota((1, feature), 1)
    in_points = narrow < half
    in_first = (narrow >= half) & (narrow < half + heads)
    in_second = (narrow >= half + heads) & (narrow < half + 2 * heads)
    member = []
    gamma_lanes = jnp.zeros((1, feature), F32)
    for head in range(heads):
        own = (
            ((narrow >= head * per_head) & (narrow < (head + 1) * per_head))
            | (narrow == half + head)
            | (narrow == half + heads + head)
        )
        member.append(own.astype(F32).astype(BF16))
        gamma_lanes = jnp.where(own, gamma_ref[head], gamma_lanes)
    block_lane = iota((1, LANES), 1)
    block_member = [
        ((block_lane >= part * head_dim) & (block_lane < (part + 1) * head_dim))
        .astype(F32)
        .astype(BF16)
        for part in range(block_heads)
    ]
    row_point = iota((feature, feature), 0)
    column = iota((feature, feature), 1)
    column_head = jnp.where(column >= half + heads, column - half - heads, column - half)
    gather_norm = (
        (
            (column >= half)
            & (column < half + 2 * heads)
            & (row_point >= column_head * per_head)
            & (row_point < (column_head + 1) * per_head)
        )
        .astype(F32)
        .astype(BF16)
    )
    diagonal = iota((LANES, block_heads * residues), 0) // head_dim == (
        iota((LANES, block_heads * residues), 1) // residues
    )

    for frame in range(frames):
        columns_ref[...] = jnp.zeros_like(columns_ref)
        columns_ref[0:9, :] = rotation_ref[:, frame, :]
        moved = translation_ref[:, frame, :]
        columns_ref[9:12, :] = moved - jnp.mean(moved, axis=1, keepdims=True)
        columns_ref[12:13, :] = mask_ref[...].astype(F32)
        columns = columns_ref[...].T
        allowed = (columns[:, 12:13] == 1.0) | (
            iota((residues, residues), 0) == iota((residues, residues), 1)
        )
        allowed = (
            (columns[:, 12:13] == 1.0)
            | (
                iota((residues, block_heads * residues), 0)
                == iota((residues, block_heads * residues), 1) % residues
            )
        )

        state = x_ref[frame].astype(F32)
        initial = jnp.concatenate([state + conditional, state + empty], axis=0)
        normed = layer_norm(initial, gain_ref[...]).astype(BF16)
        projected = matmul(normed, proj_ref[...])
        wide_ref[:, points_wide - LANES :] = jnp.zeros((BRANCHES * residues, LANES), F32)
        wide_ref[:, :all_points] = matmul(normed, points_ref[...])
        points = wide_ref[...]

        placed = None
        for step in range(-2, 3):
            factor = jnp.zeros((residues, points_wide), F32)
            for row in range(3):
                if 0 <= row + step < 3:
                    entry = 3 * row + row + step
                    factor = jnp.where(component == row, columns[:, entry : entry + 1], factor)
            shifted = points if step == 0 else pltpu.roll(points, (-step) % points_wide, 1)
            term = shifted.reshape(BRANCHES, residues, points_wide) * factor[None]
            placed = term if placed is None else placed + term
        anchor = jnp.zeros((residues, points_wide), F32)
        for row in range(3):
            anchor = jnp.where(component == row, columns[:, 9 + row : 10 + row], anchor)
        placed = (placed + anchor[None]).reshape(BRANCHES * residues, points_wide)

        query_points = placed[:, :feature]
        key_points = jnp.where(
            in_points, pltpu.roll(placed, points_wide - half, 1)[:, :feature], 0.0
        )
        query_feature = jnp.where(
            in_points,
            query_points * (gamma_lanes * (2.0 * point_scale)),
            (in_first | in_second).astype(F32),
        )
        query_high = query_feature.astype(BF16)
        query_low = (query_feature - query_high.astype(F32)).astype(BF16)

        square = key_points * key_points
        square_high = square.astype(BF16)
        rest = square - square_high.astype(F32)
        square_middle = rest.astype(BF16)
        square_low = (rest - square_middle.astype(F32)).astype(BF16)
        norm = (
            matmul(square_high, gather_norm)
            + matmul(square_middle, gather_norm)
            + matmul(square_low, gather_norm)
        )
        key_feature = key_points - norm * (gamma_lanes * point_scale)
        high = key_feature.astype(BF16)
        rest = key_feature - high.astype(F32)
        low = rest.astype(BF16)
        last = (rest - low.astype(F32)).astype(BF16)
        key_high = jnp.where(in_second, last, high)
        key_low = jnp.where(in_second, jnp.zeros_like(low), low)

        queries = (
            projected[:, :width].astype(BF16) * jnp.asarray(WEIGHT_LOGIT / math.sqrt(head_dim), BF16)
        )
        keys = projected[:, width : 2 * width].astype(BF16)
        values = projected[:, 2 * width :].astype(BF16).astype(F32)

        contexts = []
        for branch in range(BRANCHES):
            rows = slice(branch * residues, (branch + 1) * residues)
            turned = values[rows].T.astype(BF16)
            pieces = []
            for block in range(width // LANES):
                lanes = slice(block * LANES, (block + 1) * LANES)
                left = jnp.concatenate(
                    [keys[rows, lanes], key_high[rows], key_low[rows], key_high[rows]], axis=1
                )
                stacked = []
                for part in range(block_heads):
                    own = member[block * block_heads + part]
                    upper = query_high[rows] * own
                    stacked.append(
                        jnp.concatenate(
                            [
                                queries[rows, lanes] * block_member[part],
                                upper,
                                upper,
                                query_low[rows] * own,
                            ],
                            axis=1,
                        )
                    )
                logits = lax.dot_general(
                    left, jnp.concatenate(stacked, axis=0), NT, preferred_element_type=F32
                )
                attend = softmax_down(logits, allowed)
                mixed = jnp.where(diagonal, matmul(turned[lanes], attend), 0.0)
                folded = mixed[:, :fold]
                for start in range(fold, block_heads * residues, fold):
                    folded = folded + mixed[:, start : start + fold]
                pieces.append(folded)
            contexts.append(jnp.concatenate(pieces, axis=0).T.astype(BF16))
        update = matmul(jnp.concatenate(contexts, axis=0), spatial_out_ref[...])
        for branch in range(BRANCHES):
            total = initial[branch * residues : (branch + 1) * residues]
            for start in range(0, fold, residues):
                first = branch * fold + start
                total = total + update[first : first + residues]
            place = (frame * BRANCHES + branch) * share
            for group in range(groups):
                rows_ref[group, place : place + share, :] = total[group * share : (group + 1) * share]
    out_ref[...] = rows_ref[...].astype(BF16)


def temporal_kernel(
    period,
    x_ref,
    gain_ref,
    proj_ref,
    temporal_out_ref,
    hidden_gain_ref,
    hidden_in_ref,
    hidden_out_ref,
    head_gain_ref,
    head_out_ref,
    out_ref,
):
    groups, depth, width = x_ref.shape
    rows = groups * depth
    head_dim = width // THEADS
    block_heads = LANES // head_dim
    share = period // BRANCHES

    initial = x_ref[...].astype(F32).reshape(rows, width)
    normed = layer_norm(initial, gain_ref[...]).astype(BF16)
    projected = matmul(normed, proj_ref[...])
    queries = projected[:, :width].astype(BF16) * jnp.asarray(1.0 / math.sqrt(head_dim), BF16)
    keys = projected[:, width : 2 * width].astype(BF16)
    turned = projected[:, 2 * width :].astype(BF16).astype(F32).T.astype(BF16)
    block_lane = iota((1, LANES), 1)
    allowed = (
        iota((rows, block_heads * rows), 0) % period == iota((rows, block_heads * rows), 1) % period
    )
    pieces = []
    for block in range(width // LANES):
        lanes = slice(block * LANES, (block + 1) * LANES)
        stacked = []
        for part in range(block_heads):
            own = (block_lane >= part * head_dim) & (block_lane < (part + 1) * head_dim)
            stacked.append(queries[:, lanes] * own.astype(F32).astype(BF16))
        logits = lax.dot_general(
            keys[:, lanes], jnp.concatenate(stacked, axis=0), NT, preferred_element_type=F32
        )
        attend = softmax_down(logits, allowed)
        mixed = matmul(turned[lanes], attend)
        for part in range(block_heads):
            pieces.append(
                mixed[part * head_dim : (part + 1) * head_dim, part * rows : (part + 1) * rows]
            )
    context = jnp.concatenate(pieces, axis=0).T.astype(BF16)
    after_time = initial + matmul(context, temporal_out_ref[...])
    second = layer_norm(after_time, hidden_gain_ref[...]).astype(BF16)
    hidden = jax.nn.gelu(matmul(second, hidden_in_ref[...])).astype(BF16)
    result = (after_time + matmul(hidden, hidden_out_ref[...])).astype(BF16).astype(F32)
    headed = layer_norm(result, head_gain_ref[...]).astype(BF16)
    branch_velocity = matmul(headed, head_out_ref[...]).reshape(rows // period, period, width)
    conditional = branch_velocity[:, :share]
    empty = branch_velocity[:, share:]
    out_ref[...] = (empty + GUIDE * (conditional - empty)).astype(BF16)


def whole(memory_space=pltpu.VMEM):
    return pl.BlockSpec(memory_space=memory_space)


def body(
    groups,
    x_state,
    noise_field,
    rotations,
    translations,
    residue_types,
    pocket_mask,
    type_table,
    null_embed,
    spatial_gain,
    spatial_proj,
    spatial_points,
    spatial_gamma,
    spatial_out,
    temporal_gain,
    temporal_proj,
    temporal_out,
    hidden_gain,
    hidden_in,
    hidden_out,
    head_gain,
    head_out,
):
    frames, residues, width = x_state.shape
    share = residues // groups
    period = BRANCHES * share
    spatial = pl.pallas_call(
        functools.partial(spatial_kernel, groups),
        out_shape=jax.ShapeDtypeStruct((groups, frames * period, width), BF16),
        in_specs=[whole(pltpu.SMEM)] + [whole()] * 11,
        out_specs=whole(),
        scratch_shapes=[
            pltpu.VMEM((16, residues), F32),
            pltpu.VMEM((BRANCHES * residues, round_up(spatial_points.shape[1], LANES)), F32),
            pltpu.VMEM((groups, frames * period, width), F32),
        ],
        name="spatial",
    )(
        spatial_gamma,
        x_state,
        rotations,
        translations,
        residue_types[None],
        pocket_mask[None],
        type_table,
        null_embed[None],
        spatial_gain[None],
        spatial_proj,
        spatial_points,
        spatial_out,
    )
    arrived = lax.all_to_all(spatial, "seq", split_axis=0, concat_axis=0, tiled=True)
    guided = pl.pallas_call(
        functools.partial(temporal_kernel, period),
        out_shape=jax.ShapeDtypeStruct((groups * frames, share, width), BF16),
        in_specs=[whole()] * 9,
        out_specs=whole(),
        name="temporal",
    )(
        arrived,
        temporal_gain[None],
        temporal_proj,
        temporal_out,
        hidden_gain[None],
        hidden_in,
        hidden_out,
        head_gain[None],
        head_out,
    )
    velocity = lax.all_to_all(guided, "seq", split_axis=0, concat_axis=1, tiled=True)
    x_next = (
        x_state.astype(F32)
        + STEP_SIZE * velocity.astype(F32)
        + NOISE_SCALE * noise_field.astype(F32)
    ).astype(BF16)
    return (x_next, velocity)


def solution(mesh):
    tokens = P(("parts", "seq"), None, None)
    geometry = P(None, ("parts", "seq"), None)
    return jax.shard_map(
        functools.partial(body, mesh.shape["seq"]),
        mesh=mesh,
        in_specs=(tokens, tokens, geometry, geometry, P("parts"), P("parts")) + (P(),) * 15,
        out_specs=(tokens, tokens),
        check_vma=False,
    )
```

```python
import functools
import math

import jax
import jax.numpy as jnp
from jax import lax
from jax.experimental import pallas as pl
from jax.experimental.pallas import tpu as pltpu
from jax.sharding import PartitionSpec as P

THEADS = 6
BRANCHES = 2

WEIGHT_LOGIT = 0.7071067811865476
WEIGHT_POINT = 0.23570226039551584
GUIDE = 2.0
STEP_SIZE = 0.25
NOISE_SCALE = 0.2
EPSILON = 1e-05

BF16 = jnp.bfloat16
F32 = jnp.float32
LANES = 128
NT = (((1,), (1,)), ((), ()))


def round_up(value, step):
    return -(-value // step) * step


def layer_norm(values, scale_gain):
    average = jnp.mean(values, axis=-1, keepdims=True)
    centered = values - average
    spread = jnp.mean(centered * centered, axis=-1, keepdims=True)
    return centered * lax.rsqrt(spread + EPSILON) * scale_gain


def as_row(ref):
    return ref[...].reshape(1, ref.shape[0])


def matmul(left, right):
    return jnp.dot(left, right, preferred_element_type=F32)


def iota(shape, axis):
    return lax.broadcasted_iota(jnp.int32, shape, axis)


def softmax_down(logits, allowed):
    logits = jnp.where(allowed, logits, -jnp.inf)
    powers = jnp.exp(logits - jnp.max(logits, axis=0, keepdims=True))
    return (powers * (1.0 / jnp.sum(powers, axis=0, keepdims=True))).astype(BF16)


def spatial_kernel(
    groups,
    gamma_ref,
    x_ref,
    rotation_ref,
    translation_ref,
    types_ref,
    mask_ref,
    table_ref,
    null_ref,
    gain_ref,
    proj_ref,
    points_ref,
    spatial_out_ref,
    *refs,
):
    out_refs, (columns_ref, wide_ref) = refs[:groups], refs[groups:]
    frames, residues, width = x_ref.shape
    me = lax.axis_index("seq")
    heads = gamma_ref.shape[0]
    head_dim = width // heads
    block_heads = LANES // head_dim
    all_points = points_ref.shape[0]
    half = all_points // 2
    per_head = half // heads
    points_wide = wide_ref.shape[1]
    feature = round_up(half + 2 * heads, LANES)
    share = residues // groups
    fold = max(residues, LANES)
    point_scale = 0.5 * WEIGHT_LOGIT * WEIGHT_POINT

    kinds = table_ref.shape[0]
    onehot = (iota((kinds, residues), 0) == types_ref[...]).astype(F32).T.astype(BF16)
    conditional = matmul(onehot, table_ref[...])
    empty = as_row(null_ref).astype(F32)

    lane = iota((1, points_wide), 1)
    component = lane % 3
    narrow = iota((1, feature), 1)
    in_points = narrow < half
    in_first = (narrow >= half) & (narrow < half + heads)
    in_second = (narrow >= half + heads) & (narrow < half + 2 * heads)
    member = []
    gamma_lanes = jnp.zeros((1, feature), F32)
    for head in range(heads):
        own = (
            ((narrow >= head * per_head) & (narrow < (head + 1) * per_head))
            | (narrow == half + head)
            | (narrow == half + heads + head)
        )
        member.append(own.astype(F32).astype(BF16))
        gamma_lanes = jnp.where(own, gamma_ref[head], gamma_lanes)
    block_lane = iota((1, LANES), 1)
    block_member = [
        ((block_lane >= part * head_dim) & (block_lane < (part + 1) * head_dim))
        .astype(F32)
        .astype(BF16)
        for part in range(block_heads)
    ]
    row_point = iota((feature, feature), 0)
    column = iota((feature, feature), 1)
    column_head = jnp.where(column >= half + heads, column - half - heads, column - half)
    gather_norm = (
        (
            (column >= half)
            & (column < half + 2 * heads)
            & (row_point >= column_head * per_head)
            & (row_point < (column_head + 1) * per_head)
        )
        .astype(F32)
        .astype(BF16)
    )
    diagonal = iota((LANES, block_heads * residues), 0) // head_dim == (
        iota((LANES, block_heads * residues), 1) // residues
    )

    sent = [[] for _ in range(groups)]
    for frame in range(frames):
        columns_ref[...] = jnp.zeros_like(columns_ref)
        columns_ref[0:9, :] = rotation_ref[:, frame, :]
        moved = translation_ref[:, frame, :]
        columns_ref[9:12, :] = moved - jnp.mean(moved, axis=1, keepdims=True)
        columns_ref[12:13, :] = mask_ref[...].astype(F32)
        columns = columns_ref[...].T
        allowed = (columns[:, 12:13] == 1.0) | (
            iota((residues, residues), 0) == iota((residues, residues), 1)
        )
        allowed = (
            (columns[:, 12:13] == 1.0)
            | (
                iota((residues, block_heads * residues), 0)
                == iota((residues, block_heads * residues), 1) % residues
            )
        )

        state = x_ref[frame].astype(F32)
        initial = jnp.concatenate([state + conditional, state + empty], axis=0)
        normed = layer_norm(initial, as_row(gain_ref)).astype(BF16)
        projected = matmul(normed, proj_ref[...])
        wide_ref[:, points_wide - LANES :] = jnp.zeros((BRANCHES * residues, LANES), F32)
        wide_ref[:, :all_points] = lax.dot_general(
            normed, points_ref[...], NT, preferred_element_type=F32
        )
        points = wide_ref[...]

        placed = None
        for step in range(-2, 3):
            factor = jnp.zeros((residues, points_wide), F32)
            for row in range(3):
                if 0 <= row + step < 3:
                    entry = 3 * row + row + step
                    factor = jnp.where(component == row, columns[:, entry : entry + 1], factor)
            shifted = points if step == 0 else pltpu.roll(points, (-step) % points_wide, 1)
            term = shifted.reshape(BRANCHES, residues, points_wide) * factor[None]
            placed = term if placed is None else placed + term
        anchor = jnp.zeros((residues, points_wide), F32)
        for row in range(3):
            anchor = jnp.where(component == row, columns[:, 9 + row : 10 + row], anchor)
        placed = (placed + anchor[None]).reshape(BRANCHES * residues, points_wide)

        query_points = placed[:, :feature]
        key_points = jnp.where(
            in_points, pltpu.roll(placed, points_wide - half, 1)[:, :feature], 0.0
        )
        query_feature = jnp.where(
            in_points,
            query_points * (gamma_lanes * (2.0 * point_scale)),
            (in_first | in_second).astype(F32),
        )
        query_high = query_feature.astype(BF16)
        query_low = (query_feature - query_high.astype(F32)).astype(BF16)

        square = key_points * key_points
        square_high = square.astype(BF16)
        rest = square - square_high.astype(F32)
        square_middle = rest.astype(BF16)
        square_low = (rest - square_middle.astype(F32)).astype(BF16)
        norm = (
            matmul(square_high, gather_norm)
            + matmul(square_middle, gather_norm)
            + matmul(square_low, gather_norm)
        )
        key_feature = key_points - norm * (gamma_lanes * point_scale)
        high = key_feature.astype(BF16)
        rest = key_feature - high.astype(F32)
        low = rest.astype(BF16)
        last = (rest - low.astype(F32)).astype(BF16)
        key_high = jnp.where(in_second, last, high)
        key_low = jnp.where(in_second, jnp.zeros_like(low), low)

        queries = (
            projected[:, :width].astype(BF16) * jnp.asarray(WEIGHT_LOGIT / math.sqrt(head_dim), BF16)
        )
        keys = projected[:, width : 2 * width].astype(BF16)
        values = projected[:, 2 * width :].astype(BF16).astype(F32)

        contexts = []
        for branch in range(BRANCHES):
            rows = slice(branch * residues, (branch + 1) * residues)
            turned = values[rows].T.astype(BF16)
            pieces = []
            for block in range(width // LANES):
                lanes = slice(block * LANES, (block + 1) * LANES)
                left = jnp.concatenate(
                    [keys[rows, lanes], key_high[rows], key_low[rows], key_high[rows]], axis=1
                )
                stacked = []
                for part in range(block_heads):
                    own = member[block * block_heads + part]
                    upper = query_high[rows] * own
                    stacked.append(
                        jnp.concatenate(
                            [
                                queries[rows, lanes] * block_member[part],
                                upper,
                                upper,
                                query_low[rows] * own,
                            ],
                            axis=1,
                        )
                    )
                logits = lax.dot_general(
                    left, jnp.concatenate(stacked, axis=0), NT, preferred_element_type=F32
                )
                attend = softmax_down(logits, allowed)
                mixed = jnp.where(diagonal, matmul(turned[lanes], attend), 0.0)
                folded = mixed[:, :fold]
                for start in range(fold, block_heads * residues, fold):
                    folded = folded + mixed[:, start : start + fold]
                pieces.append(folded)
            contexts.append(jnp.concatenate(pieces, axis=0).T.astype(BF16))
        update = matmul(jnp.concatenate(contexts, axis=0), spatial_out_ref[...])
        for branch in range(BRANCHES):
            total = initial[branch * residues : (branch + 1) * residues]
            for start in range(0, fold, residues):
                first = branch * fold + start
                total = total + update[first : first + residues]
            total = pltpu.roll(total, residues - me * share, 0)
            for step in range(groups):
                sent[step].append(total[step * share : (step + 1) * share])
    for step in range(groups):
        out_refs[step][...] = jnp.concatenate(sent[step], axis=0).astype(BF16)


def temporal_kernel(groups, period, *refs):
    x_refs, refs = refs[:groups], refs[groups:]
    (
        gain_ref,
        proj_ref,
        temporal_out_ref,
        hidden_gain_ref,
        hidden_in_ref,
        hidden_out_ref,
        head_gain_ref,
        head_out_ref,
    ) = refs[:8]
    out_refs = refs[8:]
    depth, width = x_refs[0].shape
    rows = groups * depth
    head_dim = width // THEADS
    block_heads = LANES // head_dim
    share = period // BRANCHES

    initial = jnp.concatenate([x_ref[...].astype(F32) for x_ref in x_refs], axis=0)
    normed = layer_norm(initial, as_row(gain_ref)).astype(BF16)
    projected = matmul(normed, proj_ref[...])
    queries = projected[:, :width].astype(BF16) * jnp.asarray(1.0 / math.sqrt(head_dim), BF16)
    keys = projected[:, width : 2 * width].astype(BF16)
    turned = projected[:, 2 * width :].astype(BF16).astype(F32).T.astype(BF16)
    block_lane = iota((1, LANES), 1)
    allowed = (
        iota((rows, block_heads * rows), 0) % period == iota((rows, block_heads * rows), 1) % period
    )
    pieces = []
    for block in range(width // LANES):
        lanes = slice(block * LANES, (block + 1) * LANES)
        stacked = []
        for part in range(block_heads):
            own = (block_lane >= part * head_dim) & (block_lane < (part + 1) * head_dim)
            stacked.append(queries[:, lanes] * own.astype(F32).astype(BF16))
        logits = lax.dot_general(
            keys[:, lanes], jnp.concatenate(stacked, axis=0), NT, preferred_element_type=F32
        )
        attend = softmax_down(logits, allowed)
        mixed = matmul(turned[lanes], attend)
        for part in range(block_heads):
            pieces.append(
                mixed[part * head_dim : (part + 1) * head_dim, part * rows : (part + 1) * rows]
            )
    context = jnp.concatenate(pieces, axis=0).T.astype(BF16)
    after_time = initial + matmul(context, temporal_out_ref[...])
    second = layer_norm(after_time, as_row(hidden_gain_ref)).astype(BF16)
    hidden = jax.nn.gelu(matmul(second, hidden_in_ref[...])).astype(BF16)
    result = (after_time + matmul(hidden, hidden_out_ref[...])).astype(BF16).astype(F32)
    headed = layer_norm(result, as_row(head_gain_ref)).astype(BF16)
    branch_velocity = matmul(headed, head_out_ref[...])
    for step, out_ref in enumerate(out_refs):
        for frame in range(depth // period):
            start = step * depth + frame * period
            conditional = branch_velocity[start : start + share]
            empty = branch_velocity[start + share : start + period]
            out_ref[frame * share : (frame + 1) * share, :] = (
                empty + GUIDE * (conditional - empty)
            ).astype(BF16)


def update_kernel(groups, x_ref, noise_ref, *refs):
    parts, (next_ref, velocity_ref, rows_ref) = refs[:groups], refs[groups:]
    frames, residues, _ = x_ref.shape
    share = residues // groups
    me = lax.axis_index("seq")
    for frame in range(frames):
        for step, part in enumerate(parts):
            rows_ref[step * share : (step + 1) * share, :] = part[
                frame * share : (frame + 1) * share, :
            ].astype(F32)
        velocity = pltpu.roll(rows_ref[...], me * share, 0)
        velocity_ref[frame] = velocity.astype(BF16)
        next_ref[frame] = (
            x_ref[frame].astype(F32)
            + STEP_SIZE * velocity
            + NOISE_SCALE * noise_ref[frame].astype(F32)
        ).astype(BF16)


def exchange(pieces, direction):
    count = len(pieces)
    return [
        piece
        if step == 0
        else lax.ppermute(
            piece, "seq", [(source, (source + direction * step) % count) for source in range(count)]
        )
        for step, piece in enumerate(pieces)
    ]


def whole(memory_space=pltpu.VMEM):
    return pl.BlockSpec(memory_space=memory_space)


def body(
    groups,
    x_state,
    noise_field,
    rotations,
    translations,
    residue_types,
    pocket_mask,
    type_table,
    null_embed,
    spatial_gain,
    spatial_proj,
    spatial_points,
    spatial_gamma,
    spatial_out,
    temporal_gain,
    temporal_proj,
    temporal_out,
    hidden_gain,
    hidden_in,
    hidden_out,
    head_gain,
    head_out,
):
    frames, residues, width = x_state.shape
    share = residues // groups
    period = BRANCHES * share
    spatial = pl.pallas_call(
        functools.partial(spatial_kernel, groups),
        out_shape=[jax.ShapeDtypeStruct((frames * period, width), BF16)] * groups,
        in_specs=[whole(pltpu.SMEM)] + [whole()] * 11,
        out_specs=[whole()] * groups,
        scratch_shapes=[
            pltpu.VMEM((16, residues), F32),
            pltpu.VMEM((BRANCHES * residues, round_up(spatial_points.shape[1], LANES)), F32),
        ],
        name="spatial",
    )(
        spatial_gamma,
        x_state,
        rotations,
        translations,
        residue_types[None],
        pocket_mask[None],
        type_table,
        null_embed,
        spatial_gain,
        spatial_proj,
        spatial_points.T,
        spatial_out,
    )
    guided = pl.pallas_call(
        functools.partial(temporal_kernel, groups, period),
        out_shape=[jax.ShapeDtypeStruct((frames * share, width), BF16)] * groups,
        in_specs=[whole()] * (groups + 8),
        out_specs=[whole()] * groups,
        name="temporal",
    )(
        *exchange(spatial, 1),
        temporal_gain,
        temporal_proj,
        temporal_out,
        hidden_gain,
        hidden_in,
        hidden_out,
        head_gain,
        head_out,
    )
    return tuple(
        pl.pallas_call(
            functools.partial(update_kernel, groups),
            out_shape=[jax.ShapeDtypeStruct(x_state.shape, BF16)] * 2,
            in_specs=[whole()] * (groups + 2),
            out_specs=[whole()] * 2,
            scratch_shapes=[pltpu.VMEM((residues, width), F32)],
            name="update",
        )(x_state, noise_field, *exchange(guided, -1))
    )


def solution(mesh):
    tokens = P(("parts", "seq"), None, None)
    geometry = P(None, ("parts", "seq"), None)
    return jax.shard_map(
        functools.partial(body, mesh.shape["seq"]),
        mesh=mesh,
        in_specs=(tokens, tokens, geometry, geometry, P("parts"), P("parts")) + (P(),) * 15,
        out_specs=(tokens, tokens),
        check_vma=False,
    )
```

```python
import functools
import math

import jax
import jax.numpy as jnp
from jax import lax
from jax.experimental import pallas as pl
from jax.experimental.pallas import tpu as pltpu
from jax.sharding import PartitionSpec as P

THEADS = 6
BRANCHES = 2

WEIGHT_LOGIT = 0.7071067811865476
WEIGHT_POINT = 0.23570226039551584
GUIDE = 2.0
STEP_SIZE = 0.25
NOISE_SCALE = 0.2
EPSILON = 1e-05

BF16 = jnp.bfloat16
F32 = jnp.float32
LANES = 128
SPATIAL_VMEM = 56 * 2**20
TEMPORAL_VMEM = 40 * 2**20
NT = (((1,), (1,)), ((), ()))


def round_up(value, step):
    return -(-value // step) * step


def layer_norm(values, scale_gain):
    average = jnp.mean(values, axis=-1, keepdims=True)
    centered = values - average
    spread = jnp.mean(centered * centered, axis=-1, keepdims=True)
    return centered * lax.rsqrt(spread + EPSILON) * scale_gain


def as_row(ref):
    return ref[...].reshape(1, ref.shape[0])


def matmul(left, right):
    return jnp.dot(left, right, preferred_element_type=F32)


def iota(shape, axis):
    return lax.broadcasted_iota(jnp.int32, shape, axis)


def softmax_down(logits, allowed):
    logits = jnp.where(allowed, logits, -jnp.inf)
    powers = jnp.exp(logits - jnp.max(logits, axis=0, keepdims=True))
    return (powers * (1.0 / jnp.sum(powers, axis=0, keepdims=True))).astype(BF16)


def spatial_kernel(groups, gamma_ref, *refs):
    sources, refs = refs[:11], refs[11:]
    later, refs = refs[:5], refs[5:]
    out_ref, later_out, refs = refs[0], refs[1:6], refs[6:]
    local, (columns_ref, wide_ref, rows_ref, sems) = refs[:11], refs[11:]
    copies = [
        pltpu.make_async_copy(source, target, sems.at[index])
        for index, (source, target) in enumerate(
            zip(sources + later, local + tuple(later_out), strict=True)
        )
    ]
    for copy in copies:
        copy.start()
    (
        x_ref,
        table_ref,
        types_ref,
        null_ref,
        gain_ref,
        rotation_ref,
        translation_ref,
        mask_ref,
        proj_ref,
        points_ref,
        spatial_out_ref,
    ) = local
    for copy in copies[:8]:
        copy.wait()
    frames, residues, width = x_ref.shape
    heads = gamma_ref.shape[0]
    head_dim = width // heads
    block_heads = LANES // head_dim
    all_points = points_ref.shape[0]
    half = all_points // 2
    per_head = half // heads
    points_wide = wide_ref.shape[1]
    feature = round_up(half + 2 * heads, LANES)
    share = residues // groups
    fold = max(residues, LANES)
    point_scale = 0.5 * WEIGHT_LOGIT * WEIGHT_POINT

    kinds = table_ref.shape[0]
    onehot = (iota((kinds, residues), 0) == types_ref[...]).astype(F32).T.astype(BF16)
    conditional = matmul(onehot, table_ref[...])
    empty = as_row(null_ref).astype(F32)

    lane = iota((1, points_wide), 1)
    component = lane % 3
    narrow = iota((1, feature), 1)
    in_points = narrow < half
    in_first = (narrow >= half) & (narrow < half + heads)
    in_second = (narrow >= half + heads) & (narrow < half + 2 * heads)
    member = []
    gamma_lanes = jnp.zeros((1, feature), F32)
    for head in range(heads):
        own = (
            ((narrow >= head * per_head) & (narrow < (head + 1) * per_head))
            | (narrow == half + head)
            | (narrow == half + heads + head)
        )
        member.append(own.astype(F32).astype(BF16))
        gamma_lanes = jnp.where(own, gamma_ref[head], gamma_lanes)
    block_lane = iota((1, LANES), 1)
    block_member = [
        ((block_lane >= part * head_dim) & (block_lane < (part + 1) * head_dim))
        .astype(F32)
        .astype(BF16)
        for part in range(block_heads)
    ]
    row_point = iota((feature, feature), 0)
    column = iota((feature, feature), 1)
    column_head = jnp.where(column >= half + heads, column - half - heads, column - half)
    gather_norm = (
        (
            (column >= half)
            & (column < half + 2 * heads)
            & (row_point >= column_head * per_head)
            & (row_point < (column_head + 1) * per_head)
        )
        .astype(F32)
        .astype(BF16)
    )
    diagonal = iota((LANES, block_heads * residues), 0) // head_dim == (
        iota((LANES, block_heads * residues), 1) // residues
    )

    for frame in range(frames):
        columns_ref[...] = jnp.zeros_like(columns_ref)
        columns_ref[0:9, :] = rotation_ref[:, frame, :]
        moved = translation_ref[:, frame, :]
        columns_ref[9:12, :] = moved - jnp.mean(moved, axis=1, keepdims=True)
        columns_ref[12:13, :] = mask_ref[...].astype(F32)
        columns = columns_ref[...].T
        allowed = (columns[:, 12:13] == 1.0) | (
            iota((residues, residues), 0) == iota((residues, residues), 1)
        )
        allowed = (
            (columns[:, 12:13] == 1.0)
            | (
                iota((residues, block_heads * residues), 0)
                == iota((residues, block_heads * residues), 1) % residues
            )
        )

        state = x_ref[frame].astype(F32)
        initial = jnp.concatenate([state + conditional, state + empty], axis=0)
        normed = layer_norm(initial, as_row(gain_ref)).astype(BF16)
        if frame == 0:
            copies[8].wait()
            copies[9].wait()
        projected = matmul(normed, proj_ref[...])
        wide_ref[:, points_wide - LANES :] = jnp.zeros((BRANCHES * residues, LANES), F32)
        wide_ref[:, :all_points] = lax.dot_general(
            normed, points_ref[...], NT, preferred_element_type=F32
        )
        points = wide_ref[...]

        placed = None
        for step in range(-2, 3):
            factor = jnp.zeros((residues, points_wide), F32)
            for row in range(3):
                if 0 <= row + step < 3:
                    entry = 3 * row + row + step
                    factor = jnp.where(component == row, columns[:, entry : entry + 1], factor)
            shifted = points if step == 0 else pltpu.roll(points, (-step) % points_wide, 1)
            term = shifted.reshape(BRANCHES, residues, points_wide) * factor[None]
            placed = term if placed is None else placed + term
        anchor = jnp.zeros((residues, points_wide), F32)
        for row in range(3):
            anchor = jnp.where(component == row, columns[:, 9 + row : 10 + row], anchor)
        placed = (placed + anchor[None]).reshape(BRANCHES * residues, points_wide)

        query_points = placed[:, :feature]
        key_points = jnp.where(
            in_points, pltpu.roll(placed, points_wide - half, 1)[:, :feature], 0.0
        )
        query_feature = jnp.where(
            in_points,
            query_points * (gamma_lanes * (2.0 * point_scale)),
            (in_first | in_second).astype(F32),
        )
        query_high = query_feature.astype(BF16)
        query_low = (query_feature - query_high.astype(F32)).astype(BF16)

        square = key_points * key_points
        square_high = square.astype(BF16)
        rest = square - square_high.astype(F32)
        square_middle = rest.astype(BF16)
        square_low = (rest - square_middle.astype(F32)).astype(BF16)
        norm = (
            matmul(square_high, gather_norm)
            + matmul(square_middle, gather_norm)
            + matmul(square_low, gather_norm)
        )
        key_feature = key_points - norm * (gamma_lanes * point_scale)
        high = key_feature.astype(BF16)
        rest = key_feature - high.astype(F32)
        low = rest.astype(BF16)
        last = (rest - low.astype(F32)).astype(BF16)
        key_high = jnp.where(in_second, last, high)
        key_low = jnp.where(in_second, jnp.zeros_like(low), low)

        queries = (
            projected[:, :width].astype(BF16) * jnp.asarray(WEIGHT_LOGIT / math.sqrt(head_dim), BF16)
        )
        keys = projected[:, width : 2 * width].astype(BF16)
        values = projected[:, 2 * width :].astype(BF16).astype(F32)

        contexts = []
        for branch in range(BRANCHES):
            rows = slice(branch * residues, (branch + 1) * residues)
            turned = values[rows].T.astype(BF16)
            pieces = []
            for block in range(width // LANES):
                lanes = slice(block * LANES, (block + 1) * LANES)
                left = jnp.concatenate(
                    [keys[rows, lanes], key_high[rows], key_low[rows], key_high[rows]], axis=1
                )
                stacked = []
                for part in range(block_heads):
                    own = member[block * block_heads + part]
                    upper = query_high[rows] * own
                    stacked.append(
                        jnp.concatenate(
                            [
                                queries[rows, lanes] * block_member[part],
                                upper,
                                upper,
                                query_low[rows] * own,
                            ],
                            axis=1,
                        )
                    )
                logits = lax.dot_general(
                    left, jnp.concatenate(stacked, axis=0), NT, preferred_element_type=F32
                )
                attend = softmax_down(logits, allowed)
                mixed = jnp.where(diagonal, matmul(turned[lanes], attend), 0.0)
                folded = mixed[:, :fold]
                for start in range(fold, block_heads * residues, fold):
                    folded = folded + mixed[:, start : start + fold]
                pieces.append(folded)
            contexts.append(jnp.concatenate(pieces, axis=0).T.astype(BF16))
        if frame == 0:
            copies[10].wait()
        update = matmul(jnp.concatenate(contexts, axis=0), spatial_out_ref[...])
        for branch in range(BRANCHES):
            total = initial[branch * residues : (branch + 1) * residues]
            for start in range(0, fold, residues):
                first = branch * fold + start
                total = total + update[first : first + residues]
            place = (frame * BRANCHES + branch) * share
            for group in range(groups):
                rows_ref[group, place : place + share, :] = total[group * share : (group + 1) * share]
    out_ref[...] = rows_ref[...].astype(BF16)
    for copy in copies[11:]:
        copy.wait()


def temporal_kernel(
    period,
    x_ref,
    gain_ref,
    proj_ref,
    temporal_out_ref,
    hidden_gain_ref,
    hidden_in_ref,
    hidden_out_ref,
    head_gain_ref,
    head_out_ref,
    out_ref,
):
    groups, depth, width = x_ref.shape
    rows = groups * depth
    head_dim = width // THEADS
    block_heads = LANES // head_dim
    share = period // BRANCHES

    initial = x_ref[...].astype(F32).reshape(rows, width)
    normed = layer_norm(initial, as_row(gain_ref)).astype(BF16)
    projected = matmul(normed, proj_ref[...])
    queries = projected[:, :width].astype(BF16) * jnp.asarray(1.0 / math.sqrt(head_dim), BF16)
    keys = projected[:, width : 2 * width].astype(BF16)
    turned = projected[:, 2 * width :].astype(BF16).astype(F32).T.astype(BF16)
    block_lane = iota((1, LANES), 1)
    allowed = (
        iota((rows, block_heads * rows), 0) % period == iota((rows, block_heads * rows), 1) % period
    )
    pieces = []
    for block in range(width // LANES):
        lanes = slice(block * LANES, (block + 1) * LANES)
        stacked = []
        for part in range(block_heads):
            own = (block_lane >= part * head_dim) & (block_lane < (part + 1) * head_dim)
            stacked.append(queries[:, lanes] * own.astype(F32).astype(BF16))
        logits = lax.dot_general(
            keys[:, lanes], jnp.concatenate(stacked, axis=0), NT, preferred_element_type=F32
        )
        attend = softmax_down(logits, allowed)
        mixed = matmul(turned[lanes], attend)
        for part in range(block_heads):
            pieces.append(
                mixed[part * head_dim : (part + 1) * head_dim, part * rows : (part + 1) * rows]
            )
    context = jnp.concatenate(pieces, axis=0).T.astype(BF16)
    after_time = initial + matmul(context, temporal_out_ref[...])
    second = layer_norm(after_time, as_row(hidden_gain_ref)).astype(BF16)
    hidden = jax.nn.gelu(matmul(second, hidden_in_ref[...])).astype(BF16)
    result = (after_time + matmul(hidden, hidden_out_ref[...])).astype(BF16).astype(F32)
    headed = layer_norm(result, as_row(head_gain_ref)).astype(BF16)
    branch_velocity = matmul(headed, head_out_ref[...]).reshape(rows // period, period, width)
    conditional = branch_velocity[:, :share]
    empty = branch_velocity[:, share:]
    out_ref[...] = (empty + GUIDE * (conditional - empty)).astype(BF16)


def whole(memory_space=pltpu.VMEM):
    return pl.BlockSpec(memory_space=memory_space)


def body(
    groups,
    x_state,
    noise_field,
    rotations,
    translations,
    residue_types,
    pocket_mask,
    type_table,
    null_embed,
    spatial_gain,
    spatial_proj,
    spatial_points,
    spatial_gamma,
    spatial_out,
    temporal_gain,
    temporal_proj,
    temporal_out,
    hidden_gain,
    hidden_in,
    hidden_out,
    head_gain,
    head_out,
):
    frames, residues, width = x_state.shape
    share = residues // groups
    period = BRANCHES * share
    sources = (
        x_state,
        type_table,
        residue_types[None],
        null_embed,
        spatial_gain,
        rotations,
        translations,
        pocket_mask[None],
        spatial_proj,
        spatial_points.T,
        spatial_out,
    )
    later = (temporal_proj, temporal_out, hidden_in, hidden_out, head_out)
    spatial, *later = pl.pallas_call(
        functools.partial(spatial_kernel, groups),
        out_shape=[pltpu.VMEM((groups, frames * period, width), BF16)]
        + [pltpu.VMEM(array.shape, array.dtype) for array in later],
        in_specs=[whole(pltpu.SMEM)] + [whole(pl.ANY)] * (len(sources) + len(later)),
        out_specs=[whole()] * (1 + len(later)),
        scratch_shapes=[pltpu.VMEM(array.shape, array.dtype) for array in sources]
        + [
            pltpu.VMEM((16, residues), F32),
            pltpu.VMEM((BRANCHES * residues, round_up(spatial_points.shape[1], LANES)), F32),
            pltpu.VMEM((groups, frames * period, width), F32),
            pltpu.SemaphoreType.DMA((len(sources) + len(later),)),
        ],
        compiler_params=pltpu.CompilerParams(vmem_limit_bytes=SPATIAL_VMEM),
        name="spatial",
    )(spatial_gamma, *sources, *later)
    arrived = lax.all_to_all(spatial, "seq", split_axis=0, concat_axis=0, tiled=True)
    proj_local, out_local, in_local, hidden_local, head_local = later
    guided = pl.pallas_call(
        functools.partial(temporal_kernel, period),
        out_shape=pltpu.VMEM((groups * frames, share, width), BF16),
        in_specs=[whole()] * 9,
        out_specs=whole(),
        compiler_params=pltpu.CompilerParams(vmem_limit_bytes=TEMPORAL_VMEM),
        name="temporal",
    )(
        arrived,
        temporal_gain,
        proj_local,
        out_local,
        hidden_gain,
        in_local,
        hidden_local,
        head_gain,
        head_local,
    )
    velocity = lax.all_to_all(guided, "seq", split_axis=0, concat_axis=1, tiled=True)
    x_next = (
        x_state.astype(F32)
        + STEP_SIZE * velocity.astype(F32)
        + NOISE_SCALE * noise_field.astype(F32)
    ).astype(BF16)
    return (x_next, velocity)


def solution(mesh):
    tokens = P(("parts", "seq"), None, None)
    geometry = P(None, ("parts", "seq"), None)
    return jax.shard_map(
        functools.partial(body, mesh.shape["seq"]),
        mesh=mesh,
        in_specs=(tokens, tokens, geometry, geometry, P("parts"), P("parts")) + (P(),) * 15,
        out_specs=(tokens, tokens),
        check_vma=False,
    )
```

```python
import functools
import math

import jax
import jax.numpy as jnp
from jax import lax
from jax.experimental import pallas as pl
from jax.experimental.pallas import tpu as pltpu
from jax.sharding import PartitionSpec as P

THEADS = 6
BRANCHES = 2

WEIGHT_LOGIT = 0.7071067811865476
WEIGHT_POINT = 0.23570226039551584
GUIDE = 2.0
STEP_SIZE = 0.25
NOISE_SCALE = 0.2
EPSILON = 1e-05

BF16 = jnp.bfloat16
F32 = jnp.float32
LANES = 128
SPATIAL_VMEM = 56 * 2**20
TEMPORAL_VMEM = 40 * 2**20
NT = (((1,), (1,)), ((), ()))


def round_up(value, step):
    return -(-value // step) * step


def layer_norm(values, scale_gain):
    average = jnp.mean(values, axis=-1, keepdims=True)
    centered = values - average
    spread = jnp.mean(centered * centered, axis=-1, keepdims=True)
    return centered * lax.rsqrt(spread + EPSILON) * scale_gain


def as_row(ref):
    return ref[...].reshape(1, ref.shape[0])


def matmul(left, right):
    return jnp.dot(left, right, preferred_element_type=F32)


def iota(shape, axis):
    return lax.broadcasted_iota(jnp.int32, shape, axis)


def softmax_down(logits, allowed):
    logits = jnp.where(allowed, logits, -jnp.inf)
    powers = jnp.exp(logits - jnp.max(logits, axis=0, keepdims=True))
    return (powers * (1.0 / jnp.sum(powers, axis=0, keepdims=True))).astype(BF16)


def spatial_kernel(groups, gamma_ref, *refs):
    sources, refs = refs[:11], refs[11:]
    later, refs = refs[:5], refs[5:]
    out_ref, later_out, refs = refs[0], refs[1:6], refs[6:]
    local, (columns_ref, wide_ref, rows_ref, sems) = refs[:11], refs[11:]
    copies = [
        pltpu.make_async_copy(source, target, sems.at[index])
        for index, (source, target) in enumerate(
            zip(sources + later, local + tuple(later_out), strict=True)
        )
    ]
    for copy in copies:
        copy.start()
    (
        x_ref,
        table_ref,
        types_ref,
        null_ref,
        gain_ref,
        rotation_ref,
        translation_ref,
        mask_ref,
        proj_ref,
        points_ref,
        spatial_out_ref,
    ) = local
    for copy in copies[:8]:
        copy.wait()
    frames, residues, width = x_ref.shape
    heads = gamma_ref.shape[0]
    head_dim = width // heads
    block_heads = LANES // head_dim
    all_points = points_ref.shape[0]
    half = all_points // 2
    per_head = half // heads
    points_wide = wide_ref.shape[1]
    feature = round_up(half + 2 * heads, LANES)
    share = residues // groups
    fold = max(residues, LANES)
    point_scale = 0.5 * WEIGHT_LOGIT * WEIGHT_POINT

    kinds = table_ref.shape[0]
    onehot = (iota((kinds, residues), 0) == types_ref[...]).astype(F32).T.astype(BF16)
    conditional = matmul(onehot, table_ref[...])
    empty = as_row(null_ref).astype(F32)

    lane = iota((1, points_wide), 1)
    component = lane % 3
    narrow = iota((1, feature), 1)
    in_points = narrow < half
    in_first = (narrow >= half) & (narrow < half + heads)
    in_second = (narrow >= half + heads) & (narrow < half + 2 * heads)
    member = []
    gamma_lanes = jnp.zeros((1, feature), F32)
    for head in range(heads):
        own = (
            ((narrow >= head * per_head) & (narrow < (head + 1) * per_head))
            | (narrow == half + head)
            | (narrow == half + heads + head)
        )
        member.append(own.astype(F32).astype(BF16))
        gamma_lanes = jnp.where(own, gamma_ref[head], gamma_lanes)
    block_lane = iota((1, LANES), 1)
    block_member = [
        ((block_lane >= part * head_dim) & (block_lane < (part + 1) * head_dim))
        .astype(F32)
        .astype(BF16)
        for part in range(block_heads)
    ]
    row_point = iota((feature, feature), 0)
    column = iota((feature, feature), 1)
    column_head = jnp.where(column >= half + heads, column - half - heads, column - half)
    gather_norm = (
        (
            (column >= half)
            & (column < half + 2 * heads)
            & (row_point >= column_head * per_head)
            & (row_point < (column_head + 1) * per_head)
        )
        .astype(F32)
        .astype(BF16)
    )
    diagonal = iota((LANES, block_heads * residues), 0) // head_dim == (
        iota((LANES, block_heads * residues), 1) // residues
    )

    for frame in range(frames):
        columns_ref[...] = jnp.zeros_like(columns_ref)
        columns_ref[0:9, :] = rotation_ref[:, frame, :]
        moved = translation_ref[:, frame, :]
        columns_ref[9:12, :] = moved - jnp.mean(moved, axis=1, keepdims=True)
        columns_ref[12:13, :] = mask_ref[...].astype(F32)
        columns = columns_ref[...].T
        allowed = (columns[:, 12:13] == 1.0) | (
            iota((residues, residues), 0) == iota((residues, residues), 1)
        )
        allowed = (
            (columns[:, 12:13] == 1.0)
            | (
                iota((residues, block_heads * residues), 0)
                == iota((residues, block_heads * residues), 1) % residues
            )
        )

        state = x_ref[frame].astype(F32)
        initial = jnp.concatenate([state + conditional, state + empty], axis=0)
        normed = layer_norm(initial, as_row(gain_ref)).astype(BF16)
        if frame == 0:
            copies[8].wait()
            copies[9].wait()
        projected = matmul(normed, proj_ref[...])
        wide_ref[:, points_wide - LANES :] = jnp.zeros((BRANCHES * residues, LANES), F32)
        wide_ref[:, :all_points] = lax.dot_general(
            normed, points_ref[...], NT, preferred_element_type=F32
        )
        points = wide_ref[...]

        placed = None
        for step in range(-2, 3):
            factor = jnp.zeros((residues, points_wide), F32)
            for row in range(3):
                if 0 <= row + step < 3:
                    entry = 3 * row + row + step
                    factor = jnp.where(component == row, columns[:, entry : entry + 1], factor)
            shifted = points if step == 0 else pltpu.roll(points, (-step) % points_wide, 1)
            term = shifted.reshape(BRANCHES, residues, points_wide) * factor[None]
            placed = term if placed is None else placed + term
        anchor = jnp.zeros((residues, points_wide), F32)
        for row in range(3):
            anchor = jnp.where(component == row, columns[:, 9 + row : 10 + row], anchor)
        placed = (placed + anchor[None]).reshape(BRANCHES * residues, points_wide)

        query_points = placed[:, :feature]
        key_points = jnp.where(
            in_points, pltpu.roll(placed, points_wide - half, 1)[:, :feature], 0.0
        )
        query_feature = jnp.where(
            in_points,
            query_points * (gamma_lanes * (2.0 * point_scale)),
            (in_first | in_second).astype(F32),
        )
        query_high = query_feature.astype(BF16)
        query_low = (query_feature - query_high.astype(F32)).astype(BF16)

        square = key_points * key_points
        square_high = square.astype(BF16)
        rest = square - square_high.astype(F32)
        square_middle = rest.astype(BF16)
        square_low = (rest - square_middle.astype(F32)).astype(BF16)
        norm = (
            matmul(square_high, gather_norm)
            + matmul(square_middle, gather_norm)
            + matmul(square_low, gather_norm)
        )
        key_feature = key_points - norm * (gamma_lanes * point_scale)
        high = key_feature.astype(BF16)
        rest = key_feature - high.astype(F32)
        low = rest.astype(BF16)
        last = (rest - low.astype(F32)).astype(BF16)
        key_high = jnp.where(in_second, last, high)
        key_low = jnp.where(in_second, jnp.zeros_like(low), low)

        queries = (
            projected[:, :width].astype(BF16) * jnp.asarray(WEIGHT_LOGIT / math.sqrt(head_dim), BF16)
        )
        keys = projected[:, width : 2 * width].astype(BF16)
        values = projected[:, 2 * width :].astype(BF16).astype(F32)

        contexts = []
        for branch in range(BRANCHES):
            rows = slice(branch * residues, (branch + 1) * residues)
            turned = values[rows].T.astype(BF16)
            pieces = []
            for block in range(width // LANES):
                lanes = slice(block * LANES, (block + 1) * LANES)
                left = jnp.concatenate(
                    [keys[rows, lanes], key_high[rows], key_low[rows], key_high[rows]], axis=1
                )
                stacked = []
                for part in range(block_heads):
                    own = member[block * block_heads + part]
                    upper = query_high[rows] * own
                    stacked.append(
                        jnp.concatenate(
                            [
                                queries[rows, lanes] * block_member[part],
                                upper,
                                upper,
                                query_low[rows] * own,
                            ],
                            axis=1,
                        )
                    )
                logits = lax.dot_general(
                    left, jnp.concatenate(stacked, axis=0), NT, preferred_element_type=F32
                )
                attend = softmax_down(logits, allowed)
                mixed = jnp.where(diagonal, matmul(turned[lanes], attend), 0.0)
                folded = mixed[:, :fold]
                for start in range(fold, block_heads * residues, fold):
                    folded = folded + mixed[:, start : start + fold]
                pieces.append(folded)
            contexts.append(jnp.concatenate(pieces, axis=0).T.astype(BF16))
        if frame == 0:
            copies[10].wait()
        update = matmul(jnp.concatenate(contexts, axis=0), spatial_out_ref[...])
        for branch in range(BRANCHES):
            total = initial[branch * residues : (branch + 1) * residues]
            for start in range(0, fold, residues):
                first = branch * fold + start
                total = total + update[first : first + residues]
            place = (frame * BRANCHES + branch) * share
            for group in range(groups):
                rows_ref[group, place : place + share, :] = total[group * share : (group + 1) * share]
    out_ref[...] = rows_ref[...].astype(BF16)
    for copy in copies[11:]:
        copy.wait()


def temporal_kernel(
    period,
    gathered_ref,
    gain_ref,
    proj_ref,
    temporal_out_ref,
    hidden_gain_ref,
    hidden_in_ref,
    hidden_out_ref,
    head_gain_ref,
    head_out_ref,
    out_ref,
    x_ref,
    sem,
):
    copy = pltpu.make_async_copy(gathered_ref.at[:, lax.axis_index("seq")], x_ref, sem)
    copy.start()
    copy.wait()
    groups, depth, width = x_ref.shape
    rows = groups * depth
    head_dim = width // THEADS
    block_heads = LANES // head_dim
    share = period // BRANCHES

    initial = x_ref[...].astype(F32).reshape(rows, width)
    normed = layer_norm(initial, as_row(gain_ref)).astype(BF16)
    projected = matmul(normed, proj_ref[...])
    queries = projected[:, :width].astype(BF16) * jnp.asarray(1.0 / math.sqrt(head_dim), BF16)
    keys = projected[:, width : 2 * width].astype(BF16)
    turned = projected[:, 2 * width :].astype(BF16).astype(F32).T.astype(BF16)
    block_lane = iota((1, LANES), 1)
    allowed = (
        iota((rows, block_heads * rows), 0) % period == iota((rows, block_heads * rows), 1) % period
    )
    pieces = []
    for block in range(width // LANES):
        lanes = slice(block * LANES, (block + 1) * LANES)
        stacked = []
        for part in range(block_heads):
            own = (block_lane >= part * head_dim) & (block_lane < (part + 1) * head_dim)
            stacked.append(queries[:, lanes] * own.astype(F32).astype(BF16))
        logits = lax.dot_general(
            keys[:, lanes], jnp.concatenate(stacked, axis=0), NT, preferred_element_type=F32
        )
        attend = softmax_down(logits, allowed)
        mixed = matmul(turned[lanes], attend)
        for part in range(block_heads):
            pieces.append(
                mixed[part * head_dim : (part + 1) * head_dim, part * rows : (part + 1) * rows]
            )
    context = jnp.concatenate(pieces, axis=0).T.astype(BF16)
    after_time = initial + matmul(context, temporal_out_ref[...])
    second = layer_norm(after_time, as_row(hidden_gain_ref)).astype(BF16)
    hidden = jax.nn.gelu(matmul(second, hidden_in_ref[...])).astype(BF16)
    result = (after_time + matmul(hidden, hidden_out_ref[...])).astype(BF16).astype(F32)
    headed = layer_norm(result, as_row(head_gain_ref)).astype(BF16)
    branch_velocity = matmul(headed, head_out_ref[...]).reshape(rows // period, period, width)
    conditional = branch_velocity[:, :share]
    empty = branch_velocity[:, share:]
    out_ref[...] = (empty + GUIDE * (conditional - empty)).astype(BF16)


def whole(memory_space=pltpu.VMEM):
    return pl.BlockSpec(memory_space=memory_space)


def body(
    groups,
    x_state,
    noise_field,
    rotations,
    translations,
    residue_types,
    pocket_mask,
    type_table,
    null_embed,
    spatial_gain,
    spatial_proj,
    spatial_points,
    spatial_gamma,
    spatial_out,
    temporal_gain,
    temporal_proj,
    temporal_out,
    hidden_gain,
    hidden_in,
    hidden_out,
    head_gain,
    head_out,
):
    frames, residues, width = x_state.shape
    share = residues // groups
    period = BRANCHES * share
    sources = (
        x_state,
        type_table,
        residue_types[None],
        null_embed,
        spatial_gain,
        rotations,
        translations,
        pocket_mask[None],
        spatial_proj,
        spatial_points.T,
        spatial_out,
    )
    later = (temporal_proj, temporal_out, hidden_in, hidden_out, head_out)
    spatial, *later = pl.pallas_call(
        functools.partial(spatial_kernel, groups),
        out_shape=[pltpu.VMEM((groups, frames * period, width), BF16)]
        + [pltpu.VMEM(array.shape, array.dtype) for array in later],
        in_specs=[whole(pltpu.SMEM)] + [whole(pl.ANY)] * (len(sources) + len(later)),
        out_specs=[whole()] * (1 + len(later)),
        scratch_shapes=[pltpu.VMEM(array.shape, array.dtype) for array in sources]
        + [
            pltpu.VMEM((16, residues), F32),
            pltpu.VMEM((BRANCHES * residues, round_up(spatial_points.shape[1], LANES)), F32),
            pltpu.VMEM((groups, frames * period, width), F32),
            pltpu.SemaphoreType.DMA((len(sources) + len(later),)),
        ],
        compiler_params=pltpu.CompilerParams(vmem_limit_bytes=SPATIAL_VMEM),
        name="spatial",
    )(spatial_gamma, *sources, *later)
    arrived = lax.all_gather(spatial, "seq")
    proj_local, out_local, in_local, hidden_local, head_local = later
    guided = pl.pallas_call(
        functools.partial(temporal_kernel, period),
        out_shape=pltpu.VMEM((groups * frames, share, width), BF16),
        in_specs=[whole(pl.ANY)] + [whole()] * 8,
        out_specs=whole(),
        scratch_shapes=[
            pltpu.VMEM((groups, frames * period, width), BF16),
            pltpu.SemaphoreType.DMA,
        ],
        compiler_params=pltpu.CompilerParams(vmem_limit_bytes=TEMPORAL_VMEM),
        name="temporal",
    )(
        arrived,
        temporal_gain,
        proj_local,
        out_local,
        hidden_gain,
        in_local,
        hidden_local,
        head_gain,
        head_local,
    )
    gathered = lax.all_gather(guided.reshape(groups, frames * share, width), "seq")
    velocity = lax.dynamic_index_in_dim(gathered, lax.axis_index("seq"), 1, keepdims=False)
    velocity = jnp.moveaxis(velocity.reshape(groups, frames, share, width), 0, 1).reshape(x_state.shape)
    x_next = (
        x_state.astype(F32)
        + STEP_SIZE * velocity.astype(F32)
        + NOISE_SCALE * noise_field.astype(F32)
    ).astype(BF16)
    return (x_next, velocity)


def solution(mesh):
    tokens = P(("parts", "seq"), None, None)
    geometry = P(None, ("parts", "seq"), None)
    return jax.shard_map(
        functools.partial(body, mesh.shape["seq"]),
        mesh=mesh,
        in_specs=(tokens, tokens, geometry, geometry, P("parts"), P("parts")) + (P(),) * 15,
        out_specs=(tokens, tokens),
        check_vma=False,
    )
```

```python
import functools
import math

import jax
import jax.numpy as jnp
from jax import lax
from jax.experimental import pallas as pl
from jax.experimental.pallas import tpu as pltpu
from jax.sharding import PartitionSpec as P

THEADS = 6
BRANCHES = 2

WEIGHT_LOGIT = 0.7071067811865476
WEIGHT_POINT = 0.23570226039551584
GUIDE = 2.0
STEP_SIZE = 0.25
NOISE_SCALE = 0.2
EPSILON = 1e-05

BF16 = jnp.bfloat16
F32 = jnp.float32
LANES = 128
SLOT = 64
SPATIAL_VMEM = 56 * 2**20
TEMPORAL_VMEM = 40 * 2**20
NT = (((1,), (1,)), ((), ()))


def layer_norm(values, scale_gain):
    average = jnp.mean(values, axis=-1, keepdims=True)
    centered = values - average
    spread = jnp.mean(centered * centered, axis=-1, keepdims=True)
    return centered * lax.rsqrt(spread + EPSILON) * scale_gain


def as_row(ref):
    return ref[...].reshape(1, ref.shape[0])


def matmul(left, right):
    return jnp.dot(left, right, preferred_element_type=F32)


def iota(shape, axis):
    return lax.broadcasted_iota(jnp.int32, shape, axis)


def softmax_down(logits, allowed):
    logits = jnp.where(allowed, logits, -jnp.inf)
    powers = jnp.exp(logits - jnp.max(logits, axis=0, keepdims=True))
    return (powers * (1.0 / jnp.sum(powers, axis=0, keepdims=True))).astype(BF16)


def spatial_kernel(groups, gamma_ref, *refs):
    sources, refs = refs[:11], refs[11:]
    later, refs = refs[:5], refs[5:]
    out_ref, later_out, refs = refs[0], refs[1:6], refs[6:]
    local, (columns_ref, rows_ref, sems) = refs[:11], refs[11:]
    (
        x_ref,
        table_ref,
        types_ref,
        null_ref,
        gain_ref,
        rotation_ref,
        translation_ref,
        mask_ref,
        proj_ref,
        spatial_out_ref,
        points_ref,
    ) = local
    frames, residues, width = x_ref.shape
    heads = gamma_ref.shape[0]
    head_dim = width // heads
    blocks = width // LANES
    block_heads = LANES // head_dim
    slot_rows = sources[-1].shape[0] // (2 * blocks)
    per_head = slot_rows // block_heads
    share = residues // groups
    fold = max(residues, LANES)
    stacked_rows = block_heads * residues
    point_scale = 0.5 * WEIGHT_LOGIT * WEIGHT_POINT

    pairs = list(zip(sources[:10], local[:10], strict=True))
    for slot in range(2 * blocks):
        pairs.append(
            (
                sources[-1].at[pl.ds(slot * slot_rows, slot_rows), :],
                points_ref.at[pl.ds(slot * SLOT, slot_rows), :],
            )
        )
    pairs += list(zip(later, later_out, strict=True))
    copies = [
        pltpu.make_async_copy(source, target, sems.at[index])
        for index, (source, target) in enumerate(pairs)
    ]
    for copy in copies:
        copy.start()
    small, wide, after = copies[:8], [copies[8]] + copies[10 : 10 + 2 * blocks], copies[9]

    for slot in range(2 * blocks):
        points_ref[slot * SLOT + slot_rows : (slot + 1) * SLOT, :] = jnp.zeros(
            (SLOT - slot_rows, width), BF16
        )
    lane = iota((1, LANES), 1)
    low = lane < SLOT
    place = lane % SLOT
    component = jnp.where(place < slot_rows, place % 3, 3)
    in_first = (place >= slot_rows) & (place < slot_rows + block_heads)
    in_second = (place >= slot_rows + block_heads) & (place < slot_rows + 2 * block_heads)
    in_norm = in_first | in_second
    member, block_member = [], []
    for part in range(block_heads):
        own = (
            ((place >= part * per_head) & (place < (part + 1) * per_head))
            | (place == slot_rows + part)
            | (place == slot_rows + block_heads + part)
        )
        member.append(own)
        block_member.append((lane >= part * head_dim) & (lane < (part + 1) * head_dim))
    both_member = [
        jnp.concatenate([left, right], axis=1).astype(F32).astype(BF16)
        for left, right in zip(block_member, member, strict=True)
    ]
    gamma_lanes = []
    for block in range(blocks):
        gamma = jnp.zeros((1, LANES), F32)
        for part in range(block_heads):
            gamma = jnp.where(member[part], gamma_ref[block * block_heads + part], gamma)
        gamma_lanes.append(gamma * point_scale)
    column = iota((LANES, LANES), 1) % SLOT - slot_rows
    column = jnp.where(column >= block_heads, column - block_heads, column)
    row_head = iota((LANES, LANES), 0) // per_head
    gather_norm = (
        ((iota((LANES, LANES), 0) < slot_rows) & (row_head == column) & in_norm)
        .astype(F32)
        .astype(BF16)
    )
    diagonal = iota((LANES, stacked_rows), 0) // head_dim == (
        iota((LANES, stacked_rows), 1) // residues
    )
    same = iota((residues, stacked_rows), 0) == iota((residues, stacked_rows), 1) % residues
    columns_ref[...] = jnp.zeros_like(columns_ref)

    for copy in small:
        copy.wait()
    kinds = table_ref.shape[0]
    onehot = (iota((kinds, residues), 0) == types_ref[...]).astype(F32).T.astype(BF16)
    conditional = matmul(onehot, table_ref[...])
    empty = as_row(null_ref).astype(F32)

    for frame in range(frames):
        state = x_ref[frame].astype(F32)
        initial = jnp.concatenate([state + conditional, state + empty], axis=0)
        normed = layer_norm(initial, as_row(gain_ref)).astype(BF16)

        columns_ref[0:9, :] = rotation_ref[:, frame, :]
        moved = translation_ref[:, frame, :]
        columns_ref[9:12, :] = moved - jnp.mean(moved, axis=1, keepdims=True)
        columns_ref[12:13, :] = mask_ref[...].astype(F32)
        columns = columns_ref[...].T
        allowed = (columns[:, 12:13] == 1.0) | same
        factors = []
        for step in range(-2, 3):
            factor = jnp.zeros((residues, LANES), F32)
            for row in range(3):
                if 0 <= row + step < 3:
                    entry = 3 * row + row + step
                    factor = jnp.where(component == row, columns[:, entry : entry + 1], factor)
            factors.append(jnp.concatenate([factor] * BRANCHES, axis=0))
        anchor = jnp.zeros((residues, LANES), F32)
        for row in range(3):
            anchor = jnp.where(component == row, columns[:, 9 + row : 10 + row], anchor)
        anchor = jnp.concatenate([anchor] * BRANCHES, axis=0)

        if frame == 0:
            for copy in wide:
                copy.wait()
        points = lax.dot_general(normed, points_ref[...], NT, preferred_element_type=F32)
        projected = matmul(normed, proj_ref[...])

        slots = []
        for pair in range(blocks):
            lanes = points[:, pair * LANES : (pair + 1) * LANES]
            placed = anchor + factors[2] * lanes
            for step in (-2, -1, 1, 2):
                placed = placed + factors[step + 2] * pltpu.roll(lanes, (-step) % LANES, 1)
            swapped = pltpu.roll(placed, SLOT, 1)
            slots += [jnp.where(low, placed, swapped), jnp.where(low, swapped, placed)]

        query_feature, key_first, key_second = [], [], []
        for block in range(blocks):
            feature = jnp.where(in_norm, 1.0, slots[block] * (2.0 * gamma_lanes[block]))
            high = feature.astype(BF16)
            rest = (feature - high.astype(F32)).astype(BF16)
            query_feature.append(jnp.where(low, high, rest))

            feature = slots[blocks + block]
            square = feature * feature
            square_high = square.astype(BF16)
            rest = square - square_high.astype(F32)
            square_middle = rest.astype(BF16)
            square_low = (rest - square_middle.astype(F32)).astype(BF16)
            norm = (
                matmul(square_high, gather_norm)
                + matmul(square_middle, gather_norm)
                + matmul(square_low, gather_norm)
            )
            feature = feature - norm * gamma_lanes[block]
            high = feature.astype(BF16)
            rest = feature - high.astype(F32)
            middle = rest.astype(BF16)
            last = (rest - middle.astype(F32)).astype(BF16)
            key_first.append(jnp.where(in_second, last, high))
            key_second.append(jnp.where(low & ~in_second, middle, jnp.zeros_like(middle)))

        queries = (
            projected[:, :width].astype(BF16) * jnp.asarray(WEIGHT_LOGIT / math.sqrt(head_dim), BF16)
        )
        keys = projected[:, width : 2 * width].astype(BF16)
        values = projected[:, 2 * width :].astype(BF16).astype(F32)
        nothing = jnp.zeros((residues, LANES), BF16)

        contexts = []
        for branch in range(BRANCHES):
            rows = slice(branch * residues, (branch + 1) * residues)
            turned = values[rows].T.astype(BF16)
            pieces = []
            for block in range(blocks):
                lanes = slice(block * LANES, (block + 1) * LANES)
                left = jnp.concatenate(
                    [
                        jnp.concatenate([keys[rows, lanes], key_first[block][rows]], axis=1),
                        jnp.concatenate([nothing, key_second[block][rows]], axis=1),
                    ],
                    axis=0,
                )
                right = jnp.concatenate([queries[rows, lanes], query_feature[block][rows]], axis=1)
                right = jnp.concatenate([right * own for own in both_member], axis=0)
                logits = lax.dot_general(left, right, NT, preferred_element_type=F32)
                attend = softmax_down(logits[:residues] + logits[residues:], allowed)
                mixed = jnp.where(diagonal, matmul(turned[lanes], attend), 0.0)
                folded = mixed[:, :fold]
                for start in range(fold, stacked_rows, fold):
                    folded = folded + mixed[:, start : start + fold]
                pieces.append(folded)
            contexts.append(jnp.concatenate(pieces, axis=0).T.astype(BF16))
        if frame == 0:
            after.wait()
        update = matmul(jnp.concatenate(contexts, axis=0), spatial_out_ref[...])
        for branch in range(BRANCHES):
            total = initial[branch * residues : (branch + 1) * residues]
            for start in range(0, fold, residues):
                first = branch * fold + start
                total = total + update[first : first + residues]
            start = (frame * BRANCHES + branch) * share
            for group in range(groups):
                rows_ref[group, start : start + share, :] = total[group * share : (group + 1) * share]
    out_ref[...] = rows_ref[...].astype(BF16)
    for copy in copies[10 + 2 * blocks :]:
        copy.wait()


def temporal_kernel(
    period,
    x_ref,
    gain_ref,
    proj_ref,
    temporal_out_ref,
    hidden_gain_ref,
    hidden_in_ref,
    hidden_out_ref,
    head_gain_ref,
    head_out_ref,
    out_ref,
):
    groups, depth, width = x_ref.shape
    rows = groups * depth
    head_dim = width // THEADS
    block_heads = LANES // head_dim
    share = period // BRANCHES

    initial = x_ref[...].astype(F32).reshape(rows, width)
    normed = layer_norm(initial, as_row(gain_ref)).astype(BF16)
    projected = matmul(normed, proj_ref[...])
    queries = projected[:, :width].astype(BF16) * jnp.asarray(1.0 / math.sqrt(head_dim), BF16)
    keys = projected[:, width : 2 * width].astype(BF16)
    turned = projected[:, 2 * width :].astype(BF16).astype(F32).T.astype(BF16)
    block_lane = iota((1, LANES), 1)
    allowed = (
        iota((rows, block_heads * rows), 0) % period == iota((rows, block_heads * rows), 1) % period
    )
    pieces = []
    for block in range(width // LANES):
        lanes = slice(block * LANES, (block + 1) * LANES)
        stacked = []
        for part in range(block_heads):
            own = (block_lane >= part * head_dim) & (block_lane < (part + 1) * head_dim)
            stacked.append(queries[:, lanes] * own.astype(F32).astype(BF16))
        logits = lax.dot_general(
            keys[:, lanes], jnp.concatenate(stacked, axis=0), NT, preferred_element_type=F32
        )
        attend = softmax_down(logits, allowed)
        mixed = matmul(turned[lanes], attend)
        for part in range(block_heads):
            pieces.append(
                mixed[part * head_dim : (part + 1) * head_dim, part * rows : (part + 1) * rows]
            )
    context = jnp.concatenate(pieces, axis=0).T.astype(BF16)
    after_time = initial + matmul(context, temporal_out_ref[...])
    second = layer_norm(after_time, as_row(hidden_gain_ref)).astype(BF16)
    hidden = jax.nn.gelu(matmul(second, hidden_in_ref[...])).astype(BF16)
    result = (after_time + matmul(hidden, hidden_out_ref[...])).astype(BF16).astype(F32)
    headed = layer_norm(result, as_row(head_gain_ref)).astype(BF16)
    branch_velocity = matmul(headed, head_out_ref[...]).reshape(rows // period, period, width)
    conditional = branch_velocity[:, :share]
    empty = branch_velocity[:, share:]
    out_ref[...] = (empty + GUIDE * (conditional - empty)).astype(BF16)


def whole(memory_space=pltpu.VMEM):
    return pl.BlockSpec(memory_space=memory_space)


def body(
    groups,
    x_state,
    noise_field,
    rotations,
    translations,
    residue_types,
    pocket_mask,
    type_table,
    null_embed,
    spatial_gain,
    spatial_proj,
    spatial_points,
    spatial_gamma,
    spatial_out,
    temporal_gain,
    temporal_proj,
    temporal_out,
    hidden_gain,
    hidden_in,
    hidden_out,
    head_gain,
    head_out,
):
    frames, residues, width = x_state.shape
    share = residues // groups
    period = BRANCHES * share
    sources = (
        x_state,
        type_table,
        residue_types[None],
        null_embed,
        spatial_gain,
        rotations,
        translations,
        pocket_mask[None],
        spatial_proj,
        spatial_out,
        spatial_points.T,
    )
    slots = 2 * (width // LANES)
    later = (temporal_proj, temporal_out, hidden_in, hidden_out, head_out)
    spatial, *later = pl.pallas_call(
        functools.partial(spatial_kernel, groups),
        out_shape=[pltpu.VMEM((groups, frames * period, width), BF16)]
        + [pltpu.VMEM(array.shape, array.dtype) for array in later],
        in_specs=[whole(pltpu.SMEM)] + [whole(pl.ANY)] * (len(sources) + len(later)),
        out_specs=[whole()] * (1 + len(later)),
        scratch_shapes=[pltpu.VMEM(array.shape, array.dtype) for array in sources[:-1]]
        + [
            pltpu.VMEM((slots * SLOT, width), BF16),
            pltpu.VMEM((16, residues), F32),
            pltpu.VMEM((groups, frames * period, width), F32),
            pltpu.SemaphoreType.DMA((len(sources) - 1 + slots + len(later),)),
        ],
        compiler_params=pltpu.CompilerParams(vmem_limit_bytes=SPATIAL_VMEM),
        name="spatial",
    )(spatial_gamma, *sources, *later)
    arrived = lax.all_to_all(spatial, "seq", split_axis=0, concat_axis=0, tiled=True)
    proj_local, out_local, in_local, hidden_local, head_local = later
    guided = pl.pallas_call(
        functools.partial(temporal_kernel, period),
        out_shape=pltpu.VMEM((groups * frames, share, width), BF16),
        in_specs=[whole()] * 9,
        out_specs=whole(),
        compiler_params=pltpu.CompilerParams(vmem_limit_bytes=TEMPORAL_VMEM),
        name="temporal",
    )(
        arrived,
        temporal_gain,
        proj_local,
        out_local,
        hidden_gain,
        in_local,
        hidden_local,
        head_gain,
        head_local,
    )
    velocity = lax.all_to_all(guided, "seq", split_axis=0, concat_axis=1, tiled=True)
    x_next = (
        x_state.astype(F32)
        + STEP_SIZE * velocity.astype(F32)
        + NOISE_SCALE * noise_field.astype(F32)
    ).astype(BF16)
    return (x_next, velocity)


def solution(mesh):
    tokens = P(("parts", "seq"), None, None)
    geometry = P(None, ("parts", "seq"), None)
    return jax.shard_map(
        functools.partial(body, mesh.shape["seq"]),
        mesh=mesh,
        in_specs=(tokens, tokens, geometry, geometry, P("parts"), P("parts")) + (P(),) * 15,
        out_specs=(tokens, tokens),
        check_vma=False,
    )
```

```python
import functools
import math

import jax
import jax.numpy as jnp
from jax import lax
from jax.experimental import pallas as pl
from jax.experimental.pallas import tpu as pltpu
from jax.sharding import PartitionSpec as P

THEADS = 6
BRANCHES = 2
CORES = 2

WEIGHT_LOGIT = 0.7071067811865476
WEIGHT_POINT = 0.23570226039551584
GUIDE = 2.0
STEP_SIZE = 0.25
NOISE_SCALE = 0.2
EPSILON = 1e-05

BF16 = jnp.bfloat16
F32 = jnp.float32
LANES = 128
SLOT = 64
SPATIAL_VMEM = 56 * 2**20
TEMPORAL_VMEM = 40 * 2**20
NT = (((1,), (1,)), ((), ()))


def layer_norm(values, scale_gain):
    average = jnp.mean(values, axis=-1, keepdims=True)
    centered = values - average
    spread = jnp.mean(centered * centered, axis=-1, keepdims=True)
    return centered * lax.rsqrt(spread + EPSILON) * scale_gain


def as_row(ref):
    return ref[...].reshape(1, ref.shape[0])


def matmul(left, right):
    return jnp.dot(left, right, preferred_element_type=F32)


def iota(shape, axis):
    return lax.broadcasted_iota(jnp.int32, shape, axis)


def softmax_down(logits, allowed):
    logits = jnp.where(allowed, logits, -jnp.inf)
    powers = jnp.exp(logits - jnp.max(logits, axis=0, keepdims=True))
    return (powers * (1.0 / jnp.sum(powers, axis=0, keepdims=True))).astype(BF16)


def spatial_kernel(groups, gamma_ref, *refs):
    sources, refs = refs[:11], refs[11:]
    later, refs = refs[:5], refs[5:]
    out_ref, later_out, refs = refs[0], refs[1:6], refs[6:]
    local, (columns_ref, sems) = refs[:11], refs[11:]
    (
        x_ref,
        table_ref,
        types_ref,
        null_ref,
        gain_ref,
        rotation_ref,
        translation_ref,
        mask_ref,
        proj_ref,
        spatial_out_ref,
        points_ref,
    ) = local
    frames, residues, width = x_ref.shape
    heads = gamma_ref.shape[0]
    head_dim = width // heads
    blocks = width // LANES
    block_heads = LANES // head_dim
    slot_rows = sources[-1].shape[0] // (2 * blocks)
    per_head = slot_rows // block_heads
    share = residues // groups
    fold = max(residues, LANES)
    stacked_rows = block_heads * residues
    point_scale = 0.5 * WEIGHT_LOGIT * WEIGHT_POINT

    pairs = list(zip(sources[:10], local[:10], strict=True))
    for slot in range(2 * blocks):
        pairs.append(
            (
                sources[-1].at[pl.ds(slot * slot_rows, slot_rows), :],
                points_ref.at[pl.ds(slot * SLOT, slot_rows), :],
            )
        )
    pairs += list(zip(later, later_out, strict=True))
    copies = [
        pltpu.make_async_copy(source, target, sems.at[index])
        for index, (source, target) in enumerate(pairs)
    ]
    first = 10 + 2 * blocks
    for copy in copies[:first]:
        copy.start()
    small, wide, after = copies[:8], [copies[8]] + copies[10 : 10 + 2 * blocks], copies[9]

    for slot in range(2 * blocks):
        points_ref[slot * SLOT + slot_rows : (slot + 1) * SLOT, :] = jnp.zeros(
            (SLOT - slot_rows, width), BF16
        )
    lane = iota((1, LANES), 1)
    low = lane < SLOT
    place = lane % SLOT
    component = jnp.where(place < slot_rows, place % 3, 3)
    in_first = (place >= slot_rows) & (place < slot_rows + block_heads)
    in_second = (place >= slot_rows + block_heads) & (place < slot_rows + 2 * block_heads)
    in_norm = in_first | in_second
    member, block_member = [], []
    for part in range(block_heads):
        own = (
            ((place >= part * per_head) & (place < (part + 1) * per_head))
            | (place == slot_rows + part)
            | (place == slot_rows + block_heads + part)
        )
        member.append(own)
        block_member.append((lane >= part * head_dim) & (lane < (part + 1) * head_dim))
    both_member = [
        jnp.concatenate([left, right], axis=1).astype(F32).astype(BF16)
        for left, right in zip(block_member, member, strict=True)
    ]
    gamma_lanes = []
    for block in range(blocks):
        gamma = jnp.zeros((1, LANES), F32)
        for part in range(block_heads):
            gamma = jnp.where(member[part], gamma_ref[block * block_heads + part], gamma)
        gamma_lanes.append(gamma * point_scale)
    column = iota((LANES, LANES), 1) % SLOT - slot_rows
    column = jnp.where(column >= block_heads, column - block_heads, column)
    row_head = iota((LANES, LANES), 0) // per_head
    gather_norm = (
        ((iota((LANES, LANES), 0) < slot_rows) & (row_head == column) & in_norm)
        .astype(F32)
        .astype(BF16)
    )
    diagonal = iota((LANES, stacked_rows), 0) // head_dim == (
        iota((LANES, stacked_rows), 1) // residues
    )
    same = iota((residues, stacked_rows), 0) == iota((residues, stacked_rows), 1) % residues
    columns_ref[...] = jnp.zeros_like(columns_ref)

    for copy in small:
        copy.wait()
    kinds = table_ref.shape[0]
    onehot = (iota((kinds, residues), 0) == types_ref[...]).astype(F32).T.astype(BF16)
    conditional = matmul(onehot, table_ref[...])
    empty = as_row(null_ref).astype(F32)

    tiles = []
    for frame in range(frames):
        state = x_ref[frame].astype(F32)
        initial = jnp.concatenate([state + conditional, state + empty], axis=0)
        normed = layer_norm(initial, as_row(gain_ref)).astype(BF16)

        columns_ref[0:9, :] = rotation_ref[:, frame, :]
        moved = translation_ref[:, frame, :]
        columns_ref[9:12, :] = moved - jnp.mean(moved, axis=1, keepdims=True)
        columns_ref[12:13, :] = mask_ref[...].astype(F32)
        columns = columns_ref[...].T
        allowed = (columns[:, 12:13] == 1.0) | same
        factors = []
        for step in range(-2, 3):
            factor = jnp.zeros((residues, LANES), F32)
            for row in range(3):
                if 0 <= row + step < 3:
                    entry = 3 * row + row + step
                    factor = jnp.where(component == row, columns[:, entry : entry + 1], factor)
            factors.append(jnp.concatenate([factor] * BRANCHES, axis=0))
        anchor = jnp.zeros((residues, LANES), F32)
        for row in range(3):
            anchor = jnp.where(component == row, columns[:, 9 + row : 10 + row], anchor)
        anchor = jnp.concatenate([anchor] * BRANCHES, axis=0)

        if frame == 0:
            for copy in wide:
                copy.wait()
            for copy in copies[first:]:
                copy.start()
        points = lax.dot_general(normed, points_ref[...], NT, preferred_element_type=F32)
        projected = matmul(normed, proj_ref[...])

        slots = []
        for pair in range(blocks):
            lanes = points[:, pair * LANES : (pair + 1) * LANES]
            placed = anchor + factors[2] * lanes
            for step in (-2, -1, 1, 2):
                placed = placed + factors[step + 2] * pltpu.roll(lanes, (-step) % LANES, 1)
            swapped = pltpu.roll(placed, SLOT, 1)
            slots += [jnp.where(low, placed, swapped), jnp.where(low, swapped, placed)]

        query_feature, key_first, key_second = [], [], []
        for block in range(blocks):
            feature = jnp.where(in_norm, 1.0, slots[block] * (2.0 * gamma_lanes[block]))
            high = feature.astype(BF16)
            rest = (feature - high.astype(F32)).astype(BF16)
            query_feature.append(jnp.where(low, high, rest))

            feature = slots[blocks + block]
            square = feature * feature
            square_high = square.astype(BF16)
            rest = square - square_high.astype(F32)
            square_middle = rest.astype(BF16)
            square_low = (rest - square_middle.astype(F32)).astype(BF16)
            norm = (
                matmul(square_high, gather_norm)
                + matmul(square_middle, gather_norm)
                + matmul(square_low, gather_norm)
            )
            feature = feature - norm * gamma_lanes[block]
            high = feature.astype(BF16)
            rest = feature - high.astype(F32)
            middle = rest.astype(BF16)
            last = (rest - middle.astype(F32)).astype(BF16)
            key_first.append(jnp.where(in_second, last, high))
            key_second.append(jnp.where(low & ~in_second, middle, jnp.zeros_like(middle)))

        queries = (
            projected[:, :width].astype(BF16) * jnp.asarray(WEIGHT_LOGIT / math.sqrt(head_dim), BF16)
        )
        keys = projected[:, width : 2 * width].astype(BF16)
        values = projected[:, 2 * width :].astype(BF16).astype(F32)
        nothing = jnp.zeros((residues, LANES), BF16)

        contexts = []
        for branch in range(BRANCHES):
            rows = slice(branch * residues, (branch + 1) * residues)
            turned = values[rows].T.astype(BF16)
            pieces = []
            for block in range(blocks):
                lanes = slice(block * LANES, (block + 1) * LANES)
                left = jnp.concatenate(
                    [
                        jnp.concatenate([keys[rows, lanes], key_first[block][rows]], axis=1),
                        jnp.concatenate([nothing, key_second[block][rows]], axis=1),
                    ],
                    axis=0,
                )
                right = jnp.concatenate([queries[rows, lanes], query_feature[block][rows]], axis=1)
                right = jnp.concatenate([right * own for own in both_member], axis=0)
                logits = lax.dot_general(left, right, NT, preferred_element_type=F32)
                attend = softmax_down(logits[:residues] + logits[residues:], allowed)
                mixed = jnp.where(diagonal, matmul(turned[lanes], attend), 0.0)
                folded = mixed[:, :fold]
                for start in range(fold, stacked_rows, fold):
                    folded = folded + mixed[:, start : start + fold]
                pieces.append(folded)
            contexts.append(jnp.concatenate(pieces, axis=0).T.astype(BF16))
        if frame == 0:
            after.wait()
        update = matmul(jnp.concatenate(contexts, axis=0), spatial_out_ref[...])
        totals = []
        for branch in range(BRANCHES):
            total = initial[branch * residues : (branch + 1) * residues]
            for start in range(0, fold, residues):
                begin = branch * fold + start
                total = total + update[begin : begin + residues]
            totals.append(total)
        tiles.append(
            [
                jnp.concatenate(
                    [total[group * share : (group + 1) * share] for total in totals], axis=0
                )
                for group in range(groups)
            ]
        )
    first_core = lax.axis_index("seq") % CORES == 0
    for pair in range(groups // CORES):
        left, right = (
            jnp.concatenate([tile[CORES * pair + core] for tile in tiles], axis=0)
            for core in range(CORES)
        )
        out_ref[pair, 0] = jnp.where(first_core, left, right).astype(BF16)
        out_ref[pair, 1] = jnp.where(first_core, right, left).astype(BF16)
    for copy in copies[first:]:
        copy.wait()


def temporal_kernel(
    period,
    own_ref,
    other_ref,
    gain_ref,
    proj_ref,
    temporal_out_ref,
    hidden_gain_ref,
    hidden_in_ref,
    hidden_out_ref,
    head_gain_ref,
    head_out_ref,
    out_ref,
):
    pairs, depth, width = other_ref.shape
    rows = CORES * pairs * depth
    head_dim = width // THEADS
    block_heads = LANES // head_dim
    share = period // BRANCHES

    initial = jnp.concatenate(
        [
            own_ref[:, 0].astype(F32).reshape(rows // CORES, width),
            other_ref[...].astype(F32).reshape(rows // CORES, width),
        ],
        axis=0,
    )
    normed = layer_norm(initial, as_row(gain_ref)).astype(BF16)
    projected = matmul(normed, proj_ref[...])
    queries = projected[:, :width].astype(BF16) * jnp.asarray(1.0 / math.sqrt(head_dim), BF16)
    keys = projected[:, width : 2 * width].astype(BF16)
    turned = projected[:, 2 * width :].astype(BF16).astype(F32).T.astype(BF16)
    block_lane = iota((1, LANES), 1)
    allowed = (
        iota((rows, block_heads * rows), 0) % period == iota((rows, block_heads * rows), 1) % period
    )
    pieces = []
    for block in range(width // LANES):
        lanes = slice(block * LANES, (block + 1) * LANES)
        stacked = []
        for part in range(block_heads):
            own = (block_lane >= part * head_dim) & (block_lane < (part + 1) * head_dim)
            stacked.append(queries[:, lanes] * own.astype(F32).astype(BF16))
        logits = lax.dot_general(
            keys[:, lanes], jnp.concatenate(stacked, axis=0), NT, preferred_element_type=F32
        )
        attend = softmax_down(logits, allowed)
        mixed = matmul(turned[lanes], attend)
        for part in range(block_heads):
            pieces.append(
                mixed[part * head_dim : (part + 1) * head_dim, part * rows : (part + 1) * rows]
            )
    context = jnp.concatenate(pieces, axis=0).T.astype(BF16)
    after_time = initial + matmul(context, temporal_out_ref[...])
    second = layer_norm(after_time, as_row(hidden_gain_ref)).astype(BF16)
    hidden = jax.nn.gelu(matmul(second, hidden_in_ref[...])).astype(BF16)
    result = (after_time + matmul(hidden, hidden_out_ref[...])).astype(BF16).astype(F32)
    headed = layer_norm(result, as_row(head_gain_ref)).astype(BF16)
    branch_velocity = matmul(headed, head_out_ref[...]).reshape(rows // period, period, width)
    conditional = branch_velocity[:, :share]
    empty = branch_velocity[:, share:]
    guided = (empty + GUIDE * (conditional - empty)).astype(BF16)
    frames = depth // period
    for core in range(CORES):
        for pair in range(pairs):
            for frame in range(frames):
                out_ref[pair, core, frame * share : (frame + 1) * share, :] = guided[
                    (core * pairs + pair) * frames + frame
                ]


def exchange(array):
    count = lax.axis_size("seq")
    same_core = [list(range(core, count, CORES)) for core in range(CORES)]
    array = lax.all_to_all(
        array, "seq", split_axis=0, concat_axis=0, tiled=True, axis_index_groups=same_core
    )
    sibling = [(source, source + 1 if source % CORES == 0 else source - 1) for source in range(count)]
    return array, lax.ppermute(array[:, 1], "seq", sibling)


def whole(memory_space=pltpu.VMEM):
    return pl.BlockSpec(memory_space=memory_space)


def body(
    groups,
    x_state,
    noise_field,
    rotations,
    translations,
    residue_types,
    pocket_mask,
    type_table,
    null_embed,
    spatial_gain,
    spatial_proj,
    spatial_points,
    spatial_gamma,
    spatial_out,
    temporal_gain,
    temporal_proj,
    temporal_out,
    hidden_gain,
    hidden_in,
    hidden_out,
    head_gain,
    head_out,
):
    frames, residues, width = x_state.shape
    share = residues // groups
    period = BRANCHES * share
    sources = (
        x_state,
        type_table,
        residue_types[None],
        null_embed,
        spatial_gain,
        rotations,
        translations,
        pocket_mask[None],
        spatial_proj,
        spatial_out,
        spatial_points.T,
    )
    slots = 2 * (width // LANES)
    later = (temporal_proj, temporal_out, hidden_in, hidden_out, head_out)
    spatial, *later = pl.pallas_call(
        functools.partial(spatial_kernel, groups),
        out_shape=[pltpu.VMEM((groups // CORES, CORES, frames * period, width), BF16)]
        + [pltpu.VMEM(array.shape, array.dtype) for array in later],
        in_specs=[whole(pltpu.SMEM)] + [whole(pl.ANY)] * (len(sources) + len(later)),
        out_specs=[whole()] * (1 + len(later)),
        scratch_shapes=[pltpu.VMEM(array.shape, array.dtype) for array in sources[:-1]]
        + [
            pltpu.VMEM((slots * SLOT, width), BF16),
            pltpu.VMEM((16, residues), F32),
            pltpu.SemaphoreType.DMA((len(sources) - 1 + slots + len(later),)),
        ],
        compiler_params=pltpu.CompilerParams(vmem_limit_bytes=SPATIAL_VMEM),
        name="spatial",
    )(spatial_gamma, *sources, *later)
    proj_local, out_local, in_local, hidden_local, head_local = later
    guided = pl.pallas_call(
        functools.partial(temporal_kernel, period),
        out_shape=pltpu.VMEM((groups // CORES, CORES, frames * share, width), BF16),
        in_specs=[whole()] * 10,
        out_specs=whole(),
        compiler_params=pltpu.CompilerParams(vmem_limit_bytes=TEMPORAL_VMEM),
        name="temporal",
    )(
        *exchange(spatial),
        temporal_gain,
        proj_local,
        out_local,
        hidden_gain,
        in_local,
        hidden_local,
        head_gain,
        head_local,
    )
    own, other = exchange(guided)
    own = own[:, 0]
    first_core = lax.axis_index("seq") % CORES == 0
    velocity = jnp.stack(
        [jnp.where(first_core, own, other), jnp.where(first_core, other, own)], axis=1
    )
    velocity = jnp.moveaxis(velocity.reshape(groups, frames, share, width), 1, 0).reshape(
        x_state.shape
    )
    x_next = (
        x_state.astype(F32)
        + STEP_SIZE * velocity.astype(F32)
        + NOISE_SCALE * noise_field.astype(F32)
    ).astype(BF16)
    return (x_next, velocity)


def solution(mesh):
    tokens = P(("parts", "seq"), None, None)
    geometry = P(None, ("parts", "seq"), None)
    return jax.shard_map(
        functools.partial(body, mesh.shape["seq"]),
        mesh=mesh,
        in_specs=(tokens, tokens, geometry, geometry, P("parts"), P("parts")) + (P(),) * 15,
        out_specs=(tokens, tokens),
        check_vma=False,
    )
```

```python
import functools
import math

import jax
import jax.numpy as jnp
from jax import lax
from jax.experimental import pallas as pl
from jax.experimental.pallas import tpu as pltpu
from jax.sharding import PartitionSpec as P

THEADS = 6
BRANCHES = 2

WEIGHT_LOGIT = 0.7071067811865476
WEIGHT_POINT = 0.23570226039551584
GUIDE = 2.0
STEP_SIZE = 0.25
NOISE_SCALE = 0.2
EPSILON = 1e-05

BF16 = jnp.bfloat16
F32 = jnp.float32
LANES = 128
SLOT = 64
SPATIAL_VMEM = 56 * 2**20
TEMPORAL_VMEM = 40 * 2**20
NT = (((1,), (1,)), ((), ()))


def layer_norm(values, scale_gain):
    average = jnp.mean(values, axis=-1, keepdims=True)
    centered = values - average
    spread = jnp.mean(centered * centered, axis=-1, keepdims=True)
    return centered * lax.rsqrt(spread + EPSILON) * scale_gain


def as_row(ref):
    return ref[...].reshape(1, ref.shape[0])


def matmul(left, right):
    return jnp.dot(left, right, preferred_element_type=F32)


def iota(shape, axis):
    return lax.broadcasted_iota(jnp.int32, shape, axis)


def softmax_down(logits, allowed):
    logits = jnp.where(allowed, logits, -jnp.inf)
    powers = jnp.exp(logits - jnp.max(logits, axis=0, keepdims=True))
    return powers.astype(BF16), 1.0 / jnp.sum(powers, axis=0, keepdims=True)


def spatial_kernel(groups, gamma_ref, *refs):
    sources, refs = refs[:11], refs[11:]
    later, refs = refs[:5], refs[5:]
    out_ref, later_out, refs = refs[0], refs[1:6], refs[6:]
    local, (columns_ref, sems) = refs[:11], refs[11:]
    (
        x_ref,
        table_ref,
        types_ref,
        null_ref,
        gain_ref,
        rotation_ref,
        translation_ref,
        mask_ref,
        proj_ref,
        spatial_out_ref,
        points_ref,
    ) = local
    frames, residues, width = x_ref.shape
    heads = gamma_ref.shape[0]
    head_dim = width // heads
    blocks = width // LANES
    block_heads = LANES // head_dim
    slot_rows = sources[-1].shape[0] // (2 * blocks)
    per_head = slot_rows // block_heads
    share = residues // groups
    fold = max(residues, LANES)
    stacked_rows = block_heads * residues
    point_scale = 0.5 * WEIGHT_LOGIT * WEIGHT_POINT

    pairs = list(zip(sources[:10], local[:10], strict=True))
    for slot in range(2 * blocks):
        pairs.append(
            (
                sources[-1].at[pl.ds(slot * slot_rows, slot_rows), :],
                points_ref.at[pl.ds(slot * SLOT, slot_rows), :],
            )
        )
    pairs += list(zip(later, later_out, strict=True))
    copies = [
        pltpu.make_async_copy(source, target, sems.at[index])
        for index, (source, target) in enumerate(pairs)
    ]
    first = 10 + 2 * blocks
    for copy in copies[:first]:
        copy.start()
    small, wide, after = copies[:8], [copies[8]] + copies[10 : 10 + 2 * blocks], copies[9]

    for slot in range(2 * blocks):
        points_ref[slot * SLOT + slot_rows : (slot + 1) * SLOT, :] = jnp.zeros(
            (SLOT - slot_rows, width), BF16
        )
    lane = iota((1, LANES), 1)
    low = lane < SLOT
    place = lane % SLOT
    component = jnp.where(place < slot_rows, place % 3, 3)
    member, block_member = [], []
    for part in range(block_heads):
        member.append((place >= part * per_head) & (place < (part + 1) * per_head))
        block_member.append((lane >= part * head_dim) & (lane < (part + 1) * head_dim))
    both_member = [
        jnp.concatenate([left, right, right], axis=1).astype(F32).astype(BF16)
        for left, right in zip(block_member, member, strict=True)
    ]
    gamma_lanes = []
    for block in range(blocks):
        gamma = jnp.zeros((1, LANES), F32)
        for part in range(block_heads):
            gamma = jnp.where(member[part], gamma_ref[block * block_heads + part], gamma)
        gamma_lanes.append(gamma * point_scale)
    diagonal = iota((LANES, stacked_rows), 0) // head_dim == (
        iota((LANES, stacked_rows), 1) // residues
    )
    same = iota((residues, stacked_rows), 0) == iota((residues, stacked_rows), 1) % residues
    columns_ref[...] = jnp.zeros_like(columns_ref)

    for copy in small:
        copy.wait()
    kinds = table_ref.shape[0]
    onehot = (iota((kinds, residues), 0) == types_ref[...]).astype(F32).T.astype(BF16)
    conditional = matmul(onehot, table_ref[...])
    empty = as_row(null_ref).astype(F32)

    tiles = []
    for frame in range(frames):
        state = x_ref[frame].astype(F32)
        initial = jnp.concatenate([state + conditional, state + empty], axis=0)
        normed = layer_norm(initial, as_row(gain_ref)).astype(BF16)

        columns_ref[0:9, :] = rotation_ref[:, frame, :]
        moved = translation_ref[:, frame, :]
        columns_ref[9:12, :] = moved - jnp.mean(moved, axis=1, keepdims=True)
        columns_ref[12:13, :] = mask_ref[...].astype(F32)
        columns = columns_ref[...].T
        allowed = (columns[:, 12:13] == 1.0) | same
        factors = []
        for step in range(-2, 3):
            factor = jnp.zeros((residues, LANES), F32)
            for row in range(3):
                if 0 <= row + step < 3:
                    entry = 3 * row + row + step
                    factor = jnp.where(component == row, columns[:, entry : entry + 1], factor)
            factors.append(jnp.concatenate([factor] * BRANCHES, axis=0))
        anchor = jnp.zeros((residues, LANES), F32)
        for row in range(3):
            anchor = jnp.where(component == row, columns[:, 9 + row : 10 + row], anchor)
        anchor = jnp.concatenate([anchor] * BRANCHES, axis=0)

        if frame == 0:
            for copy in wide:
                copy.wait()
            for copy in copies[first:]:
                copy.start()
        points = lax.dot_general(normed, points_ref[...], NT, preferred_element_type=F32)
        projected = matmul(normed, proj_ref[...])

        slots = []
        for pair in range(blocks):
            lanes = points[:, pair * LANES : (pair + 1) * LANES]
            placed = anchor + factors[2] * lanes
            for step in (-2, -1, 1, 2):
                placed = placed + factors[step + 2] * pltpu.roll(lanes, (-step) % LANES, 1)
            swapped = pltpu.roll(placed, SLOT, 1)
            slots += [jnp.where(low, placed, swapped), jnp.where(low, swapped, placed)]

        query_feature, key_first, key_second = [], [], []
        nothing = jnp.zeros((BRANCHES * residues, LANES), BF16)
        ones = jnp.ones((residues, LANES), BF16)
        for block in range(blocks):
            feature = slots[block] * (2.0 * gamma_lanes[block])
            high = feature.astype(BF16)
            rest = (feature - high.astype(F32)).astype(BF16)
            query_feature.append(jnp.where(low, high, rest))

            feature = slots[blocks + block]
            high = feature.astype(BF16)
            rest = (feature - high.astype(F32)).astype(BF16)
            key_first.append([high])
            key_second.append([jnp.where(low, rest, nothing)])
            square = feature * feature * (-gamma_lanes[block])
            high = square.astype(BF16)
            rest = square - high.astype(F32)
            middle = rest.astype(BF16)
            last = (rest - middle.astype(F32)).astype(BF16)
            key_first[block].append(jnp.where(low, high, middle))
            key_second[block].append(jnp.where(low, last, nothing))

        queries = (
            projected[:, :width].astype(BF16) * jnp.asarray(WEIGHT_LOGIT / math.sqrt(head_dim), BF16)
        )
        keys = projected[:, width : 2 * width].astype(BF16)
        values = projected[:, 2 * width :].astype(BF16)
        contexts = []
        for branch in range(BRANCHES):
            rows = slice(branch * residues, (branch + 1) * residues)
            turned = values[rows].T
            pieces = []
            for block in range(blocks):
                lanes = slice(block * LANES, (block + 1) * LANES)
                left = jnp.concatenate(
                    [
                        jnp.concatenate(
                            [piece[rows] for piece in (keys[:, lanes], *key_first[block])], axis=1
                        ),
                        jnp.concatenate(
                            [piece[rows] for piece in (nothing, *key_second[block])], axis=1
                        ),
                    ],
                    axis=0,
                )
                right = jnp.concatenate(
                    [queries[rows, lanes], query_feature[block][rows], ones], axis=1
                )
                right = jnp.concatenate([right * own for own in both_member], axis=0)
                logits = lax.dot_general(left, right, NT, preferred_element_type=F32)
                powers, scale = softmax_down(logits[:residues] + logits[residues:], allowed)
                mixed = jnp.where(diagonal, matmul(turned[lanes], powers) * scale, 0.0)
                folded = mixed[:, :fold]
                for start in range(fold, stacked_rows, fold):
                    folded = folded + mixed[:, start : start + fold]
                pieces.append(folded)
            contexts.append(jnp.concatenate(pieces, axis=0).astype(BF16).T)
        if frame == 0:
            after.wait()
        update = matmul(jnp.concatenate(contexts, axis=0), spatial_out_ref[...])
        totals = []
        for branch in range(BRANCHES):
            total = initial[branch * residues : (branch + 1) * residues]
            for start in range(0, fold, residues):
                begin = branch * fold + start
                total = total + update[begin : begin + residues]
            totals.append(total)
        tiles.append(
            [
                jnp.concatenate(
                    [total[group * share : (group + 1) * share] for total in totals], axis=0
                )
                for group in range(groups)
            ]
        )
    for group in range(groups):
        out_ref[group] = jnp.concatenate([tile[group] for tile in tiles], axis=0).astype(BF16)
    for copy in copies[first:]:
        copy.wait()


def temporal_kernel(
    period,
    x_ref,
    gain_ref,
    proj_ref,
    temporal_out_ref,
    hidden_gain_ref,
    hidden_in_ref,
    hidden_out_ref,
    head_gain_ref,
    head_out_ref,
    out_ref,
):
    groups, depth, width = x_ref.shape
    rows = groups * depth
    head_dim = width // THEADS
    block_heads = LANES // head_dim
    share = period // BRANCHES

    initial = x_ref[...].astype(F32).reshape(rows, width)
    normed = layer_norm(initial, as_row(gain_ref)).astype(BF16)
    projected = matmul(normed, proj_ref[...])
    queries = projected[:, :width].astype(BF16) * jnp.asarray(1.0 / math.sqrt(head_dim), BF16)
    keys = projected[:, width : 2 * width].astype(BF16)
    turned = projected[:, 2 * width :].astype(BF16).T
    block_lane = iota((1, LANES), 1)
    allowed = (
        iota((rows, block_heads * rows), 0) % period == iota((rows, block_heads * rows), 1) % period
    )
    pieces = []
    for block in range(width // LANES):
        lanes = slice(block * LANES, (block + 1) * LANES)
        stacked = []
        for part in range(block_heads):
            own = (block_lane >= part * head_dim) & (block_lane < (part + 1) * head_dim)
            stacked.append(queries[:, lanes] * own.astype(F32).astype(BF16))
        logits = lax.dot_general(
            keys[:, lanes], jnp.concatenate(stacked, axis=0), NT, preferred_element_type=F32
        )
        powers, scale = softmax_down(logits, allowed)
        mixed = matmul(turned[lanes], powers) * scale
        for part in range(block_heads):
            pieces.append(
                mixed[part * head_dim : (part + 1) * head_dim, part * rows : (part + 1) * rows]
            )
    context = jnp.concatenate(pieces, axis=0).astype(BF16).T
    after_time = initial + matmul(context, temporal_out_ref[...])
    second = layer_norm(after_time, as_row(hidden_gain_ref)).astype(BF16)
    hidden = jax.nn.gelu(matmul(second, hidden_in_ref[...])).astype(BF16)
    result = (after_time + matmul(hidden, hidden_out_ref[...])).astype(BF16).astype(F32)
    headed = layer_norm(result, as_row(head_gain_ref)).astype(BF16)
    branch_velocity = matmul(headed, head_out_ref[...]).reshape(rows // period, period, width)
    conditional = branch_velocity[:, :share]
    empty = branch_velocity[:, share:]
    out_ref[...] = (empty + GUIDE * (conditional - empty)).astype(BF16)


def whole(memory_space=pltpu.VMEM):
    return pl.BlockSpec(memory_space=memory_space)


def body(
    groups,
    x_state,
    noise_field,
    rotations,
    translations,
    residue_types,
    pocket_mask,
    type_table,
    null_embed,
    spatial_gain,
    spatial_proj,
    spatial_points,
    spatial_gamma,
    spatial_out,
    temporal_gain,
    temporal_proj,
    temporal_out,
    hidden_gain,
    hidden_in,
    hidden_out,
    head_gain,
    head_out,
):
    frames, residues, width = x_state.shape
    share = residues // groups
    period = BRANCHES * share
    sources = (
        x_state,
        type_table,
        residue_types[None],
        null_embed,
        spatial_gain,
        rotations,
        translations,
        pocket_mask[None],
        spatial_proj,
        spatial_out,
        spatial_points.T,
    )
    slots = 2 * (width // LANES)
    later = (temporal_proj, temporal_out, hidden_in, hidden_out, head_out)
    spatial, *later = pl.pallas_call(
        functools.partial(spatial_kernel, groups),
        out_shape=[pltpu.VMEM((groups, frames * period, width), BF16)]
        + [pltpu.VMEM(array.shape, array.dtype) for array in later],
        in_specs=[whole(pltpu.SMEM)] + [whole(pl.ANY)] * (len(sources) + len(later)),
        out_specs=[whole()] * (1 + len(later)),
        scratch_shapes=[pltpu.VMEM(array.shape, array.dtype) for array in sources[:-1]]
        + [
            pltpu.VMEM((slots * SLOT, width), BF16),
            pltpu.VMEM((16, residues), F32),
            pltpu.SemaphoreType.DMA((len(sources) - 1 + slots + len(later),)),
        ],
        compiler_params=pltpu.CompilerParams(vmem_limit_bytes=SPATIAL_VMEM),
        name="spatial",
    )(spatial_gamma, *sources, *later)
    arrived = lax.all_to_all(spatial, "seq", split_axis=0, concat_axis=0, tiled=True)
    proj_local, out_local, in_local, hidden_local, head_local = later
    guided = pl.pallas_call(
        functools.partial(temporal_kernel, period),
        out_shape=pltpu.VMEM((groups * frames, share, width), BF16),
        in_specs=[whole()] * 9,
        out_specs=whole(),
        compiler_params=pltpu.CompilerParams(vmem_limit_bytes=TEMPORAL_VMEM),
        name="temporal",
    )(
        arrived,
        temporal_gain,
        proj_local,
        out_local,
        hidden_gain,
        in_local,
        hidden_local,
        head_gain,
        head_local,
    )
    velocity = lax.all_to_all(guided, "seq", split_axis=0, concat_axis=1, tiled=True)
    x_next = (
        x_state.astype(F32)
        + STEP_SIZE * velocity.astype(F32)
        + NOISE_SCALE * noise_field.astype(F32)
    ).astype(BF16)
    return (x_next, velocity)


def solution(mesh):
    tokens = P(("parts", "seq"), None, None)
    geometry = P(None, ("parts", "seq"), None)
    return jax.shard_map(
        functools.partial(body, mesh.shape["seq"]),
        mesh=mesh,
        in_specs=(tokens, tokens, geometry, geometry, P("parts"), P("parts")) + (P(),) * 15,
        out_specs=(tokens, tokens),
        check_vma=False,
    )
```

```python
import functools
import math

import jax
import jax.numpy as jnp
from jax import lax
from jax.experimental import pallas as pl
from jax.experimental.pallas import tpu as pltpu
from jax.sharding import PartitionSpec as P

THEADS = 6
BRANCHES = 2

WEIGHT_LOGIT = 0.7071067811865476
WEIGHT_POINT = 0.23570226039551584
GUIDE = 2.0
STEP_SIZE = 0.25
NOISE_SCALE = 0.2
EPSILON = 1e-05

BF16 = jnp.bfloat16
F32 = jnp.float32
LANES = 128
SLOT = 64
SPATIAL_VMEM = 56 * 2**20
TEMPORAL_VMEM = 40 * 2**20
NT = (((1,), (1,)), ((), ()))


def layer_norm(values, scale_gain):
    average = jnp.mean(values, axis=-1, keepdims=True)
    centered = values - average
    spread = jnp.mean(centered * centered, axis=-1, keepdims=True)
    return centered * lax.rsqrt(spread + EPSILON) * scale_gain


def as_row(ref):
    return ref[...].reshape(1, ref.shape[0])


def matmul(left, right):
    return jnp.dot(left, right, preferred_element_type=F32)


def iota(shape, axis):
    return lax.broadcasted_iota(jnp.int32, shape, axis)


def softmax_down(logits, allowed):
    logits = jnp.where(allowed, logits, -jnp.inf)
    powers = jnp.exp(logits - jnp.max(logits, axis=0, keepdims=True))
    return powers.astype(BF16), 1.0 / jnp.sum(powers, axis=0, keepdims=True)


def spatial_kernel(groups, gamma_ref, *refs):
    sources, refs = refs[:11], refs[11:]
    later, refs = refs[:5], refs[5:]
    out_ref, later_out, refs = refs[0], refs[1:6], refs[6:]
    local, (columns_ref, sems) = refs[:11], refs[11:]
    (
        x_ref,
        table_ref,
        types_ref,
        null_ref,
        gain_ref,
        rotation_ref,
        translation_ref,
        mask_ref,
        proj_ref,
        spatial_out_ref,
        points_ref,
    ) = local
    frames, residues, width = x_ref.shape
    heads = gamma_ref.shape[0]
    head_dim = width // heads
    blocks = width // LANES
    block_heads = LANES // head_dim
    slot_rows = sources[-1].shape[0] // (2 * blocks)
    per_head = slot_rows // block_heads
    share = residues // groups
    fold = max(residues, LANES)
    stacked_rows = block_heads * residues
    point_scale = 0.5 * WEIGHT_LOGIT * WEIGHT_POINT

    pairs = list(zip(sources[:10], local[:10], strict=True))
    for slot in range(2 * blocks):
        pairs.append(
            (
                sources[-1].at[pl.ds(slot * slot_rows, slot_rows), :],
                points_ref.at[pl.ds(slot * SLOT, slot_rows), :],
            )
        )
    pairs += list(zip(later, later_out, strict=True))
    copies = [
        pltpu.make_async_copy(source, target, sems.at[index])
        for index, (source, target) in enumerate(pairs)
    ]
    first = 10 + 2 * blocks
    for copy in copies[:first]:
        copy.start()
    small, wide, after = copies[:8], [copies[8]] + copies[10 : 10 + 2 * blocks], copies[9]

    for slot in range(2 * blocks):
        points_ref[slot * SLOT + slot_rows : (slot + 1) * SLOT, :] = jnp.zeros(
            (SLOT - slot_rows, width), BF16
        )
    lane = iota((1, LANES), 1)
    low = lane < SLOT
    place = lane % SLOT
    component = jnp.where(place < slot_rows, place % 3, 3)
    member, block_member = [], []
    for part in range(block_heads):
        member.append((place >= part * per_head) & (place < (part + 1) * per_head))
        block_member.append((lane >= part * head_dim) & (lane < (part + 1) * head_dim))
    both_member = [
        jnp.concatenate([left, right, right], axis=1).astype(F32).astype(BF16)
        for left, right in zip(block_member, member, strict=True)
    ]
    gamma_lanes = []
    for block in range(blocks):
        gamma = jnp.zeros((1, LANES), F32)
        for part in range(block_heads):
            gamma = jnp.where(member[part], gamma_ref[block * block_heads + part], gamma)
        gamma_lanes.append(gamma * point_scale)
    diagonal = iota((LANES, stacked_rows), 0) // head_dim == (
        iota((LANES, stacked_rows), 1) // residues
    )
    same = iota((residues, stacked_rows), 0) == iota((residues, stacked_rows), 1) % residues
    columns_ref[...] = jnp.zeros_like(columns_ref)

    for copy in small:
        copy.wait()
    kinds = table_ref.shape[0]
    onehot = (iota((kinds, residues), 0) == types_ref[...]).astype(F32).T.astype(BF16)
    conditional = matmul(onehot, table_ref[...])
    empty = as_row(null_ref).astype(F32)

    tiles = []
    for frame in range(frames):
        state = x_ref[frame].astype(F32)
        initial = jnp.concatenate([state + conditional, state + empty], axis=0)
        normed = layer_norm(initial, as_row(gain_ref)).astype(BF16)

        columns_ref[0:9, :] = rotation_ref[:, frame, :]
        moved = translation_ref[:, frame, :]
        columns_ref[9:12, :] = moved - jnp.mean(moved, axis=1, keepdims=True)
        columns_ref[12:13, :] = mask_ref[...].astype(F32)
        columns = columns_ref[...].T
        allowed = (columns[:, 12:13] == 1.0) | same
        factors = []
        for step in range(-2, 3):
            factor = jnp.zeros((residues, LANES), F32)
            for row in range(3):
                if 0 <= row + step < 3:
                    entry = 3 * row + row + step
                    factor = jnp.where(component == row, columns[:, entry : entry + 1], factor)
            factors.append(jnp.concatenate([factor] * BRANCHES, axis=0))
        anchor = jnp.zeros((residues, LANES), F32)
        for row in range(3):
            anchor = jnp.where(component == row, columns[:, 9 + row : 10 + row], anchor)
        anchor = jnp.concatenate([anchor] * BRANCHES, axis=0)

        if frame == 0:
            for copy in wide:
                copy.wait()
            for copy in copies[first:]:
                copy.start()
        points = lax.dot_general(normed, points_ref[...], NT, preferred_element_type=F32)
        projected = matmul(normed, proj_ref[...])

        slots = []
        for pair in range(blocks):
            lanes = points[:, pair * LANES : (pair + 1) * LANES]
            placed = anchor + factors[2] * lanes
            for step in (-2, -1, 1, 2):
                placed = placed + factors[step + 2] * pltpu.roll(lanes, (-step) % LANES, 1)
            swapped = pltpu.roll(placed, SLOT, 1)
            slots += [jnp.where(low, placed, swapped), jnp.where(low, swapped, placed)]

        query_feature, key_first, key_second = [], [], []
        nothing = jnp.zeros((BRANCHES * residues, LANES), BF16)
        ones = jnp.ones((residues, LANES), BF16)
        for block in range(blocks):
            feature = slots[block] * (2.0 * gamma_lanes[block])
            high = feature.astype(BF16)
            rest = (feature - high.astype(F32)).astype(BF16)
            query_feature.append(jnp.where(low, high, rest))

            feature = slots[blocks + block]
            high = feature.astype(BF16)
            rest = (feature - high.astype(F32)).astype(BF16)
            key_first.append([high])
            key_second.append([jnp.where(low, rest, nothing)])
            square = feature * feature * (-gamma_lanes[block])
            high = square.astype(BF16)
            rest = square - high.astype(F32)
            middle = rest.astype(BF16)
            last = (rest - middle.astype(F32)).astype(BF16)
            key_first[block].append(jnp.where(low, high, middle))
            key_second[block].append(jnp.where(low, last, nothing))

        queries = (
            projected[:, :width].astype(BF16) * jnp.asarray(WEIGHT_LOGIT / math.sqrt(head_dim), BF16)
        )
        keys = projected[:, width : 2 * width].astype(BF16)
        values = projected[:, 2 * width :].astype(BF16)
        contexts = []
        for branch in range(BRANCHES):
            rows = slice(branch * residues, (branch + 1) * residues)
            turned = values[rows].T
            pieces = []
            for block in range(blocks):
                lanes = slice(block * LANES, (block + 1) * LANES)
                left = jnp.concatenate(
                    [
                        jnp.concatenate(
                            [piece[rows] for piece in (keys[:, lanes], *key_first[block])], axis=1
                        ),
                        jnp.concatenate(
                            [piece[rows] for piece in (nothing, *key_second[block])], axis=1
                        ),
                    ],
                    axis=0,
                )
                right = jnp.concatenate(
                    [queries[rows, lanes], query_feature[block][rows], ones], axis=1
                )
                right = jnp.concatenate([right * own for own in both_member], axis=0)
                logits = lax.dot_general(left, right, NT, preferred_element_type=F32)
                powers, scale = softmax_down(logits[:residues] + logits[residues:], allowed)
                mixed = jnp.where(diagonal, matmul(turned[lanes], powers) * scale, 0.0)
                folded = mixed[:, :fold]
                for start in range(fold, stacked_rows, fold):
                    folded = folded + mixed[:, start : start + fold]
                pieces.append(folded)
            contexts.append(jnp.concatenate(pieces, axis=0).astype(BF16).T)
        if frame == 0:
            after.wait()
        update = matmul(jnp.concatenate(contexts, axis=0), spatial_out_ref[...])
        totals = []
        for branch in range(BRANCHES):
            total = initial[branch * residues : (branch + 1) * residues]
            for start in range(0, fold, residues):
                begin = branch * fold + start
                total = total + update[begin : begin + residues]
            totals.append(total)
        tiles.append(
            [
                jnp.concatenate(
                    [total[group * share : (group + 1) * share] for total in totals], axis=0
                )
                for group in range(groups)
            ]
        )
    for group in range(groups):
        out_ref[group] = jnp.concatenate([tile[group] for tile in tiles], axis=0).astype(BF16)
    for copy in copies[first:]:
        copy.wait()


def temporal_kernel(
    period,
    x_ref,
    gain_ref,
    proj_ref,
    temporal_out_ref,
    hidden_gain_ref,
    hidden_in_ref,
    hidden_out_ref,
    head_gain_ref,
    head_out_ref,
    out_ref,
    rows_ref,
):
    groups, depth, width = x_ref.shape
    rows = groups * depth
    head_dim = width // THEADS
    block_heads = LANES // head_dim
    share = period // BRANCHES

    initial = x_ref[...].astype(F32).reshape(rows, width)
    normed = layer_norm(initial, as_row(gain_ref)).astype(BF16)
    projected = matmul(normed, proj_ref[...])
    queries = projected[:, :width].astype(BF16) * jnp.asarray(1.0 / math.sqrt(head_dim), BF16)
    keys = projected[:, width : 2 * width].astype(BF16)
    turned = projected[:, 2 * width :].astype(BF16).T
    block_lane = iota((1, LANES), 1)
    allowed = (
        iota((rows, block_heads * rows), 0) % period == iota((rows, block_heads * rows), 1) % period
    )
    pieces = []
    for block in range(width // LANES):
        lanes = slice(block * LANES, (block + 1) * LANES)
        stacked = []
        for part in range(block_heads):
            own = (block_lane >= part * head_dim) & (block_lane < (part + 1) * head_dim)
            stacked.append(queries[:, lanes] * own.astype(F32).astype(BF16))
        logits = lax.dot_general(
            keys[:, lanes], jnp.concatenate(stacked, axis=0), NT, preferred_element_type=F32
        )
        powers, scale = softmax_down(logits, allowed)
        mixed = matmul(turned[lanes], powers) * scale
        for part in range(block_heads):
            pieces.append(
                mixed[part * head_dim : (part + 1) * head_dim, part * rows : (part + 1) * rows]
            )
    context = jnp.concatenate(pieces, axis=0).astype(BF16).T
    after_time = initial + matmul(context, temporal_out_ref[...])
    second = layer_norm(after_time, as_row(hidden_gain_ref)).astype(BF16)
    hidden = jax.nn.gelu(matmul(second, hidden_in_ref[...])).astype(BF16)
    result = (after_time + matmul(hidden, hidden_out_ref[...])).astype(BF16).astype(F32)
    headed = layer_norm(result, as_row(head_gain_ref)).astype(BF16)
    branch_velocity = matmul(headed, head_out_ref[...]).reshape(rows // period, period, width)
    conditional = branch_velocity[:, :share]
    empty = branch_velocity[:, share:]
    guided = empty + GUIDE * (conditional - empty)
    frames = depth // period
    for group in range(groups):
        for frame in range(frames):
            rows_ref[group, frame * share : (frame + 1) * share, :] = guided[group * frames + frame]
    me = lax.axis_index("seq")
    for group in range(groups):
        out_ref[group] = rows_ref[me ^ group].astype(BF16)


def update_kernel(x_ref, noise_ref, guided_ref, next_ref, velocity_ref, rows_ref):
    groups = guided_ref.shape[0]
    frames, residues, _ = x_ref.shape
    share = residues // groups
    me = lax.axis_index("seq")
    even = me % 2 == 0
    for frame in range(frames):
        rows = slice(frame * share, (frame + 1) * share)
        for pair in range(groups // 2):
            first = guided_ref[2 * pair, rows].astype(F32)
            second = guided_ref[2 * pair + 1, rows].astype(F32)
            rows_ref[(me // 2) ^ pair] = jnp.concatenate(
                [jnp.where(even, first, second), jnp.where(even, second, first)], axis=0
            )
        velocity = rows_ref[...].reshape(x_ref.shape[1:])
        velocity_ref[frame] = velocity.astype(BF16)
        next_ref[frame] = (
            x_ref[frame].astype(F32)
            + STEP_SIZE * velocity
            + NOISE_SCALE * noise_ref[frame].astype(F32)
        ).astype(BF16)


def exchange(array):
    count = array.shape[0]
    stride = count
    while stride > 1:
        radix = 4 if stride % 4 == 0 else 2
        stride //= radix
        view = array.reshape(count // (radix * stride), radix, stride, *array.shape[1:])
        parts = [view[:, 0]]
        for digit in range(1, radix):
            partners = [(source, source ^ (digit * stride)) for source in range(count)]
            parts.append(lax.ppermute(view[:, digit], "seq", partners))
        array = jnp.stack(parts, axis=1).reshape(array.shape)
    return array


def whole(memory_space=pltpu.VMEM):
    return pl.BlockSpec(memory_space=memory_space)


def body(
    groups,
    x_state,
    noise_field,
    rotations,
    translations,
    residue_types,
    pocket_mask,
    type_table,
    null_embed,
    spatial_gain,
    spatial_proj,
    spatial_points,
    spatial_gamma,
    spatial_out,
    temporal_gain,
    temporal_proj,
    temporal_out,
    hidden_gain,
    hidden_in,
    hidden_out,
    head_gain,
    head_out,
):
    frames, residues, width = x_state.shape
    share = residues // groups
    period = BRANCHES * share
    sources = (
        x_state,
        type_table,
        residue_types[None],
        null_embed,
        spatial_gain,
        rotations,
        translations,
        pocket_mask[None],
        spatial_proj,
        spatial_out,
        spatial_points.T,
    )
    slots = 2 * (width // LANES)
    later = (temporal_proj, temporal_out, hidden_in, hidden_out, head_out)
    spatial, *later = pl.pallas_call(
        functools.partial(spatial_kernel, groups),
        out_shape=[pltpu.VMEM((groups, frames * period, width), BF16)]
        + [pltpu.VMEM(array.shape, array.dtype) for array in later],
        in_specs=[whole(pltpu.SMEM)] + [whole(pl.ANY)] * (len(sources) + len(later)),
        out_specs=[whole()] * (1 + len(later)),
        scratch_shapes=[pltpu.VMEM(array.shape, array.dtype) for array in sources[:-1]]
        + [
            pltpu.VMEM((slots * SLOT, width), BF16),
            pltpu.VMEM((16, residues), F32),
            pltpu.SemaphoreType.DMA((len(sources) - 1 + slots + len(later),)),
        ],
        compiler_params=pltpu.CompilerParams(vmem_limit_bytes=SPATIAL_VMEM),
        name="spatial",
    )(spatial_gamma, *sources, *later)
    arrived = lax.all_to_all(spatial, "seq", split_axis=0, concat_axis=0, tiled=True)
    proj_local, out_local, in_local, hidden_local, head_local = later
    guided = pl.pallas_call(
        functools.partial(temporal_kernel, period),
        out_shape=pltpu.VMEM((groups, frames * share, width), BF16),
        in_specs=[whole()] * 9,
        out_specs=whole(),
        scratch_shapes=[pltpu.VMEM((groups, frames * share, width), F32)],
        compiler_params=pltpu.CompilerParams(vmem_limit_bytes=TEMPORAL_VMEM),
        name="temporal",
    )(
        arrived,
        temporal_gain,
        proj_local,
        out_local,
        hidden_gain,
        in_local,
        hidden_local,
        head_gain,
        head_local,
    )
    return tuple(
        pl.pallas_call(
            update_kernel,
            out_shape=[jax.ShapeDtypeStruct(x_state.shape, BF16)] * 2,
            in_specs=[whole()] * 3,
            out_specs=[whole()] * 2,
            scratch_shapes=[pltpu.VMEM((groups // 2, 2 * share, width), F32)],
            compiler_params=pltpu.CompilerParams(vmem_limit_bytes=TEMPORAL_VMEM),
            name="update",
        )(x_state, noise_field, exchange(guided))
    )


def solution(mesh):
    tokens = P(("parts", "seq"), None, None)
    geometry = P(None, ("parts", "seq"), None)
    return jax.shard_map(
        functools.partial(body, mesh.shape["seq"]),
        mesh=mesh,
        in_specs=(tokens, tokens, geometry, geometry, P("parts"), P("parts")) + (P(),) * 15,
        out_specs=(tokens, tokens),
        check_vma=False,
    )
```

```python
import functools
import math

import jax
import jax.numpy as jnp
from jax import lax
from jax.experimental import pallas as pl
from jax.experimental.pallas import tpu as pltpu
from jax.sharding import PartitionSpec as P

THEADS = 6
BRANCHES = 2

WEIGHT_LOGIT = 0.7071067811865476
WEIGHT_POINT = 0.23570226039551584
GUIDE = 2.0
STEP_SIZE = 0.25
NOISE_SCALE = 0.2
EPSILON = 1e-05

BF16 = jnp.bfloat16
F32 = jnp.float32
LANES = 128
SLOT = 64
CHUNKS = 4
SPATIAL_VMEM = 56 * 2**20
TEMPORAL_VMEM = 40 * 2**20
NT = (((1,), (1,)), ((), ()))


def layer_norm(values, scale_gain):
    average = jnp.mean(values, axis=-1, keepdims=True)
    centered = values - average
    spread = jnp.mean(centered * centered, axis=-1, keepdims=True)
    return centered * lax.rsqrt(spread + EPSILON) * scale_gain


def as_row(ref):
    return ref[...].reshape(1, ref.shape[0])


def matmul(left, right):
    return jnp.dot(left, right, preferred_element_type=F32)


def iota(shape, axis):
    return lax.broadcasted_iota(jnp.int32, shape, axis)


def softmax_down(logits, allowed):
    logits = jnp.where(allowed, logits, -jnp.inf)
    powers = jnp.exp(logits - jnp.max(logits, axis=0, keepdims=True))
    return powers.astype(BF16), 1.0 / jnp.sum(powers, axis=0, keepdims=True)


def spatial_kernel(groups, gamma_ref, *refs):
    sources, refs = refs[:11], refs[11:]
    later, refs = refs[:5], refs[5:]
    out_ref, later_out, refs = refs[0], refs[1:6], refs[6:]
    local, (columns_ref, sems) = refs[:11], refs[11:]
    (
        x_ref,
        table_ref,
        types_ref,
        null_ref,
        gain_ref,
        rotation_ref,
        translation_ref,
        mask_ref,
        proj_ref,
        spatial_out_ref,
        points_ref,
    ) = local
    frames, residues, width = x_ref.shape
    heads = gamma_ref.shape[0]
    head_dim = width // heads
    blocks = width // LANES
    block_heads = LANES // head_dim
    slot_rows = sources[-1].shape[0] // (2 * blocks)
    per_head = slot_rows // block_heads
    share = residues // groups
    fold = max(residues, LANES)
    stacked_rows = block_heads * residues
    point_scale = 0.5 * WEIGHT_LOGIT * WEIGHT_POINT

    proj_source, out_source, points_source = sources[8:]
    pairs = list(zip(sources[:8], local[:8], strict=True))
    for slot in range(2 * blocks):
        pairs.append(
            (
                points_source.at[pl.ds(slot * slot_rows, slot_rows), :],
                points_ref.at[pl.ds(slot * SLOT, slot_rows), :],
            )
        )
    rows = width // CHUNKS
    for chunk in range(CHUNKS):
        taken = pl.ds(chunk * rows, rows)
        pairs.append((proj_source.at[taken, :], proj_ref.at[taken, :]))
    pairs.append((out_source, spatial_out_ref))
    first = len(pairs)
    pairs += list(zip(later, later_out, strict=True))
    copies = [
        pltpu.make_async_copy(source, target, sems.at[index])
        for index, (source, target) in enumerate(pairs)
    ]
    for copy in copies[:first]:
        copy.start()
    small, narrow, wide, after = (
        copies[:8],
        copies[8 : 8 + 2 * blocks],
        copies[8 + 2 * blocks : first - 1],
        copies[first - 1],
    )

    for slot in range(2 * blocks):
        points_ref[slot * SLOT + slot_rows : (slot + 1) * SLOT, :] = jnp.zeros(
            (SLOT - slot_rows, width), BF16
        )
    lane = iota((1, LANES), 1)
    low = lane < SLOT
    place = lane % SLOT
    component = jnp.where(place < slot_rows, place % 3, 3)
    member, block_member = [], []
    for part in range(block_heads):
        member.append((place >= part * per_head) & (place < (part + 1) * per_head))
        block_member.append((lane >= part * head_dim) & (lane < (part + 1) * head_dim))
    both_member = [
        jnp.concatenate([left, right, right], axis=1).astype(F32).astype(BF16)
        for left, right in zip(block_member, member, strict=True)
    ]
    gamma_lanes = []
    for block in range(blocks):
        gamma = jnp.zeros((1, LANES), F32)
        for part in range(block_heads):
            gamma = jnp.where(member[part], gamma_ref[block * block_heads + part], gamma)
        gamma_lanes.append(gamma * point_scale)
    diagonal = iota((LANES, stacked_rows), 0) // head_dim == (
        iota((LANES, stacked_rows), 1) // residues
    )
    same = iota((residues, stacked_rows), 0) == iota((residues, stacked_rows), 1) % residues
    columns_ref[...] = jnp.zeros_like(columns_ref)

    for copy in small:
        copy.wait()
    kinds = table_ref.shape[0]
    onehot = (iota((kinds, residues), 0) == types_ref[...]).astype(F32).T.astype(BF16)
    conditional = matmul(onehot, table_ref[...])
    empty = as_row(null_ref).astype(F32)

    tiles = []
    for frame in range(frames):
        state = x_ref[frame].astype(F32)
        initial = jnp.concatenate([state + conditional, state + empty], axis=0)
        normed = layer_norm(initial, as_row(gain_ref)).astype(BF16)

        columns_ref[0:9, :] = rotation_ref[:, frame, :]
        moved = translation_ref[:, frame, :]
        columns_ref[9:12, :] = moved - jnp.mean(moved, axis=1, keepdims=True)
        columns_ref[12:13, :] = mask_ref[...].astype(F32)
        columns = columns_ref[...].T
        allowed = (columns[:, 12:13] == 1.0) | same
        factors = []
        for step in range(-2, 3):
            factor = jnp.zeros((residues, LANES), F32)
            for row in range(3):
                if 0 <= row + step < 3:
                    entry = 3 * row + row + step
                    factor = jnp.where(component == row, columns[:, entry : entry + 1], factor)
            factors.append(jnp.concatenate([factor] * BRANCHES, axis=0))
        anchor = jnp.zeros((residues, LANES), F32)
        for row in range(3):
            anchor = jnp.where(component == row, columns[:, 9 + row : 10 + row], anchor)
        anchor = jnp.concatenate([anchor] * BRANCHES, axis=0)

        if frame == 0:
            for copy in narrow:
                copy.wait()
        points = lax.dot_general(normed, points_ref[...], NT, preferred_element_type=F32)

        slots = []
        for pair in range(blocks):
            lanes = points[:, pair * LANES : (pair + 1) * LANES]
            placed = anchor + factors[2] * lanes
            for step in (-2, -1, 1, 2):
                placed = placed + factors[step + 2] * pltpu.roll(lanes, (-step) % LANES, 1)
            swapped = pltpu.roll(placed, SLOT, 1)
            slots += [jnp.where(low, placed, swapped), jnp.where(low, swapped, placed)]

        query_feature, key_first, key_second = [], [], []
        nothing = jnp.zeros((BRANCHES * residues, LANES), BF16)
        ones = jnp.ones((residues, LANES), BF16)
        for block in range(blocks):
            feature = slots[block] * (2.0 * gamma_lanes[block])
            high = feature.astype(BF16)
            rest = (feature - high.astype(F32)).astype(BF16)
            query_feature.append(jnp.where(low, high, rest))

            feature = slots[blocks + block]
            high = feature.astype(BF16)
            rest = (feature - high.astype(F32)).astype(BF16)
            key_first.append([high])
            key_second.append([jnp.where(low, rest, nothing)])
            square = feature * feature * (-gamma_lanes[block])
            high = square.astype(BF16)
            rest = square - high.astype(F32)
            middle = rest.astype(BF16)
            last = (rest - middle.astype(F32)).astype(BF16)
            key_first[block].append(jnp.where(low, high, middle))
            key_second[block].append(jnp.where(low, last, nothing))

        if frame == 0:
            for copy in wide:
                copy.wait()
            for copy in copies[first:]:
                copy.start()
        projected = matmul(normed, proj_ref[...])
        queries = (
            projected[:, :width].astype(BF16) * jnp.asarray(WEIGHT_LOGIT / math.sqrt(head_dim), BF16)
        )
        keys = projected[:, width : 2 * width].astype(BF16)
        values = projected[:, 2 * width :].astype(BF16)
        contexts = []
        for branch in range(BRANCHES):
            rows = slice(branch * residues, (branch + 1) * residues)
            turned = values[rows].T
            pieces = []
            for block in range(blocks):
                lanes = slice(block * LANES, (block + 1) * LANES)
                left = jnp.concatenate(
                    [
                        jnp.concatenate(
                            [piece[rows] for piece in (keys[:, lanes], *key_first[block])], axis=1
                        ),
                        jnp.concatenate(
                            [piece[rows] for piece in (nothing, *key_second[block])], axis=1
                        ),
                    ],
                    axis=0,
                )
                right = jnp.concatenate(
                    [queries[rows, lanes], query_feature[block][rows], ones], axis=1
                )
                right = jnp.concatenate([right * own for own in both_member], axis=0)
                logits = lax.dot_general(left, right, NT, preferred_element_type=F32)
                powers, scale = softmax_down(logits[:residues] + logits[residues:], allowed)
                mixed = jnp.where(diagonal, matmul(turned[lanes], powers) * scale, 0.0)
                folded = mixed[:, :fold]
                for start in range(fold, stacked_rows, fold):
                    folded = folded + mixed[:, start : start + fold]
                pieces.append(folded)
            contexts.append(jnp.concatenate(pieces, axis=0).astype(BF16).T)
        if frame == 0:
            after.wait()
        update = matmul(jnp.concatenate(contexts, axis=0), spatial_out_ref[...])
        totals = []
        for branch in range(BRANCHES):
            total = initial[branch * residues : (branch + 1) * residues]
            for start in range(0, fold, residues):
                begin = branch * fold + start
                total = total + update[begin : begin + residues]
            totals.append(total)
        tiles.append(
            [
                jnp.concatenate(
                    [total[group * share : (group + 1) * share] for total in totals], axis=0
                )
                for group in range(groups)
            ]
        )
    for group in range(groups):
        out_ref[group] = jnp.concatenate([tile[group] for tile in tiles], axis=0).astype(BF16)
    for copy in copies[first:]:
        copy.wait()


def temporal_kernel(
    period,
    x_ref,
    gain_ref,
    proj_ref,
    temporal_out_ref,
    hidden_gain_ref,
    hidden_in_ref,
    hidden_out_ref,
    head_gain_ref,
    head_out_ref,
    out_ref,
):
    groups, depth, width = x_ref.shape
    rows = groups * depth
    head_dim = width // THEADS
    block_heads = LANES // head_dim
    share = period // BRANCHES

    initial = x_ref[...].astype(F32).reshape(rows, width)
    normed = layer_norm(initial, as_row(gain_ref)).astype(BF16)
    projected = matmul(normed, proj_ref[...])
    queries = projected[:, :width].astype(BF16) * jnp.asarray(1.0 / math.sqrt(head_dim), BF16)
    keys = projected[:, width : 2 * width].astype(BF16)
    turned = projected[:, 2 * width :].astype(BF16).T
    block_lane = iota((1, LANES), 1)
    allowed = (
        iota((rows, block_heads * rows), 0) % period == iota((rows, block_heads * rows), 1) % period
    )
    pieces = []
    for block in range(width // LANES):
        lanes = slice(block * LANES, (block + 1) * LANES)
        stacked = []
        for part in range(block_heads):
            own = (block_lane >= part * head_dim) & (block_lane < (part + 1) * head_dim)
            stacked.append(queries[:, lanes] * own.astype(F32).astype(BF16))
        logits = lax.dot_general(
            keys[:, lanes], jnp.concatenate(stacked, axis=0), NT, preferred_element_type=F32
        )
        powers, scale = softmax_down(logits, allowed)
        mixed = matmul(turned[lanes], powers) * scale
        for part in range(block_heads):
            pieces.append(
                mixed[part * head_dim : (part + 1) * head_dim, part * rows : (part + 1) * rows]
            )
    context = jnp.concatenate(pieces, axis=0).astype(BF16).T
    after_time = initial + matmul(context, temporal_out_ref[...])
    second = layer_norm(after_time, as_row(hidden_gain_ref)).astype(BF16)
    hidden = jax.nn.gelu(matmul(second, hidden_in_ref[...])).astype(BF16)
    result = (after_time + matmul(hidden, hidden_out_ref[...])).astype(BF16).astype(F32)
    headed = layer_norm(result, as_row(head_gain_ref)).astype(BF16)
    branch_velocity = matmul(headed, head_out_ref[...]).reshape(rows // period, period, width)
    conditional = branch_velocity[:, :share]
    empty = branch_velocity[:, share:]
    out_ref[...] = (empty + GUIDE * (conditional - empty)).astype(BF16)


def whole(memory_space=pltpu.VMEM):
    return pl.BlockSpec(memory_space=memory_space)


def body(
    groups,
    x_state,
    noise_field,
    rotations,
    translations,
    residue_types,
    pocket_mask,
    type_table,
    null_embed,
    spatial_gain,
    spatial_proj,
    spatial_points,
    spatial_gamma,
    spatial_out,
    temporal_gain,
    temporal_proj,
    temporal_out,
    hidden_gain,
    hidden_in,
    hidden_out,
    head_gain,
    head_out,
):
    frames, residues, width = x_state.shape
    share = residues // groups
    period = BRANCHES * share
    sources = (
        x_state,
        type_table,
        residue_types[None],
        null_embed,
        spatial_gain,
        rotations,
        translations,
        pocket_mask[None],
        spatial_proj,
        spatial_out,
        spatial_points.T,
    )
    slots = 2 * (width // LANES)
    later = (temporal_proj, temporal_out, hidden_in, hidden_out, head_out)
    spatial, *later = pl.pallas_call(
        functools.partial(spatial_kernel, groups),
        out_shape=[pltpu.VMEM((groups, frames * period, width), BF16)]
        + [pltpu.VMEM(array.shape, array.dtype) for array in later],
        in_specs=[whole(pltpu.SMEM)] + [whole(pl.ANY)] * (len(sources) + len(later)),
        out_specs=[whole()] * (1 + len(later)),
        scratch_shapes=[pltpu.VMEM(array.shape, array.dtype) for array in sources[:-1]]
        + [
            pltpu.VMEM((slots * SLOT, width), BF16),
            pltpu.VMEM((16, residues), F32),
            pltpu.SemaphoreType.DMA((len(sources) - 2 + slots + CHUNKS + len(later),)),
        ],
        compiler_params=pltpu.CompilerParams(vmem_limit_bytes=SPATIAL_VMEM),
        name="spatial",
    )(spatial_gamma, *sources, *later)
    arrived = lax.all_to_all(spatial, "seq", split_axis=0, concat_axis=0, tiled=True)
    proj_local, out_local, in_local, hidden_local, head_local = later
    guided = pl.pallas_call(
        functools.partial(temporal_kernel, period),
        out_shape=pltpu.VMEM((groups * frames, share, width), BF16),
        in_specs=[whole()] * 9,
        out_specs=whole(),
        compiler_params=pltpu.CompilerParams(vmem_limit_bytes=TEMPORAL_VMEM),
        name="temporal",
    )(
        arrived,
        temporal_gain,
        proj_local,
        out_local,
        hidden_gain,
        in_local,
        hidden_local,
        head_gain,
        head_local,
    )
    velocity = lax.all_to_all(guided, "seq", split_axis=0, concat_axis=1, tiled=True)
    x_next = (
        x_state.astype(F32)
        + STEP_SIZE * velocity.astype(F32)
        + NOISE_SCALE * noise_field.astype(F32)
    ).astype(BF16)
    return (x_next, velocity)


def solution(mesh):
    tokens = P(("parts", "seq"), None, None)
    geometry = P(None, ("parts", "seq"), None)
    return jax.shard_map(
        functools.partial(body, mesh.shape["seq"]),
        mesh=mesh,
        in_specs=(tokens, tokens, geometry, geometry, P("parts"), P("parts")) + (P(),) * 15,
        out_specs=(tokens, tokens),
        check_vma=False,
    )
```

```python
import functools
import math

import jax
import jax.numpy as jnp
from jax import lax
from jax.experimental import pallas as pl
from jax.experimental.pallas import tpu as pltpu
from jax.sharding import PartitionSpec as P

THEADS = 6
BRANCHES = 2

WEIGHT_LOGIT = 0.7071067811865476
WEIGHT_POINT = 0.23570226039551584
GUIDE = 2.0
STEP_SIZE = 0.25
NOISE_SCALE = 0.2
EPSILON = 1e-05

BF16 = jnp.bfloat16
F32 = jnp.float32
LANES = 128
SLOT = 64
SPATIAL_VMEM = 56 * 2**20
TEMPORAL_VMEM = 40 * 2**20
NT = (((1,), (1,)), ((), ()))


def layer_norm(values, scale_gain):
    average = jnp.mean(values, axis=-1, keepdims=True)
    centered = values - average
    spread = jnp.mean(centered * centered, axis=-1, keepdims=True)
    return centered * lax.rsqrt(spread + EPSILON) * scale_gain


def as_row(ref):
    return ref[...].reshape(1, ref.shape[0])


def matmul(left, right):
    return jnp.dot(left, right, preferred_element_type=F32)


def iota(shape, axis):
    return lax.broadcasted_iota(jnp.int32, shape, axis)


def softmax_down(logits, allowed):
    logits = jnp.where(allowed, logits, -jnp.inf)
    powers = jnp.exp(logits - jnp.max(logits, axis=0, keepdims=True))
    return powers.astype(BF16), 1.0 / jnp.sum(powers, axis=0, keepdims=True)


def spatial_kernel(groups, gamma_ref, *refs):
    sources, refs = refs[:11], refs[11:]
    later, refs = refs[:5], refs[5:]
    out_ref, later_out, refs = refs[0], refs[1:6], refs[6:]
    local, (columns_ref, sems) = refs[:11], refs[11:]
    (
        x_ref,
        table_ref,
        types_ref,
        null_ref,
        gain_ref,
        rotation_ref,
        translation_ref,
        mask_ref,
        proj_ref,
        spatial_out_ref,
        points_ref,
    ) = local
    frames, residues, width = x_ref.shape
    heads = gamma_ref.shape[0]
    head_dim = width // heads
    blocks = width // LANES
    block_heads = LANES // head_dim
    slot_rows = sources[-1].shape[0] // (2 * blocks)
    per_head = slot_rows // block_heads
    share = residues // groups
    fold = max(residues, LANES)
    stacked_rows = block_heads * residues
    point_scale = 0.5 * WEIGHT_LOGIT * WEIGHT_POINT

    pairs = list(zip(sources[:10], local[:10], strict=True))
    for slot in range(2 * blocks):
        pairs.append(
            (
                sources[-1].at[pl.ds(slot * slot_rows, slot_rows), :],
                points_ref.at[pl.ds(slot * SLOT, slot_rows), :],
            )
        )
    pairs += list(zip(later, later_out, strict=True))
    copies = [
        pltpu.make_async_copy(source, target, sems.at[index])
        for index, (source, target) in enumerate(pairs)
    ]
    first = 10 + 2 * blocks
    for copy in copies[:first]:
        copy.start()
    small, wide = copies[:8], copies[8:first]

    for slot in range(2 * blocks):
        points_ref[slot * SLOT + slot_rows : (slot + 1) * SLOT, :] = jnp.zeros(
            (SLOT - slot_rows, width), BF16
        )
    lane = iota((1, LANES), 1)
    low = lane < SLOT
    place = lane % SLOT
    component = jnp.where(place < slot_rows, place % 3, 3)
    member, block_member = [], []
    for part in range(block_heads):
        member.append((place >= part * per_head) & (place < (part + 1) * per_head))
        block_member.append((lane >= part * head_dim) & (lane < (part + 1) * head_dim))
    both_member = [
        jnp.concatenate([left, right, right], axis=1).astype(F32).astype(BF16)
        for left, right in zip(block_member, member, strict=True)
    ]
    gamma_lanes = []
    for block in range(blocks):
        gamma = jnp.zeros((1, LANES), F32)
        for part in range(block_heads):
            gamma = jnp.where(member[part], gamma_ref[block * block_heads + part], gamma)
        gamma_lanes.append(gamma * point_scale)
    diagonal = iota((LANES, stacked_rows), 0) // head_dim == (
        iota((LANES, stacked_rows), 1) // residues
    )
    same = iota((residues, stacked_rows), 0) == iota((residues, stacked_rows), 1) % residues
    columns_ref[...] = jnp.zeros_like(columns_ref)

    for copy in small:
        copy.wait()
    kinds = table_ref.shape[0]
    onehot = (iota((kinds, residues), 0) == types_ref[...]).astype(F32).T.astype(BF16)
    conditional = matmul(onehot, table_ref[...])
    empty = as_row(null_ref).astype(F32)

    tiles = []
    for frame in range(frames):
        state = x_ref[frame].astype(F32)
        initial = jnp.concatenate([state + conditional, state + empty], axis=0)
        normed = layer_norm(initial, as_row(gain_ref)).astype(BF16)

        columns_ref[0:9, :] = rotation_ref[:, frame, :]
        moved = translation_ref[:, frame, :]
        columns_ref[9:12, :] = moved - jnp.mean(moved, axis=1, keepdims=True)
        columns_ref[12:13, :] = mask_ref[...].astype(F32)
        columns = columns_ref[...].T
        allowed = (columns[:, 12:13] == 1.0) | same
        factors = []
        for step in range(-2, 3):
            factor = jnp.zeros((residues, LANES), F32)
            for row in range(3):
                if 0 <= row + step < 3:
                    entry = 3 * row + row + step
                    factor = jnp.where(component == row, columns[:, entry : entry + 1], factor)
            factors.append(jnp.concatenate([factor] * BRANCHES, axis=0))
        anchor = jnp.zeros((residues, LANES), F32)
        for row in range(3):
            anchor = jnp.where(component == row, columns[:, 9 + row : 10 + row], anchor)
        anchor = jnp.concatenate([anchor] * BRANCHES, axis=0)

        if frame == 0:
            for copy in wide:
                copy.wait()
            for copy in copies[first:]:
                copy.start()
        points = lax.dot_general(normed, points_ref[...], NT, preferred_element_type=F32)
        projected = matmul(normed, proj_ref[...])

        slots = []
        for pair in range(blocks):
            lanes = points[:, pair * LANES : (pair + 1) * LANES]
            placed = anchor + factors[2] * lanes
            for step in (-2, -1, 1, 2):
                placed = placed + factors[step + 2] * pltpu.roll(lanes, (-step) % LANES, 1)
            swapped = pltpu.roll(placed, SLOT, 1)
            slots += [jnp.where(low, placed, swapped), jnp.where(low, swapped, placed)]

        query_feature, key_first, key_second = [], [], []
        nothing = jnp.zeros((BRANCHES * residues, LANES), BF16)
        ones = jnp.ones((residues, LANES), BF16)
        for block in range(blocks):
            feature = slots[block] * (2.0 * gamma_lanes[block])
            high = feature.astype(BF16)
            rest = (feature - high.astype(F32)).astype(BF16)
            query_feature.append(jnp.where(low, high, rest))

            feature = slots[blocks + block]
            high = feature.astype(BF16)
            rest = (feature - high.astype(F32)).astype(BF16)
            key_first.append([high])
            key_second.append([jnp.where(low, rest, nothing)])
            square = feature * feature * (-gamma_lanes[block])
            high = square.astype(BF16)
            rest = square - high.astype(F32)
            middle = rest.astype(BF16)
            last = (rest - middle.astype(F32)).astype(BF16)
            key_first[block].append(jnp.where(low, high, middle))
            key_second[block].append(jnp.where(low, last, nothing))

        queries = (
            projected[:, :width].astype(BF16) * jnp.asarray(WEIGHT_LOGIT / math.sqrt(head_dim), BF16)
        )
        keys = projected[:, width : 2 * width].astype(BF16)
        values = projected[:, 2 * width :].astype(BF16)
        turned, logits = [], []
        for branch in range(BRANCHES):
            rows = slice(branch * residues, (branch + 1) * residues)
            turned.append(values[rows].T)
            for block in range(blocks):
                lanes = slice(block * LANES, (block + 1) * LANES)
                left = jnp.concatenate(
                    [
                        jnp.concatenate(
                            [piece[rows] for piece in (keys[:, lanes], *key_first[block])], axis=1
                        ),
                        jnp.concatenate(
                            [piece[rows] for piece in (nothing, *key_second[block])], axis=1
                        ),
                    ],
                    axis=0,
                )
                right = jnp.concatenate(
                    [queries[rows, lanes], query_feature[block][rows], ones], axis=1
                )
                right = jnp.concatenate([right * own for own in both_member], axis=0)
                both = lax.dot_general(left, right, NT, preferred_element_type=F32)
                logits.append(both[:residues] + both[residues:])
        attends = [softmax_down(each, allowed) for each in logits]
        mixes = [
            matmul(turned[index // blocks][index % blocks * LANES :][:LANES], powers)
            for index, (powers, _) in enumerate(attends)
        ]
        contexts = []
        for branch in range(BRANCHES):
            pieces = []
            for block in range(blocks):
                index = branch * blocks + block
                mixed = jnp.where(diagonal, mixes[index] * attends[index][1], 0.0)
                folded = mixed[:, :fold]
                for start in range(fold, stacked_rows, fold):
                    folded = folded + mixed[:, start : start + fold]
                pieces.append(folded)
            contexts.append(jnp.concatenate(pieces, axis=0).astype(BF16).T)
        update = matmul(jnp.concatenate(contexts, axis=0), spatial_out_ref[...])
        totals = []
        for branch in range(BRANCHES):
            total = initial[branch * residues : (branch + 1) * residues]
            for start in range(0, fold, residues):
                begin = branch * fold + start
                total = total + update[begin : begin + residues]
            totals.append(total)
        tiles.append(
            [
                jnp.concatenate(
                    [total[group * share : (group + 1) * share] for total in totals], axis=0
                )
                for group in range(groups)
            ]
        )
    for group in range(groups):
        out_ref[group] = jnp.concatenate([tile[group] for tile in tiles], axis=0).astype(BF16)
    for copy in copies[first:]:
        copy.wait()


def temporal_kernel(
    period,
    x_ref,
    gain_ref,
    proj_ref,
    temporal_out_ref,
    hidden_gain_ref,
    hidden_in_ref,
    hidden_out_ref,
    head_gain_ref,
    head_out_ref,
    out_ref,
):
    groups, depth, width = x_ref.shape
    rows = groups * depth
    head_dim = width // THEADS
    block_heads = LANES // head_dim
    share = period // BRANCHES

    initial = x_ref[...].astype(F32).reshape(rows, width)
    normed = layer_norm(initial, as_row(gain_ref)).astype(BF16)
    projected = matmul(normed, proj_ref[...])
    queries = projected[:, :width].astype(BF16) * jnp.asarray(1.0 / math.sqrt(head_dim), BF16)
    keys = projected[:, width : 2 * width].astype(BF16)
    turned = projected[:, 2 * width :].astype(BF16).T
    block_lane = iota((1, LANES), 1)
    allowed = (
        iota((rows, block_heads * rows), 0) % period == iota((rows, block_heads * rows), 1) % period
    )
    logits = []
    for block in range(width // LANES):
        lanes = slice(block * LANES, (block + 1) * LANES)
        stacked = []
        for part in range(block_heads):
            own = (block_lane >= part * head_dim) & (block_lane < (part + 1) * head_dim)
            stacked.append(queries[:, lanes] * own.astype(F32).astype(BF16))
        logits.append(
            lax.dot_general(
                keys[:, lanes], jnp.concatenate(stacked, axis=0), NT, preferred_element_type=F32
            )
        )
    attends = [softmax_down(each, allowed) for each in logits]
    mixes = [
        matmul(turned[block * LANES : (block + 1) * LANES], powers)
        for block, (powers, _) in enumerate(attends)
    ]
    pieces = []
    for mixed, (_, scale) in zip(mixes, attends, strict=True):
        for part in range(block_heads):
            lanes = slice(part * rows, (part + 1) * rows)
            pieces.append(mixed[part * head_dim : (part + 1) * head_dim, lanes] * scale[:, lanes])
    context = jnp.concatenate(pieces, axis=0).astype(BF16).T
    after_time = initial + matmul(context, temporal_out_ref[...])
    second = layer_norm(after_time, as_row(hidden_gain_ref)).astype(BF16)
    hidden = jax.nn.gelu(matmul(second, hidden_in_ref[...])).astype(BF16)
    result = (after_time + matmul(hidden, hidden_out_ref[...])).astype(BF16).astype(F32)
    headed = layer_norm(result, as_row(head_gain_ref)).astype(BF16)
    branch_velocity = matmul(headed, head_out_ref[...]).reshape(rows // period, period, width)
    conditional = branch_velocity[:, :share]
    empty = branch_velocity[:, share:]
    out_ref[...] = (empty + GUIDE * (conditional - empty)).astype(BF16)


def whole(memory_space=pltpu.VMEM):
    return pl.BlockSpec(memory_space=memory_space)


def body(
    groups,
    x_state,
    noise_field,
    rotations,
    translations,
    residue_types,
    pocket_mask,
    type_table,
    null_embed,
    spatial_gain,
    spatial_proj,
    spatial_points,
    spatial_gamma,
    spatial_out,
    temporal_gain,
    temporal_proj,
    temporal_out,
    hidden_gain,
    hidden_in,
    hidden_out,
    head_gain,
    head_out,
):
    frames, residues, width = x_state.shape
    share = residues // groups
    period = BRANCHES * share
    sources = (
        x_state,
        type_table,
        residue_types[None],
        null_embed,
        spatial_gain,
        rotations,
        translations,
        pocket_mask[None],
        spatial_proj,
        spatial_out,
        spatial_points.T,
    )
    slots = 2 * (width // LANES)
    later = (temporal_proj, temporal_out, hidden_in, hidden_out, head_out)
    spatial, *later = pl.pallas_call(
        functools.partial(spatial_kernel, groups),
        out_shape=[pltpu.VMEM((groups, frames * period, width), BF16)]
        + [pltpu.VMEM(array.shape, array.dtype) for array in later],
        in_specs=[whole(pltpu.SMEM)] + [whole(pl.ANY)] * (len(sources) + len(later)),
        out_specs=[whole()] * (1 + len(later)),
        scratch_shapes=[pltpu.VMEM(array.shape, array.dtype) for array in sources[:-1]]
        + [
            pltpu.VMEM((slots * SLOT, width), BF16),
            pltpu.VMEM((16, residues), F32),
            pltpu.SemaphoreType.DMA((len(sources) - 1 + slots + len(later),)),
        ],
        compiler_params=pltpu.CompilerParams(vmem_limit_bytes=SPATIAL_VMEM),
        name="spatial",
    )(spatial_gamma, *sources, *later)
    arrived = lax.all_to_all(spatial, "seq", split_axis=0, concat_axis=0, tiled=True)
    proj_local, out_local, in_local, hidden_local, head_local = later
    guided = pl.pallas_call(
        functools.partial(temporal_kernel, period),
        out_shape=pltpu.VMEM((groups * frames, share, width), BF16),
        in_specs=[whole()] * 9,
        out_specs=whole(),
        compiler_params=pltpu.CompilerParams(vmem_limit_bytes=TEMPORAL_VMEM),
        name="temporal",
    )(
        arrived,
        temporal_gain,
        proj_local,
        out_local,
        hidden_gain,
        in_local,
        hidden_local,
        head_gain,
        head_local,
    )
    velocity = lax.all_to_all(guided, "seq", split_axis=0, concat_axis=1, tiled=True)
    x_next = (
        x_state.astype(F32)
        + STEP_SIZE * velocity.astype(F32)
        + NOISE_SCALE * noise_field.astype(F32)
    ).astype(BF16)
    return (x_next, velocity)


def solution(mesh):
    tokens = P(("parts", "seq"), None, None)
    geometry = P(None, ("parts", "seq"), None)
    return jax.shard_map(
        functools.partial(body, mesh.shape["seq"]),
        mesh=mesh,
        in_specs=(tokens, tokens, geometry, geometry, P("parts"), P("parts")) + (P(),) * 15,
        out_specs=(tokens, tokens),
        check_vma=False,
    )
```

```python
import functools
import math

import jax
import jax.numpy as jnp
from jax import lax
from jax.experimental import pallas as pl
from jax.experimental.pallas import tpu as pltpu
from jax.sharding import PartitionSpec as P

THEADS = 6
BRANCHES = 2

WEIGHT_LOGIT = 0.7071067811865476
WEIGHT_POINT = 0.23570226039551584
GUIDE = 2.0
STEP_SIZE = 0.25
NOISE_SCALE = 0.2
EPSILON = 1e-05

BF16 = jnp.bfloat16
F32 = jnp.float32
LANES = 128
SLOT = 64
FEED = 512
SPATIAL_VMEM = 56 * 2**20
TEMPORAL_VMEM = 40 * 2**20
NT = (((1,), (1,)), ((), ()))


def layer_norm(values, scale_gain):
    average = jnp.mean(values, axis=-1, keepdims=True)
    centered = values - average
    spread = jnp.mean(centered * centered, axis=-1, keepdims=True)
    return centered * lax.rsqrt(spread + EPSILON) * scale_gain


def as_row(ref):
    return ref[...].reshape(1, ref.shape[0])


def matmul(left, right):
    return jnp.dot(left, right, preferred_element_type=F32)


def iota(shape, axis):
    return lax.broadcasted_iota(jnp.int32, shape, axis)


def softmax_down(logits, allowed):
    logits = jnp.where(allowed, logits, -jnp.inf)
    powers = jnp.exp(logits - jnp.max(logits, axis=0, keepdims=True))
    return powers.astype(BF16), 1.0 / jnp.sum(powers, axis=0, keepdims=True)


def spatial_kernel(groups, gamma_ref, *refs):
    sources, refs = refs[:11], refs[11:]
    later, refs = refs[:5], refs[5:]
    out_ref, later_out, refs = refs[0], refs[1:6], refs[6:]
    local, (columns_ref, sems) = refs[:11], refs[11:]
    (
        x_ref,
        table_ref,
        types_ref,
        null_ref,
        gain_ref,
        rotation_ref,
        translation_ref,
        mask_ref,
        proj_ref,
        spatial_out_ref,
        points_ref,
    ) = local
    frames, residues, width = x_ref.shape
    heads = gamma_ref.shape[0]
    head_dim = width // heads
    blocks = width // LANES
    block_heads = LANES // head_dim
    slot_rows = sources[-1].shape[0] // (2 * blocks)
    per_head = slot_rows // block_heads
    share = residues // groups
    fold = max(residues, LANES)
    stacked_rows = block_heads * residues
    point_scale = 0.5 * WEIGHT_LOGIT * WEIGHT_POINT

    pairs = list(zip(sources[:10], local[:10], strict=True))
    for slot in range(2 * blocks):
        pairs.append(
            (
                sources[-1].at[pl.ds(slot * slot_rows, slot_rows), :],
                points_ref.at[pl.ds(slot * SLOT, slot_rows), :],
            )
        )
    pairs += list(zip(later, later_out, strict=True))
    copies = [
        pltpu.make_async_copy(source, target, sems.at[index])
        for index, (source, target) in enumerate(pairs)
    ]
    first = 10 + 2 * blocks
    for copy in copies[:first]:
        copy.start()
    small, wide = copies[:8], copies[8:first]

    for slot in range(2 * blocks):
        points_ref[slot * SLOT + slot_rows : (slot + 1) * SLOT, :] = jnp.zeros(
            (SLOT - slot_rows, width), BF16
        )
    lane = iota((1, LANES), 1)
    low = lane < SLOT
    place = lane % SLOT
    component = jnp.where(place < slot_rows, place % 3, 3)
    member, block_member = [], []
    for part in range(block_heads):
        member.append((place >= part * per_head) & (place < (part + 1) * per_head))
        block_member.append((lane >= part * head_dim) & (lane < (part + 1) * head_dim))
    both_member = [
        jnp.concatenate([left, right, right], axis=1).astype(F32).astype(BF16)
        for left, right in zip(block_member, member, strict=True)
    ]
    gamma_lanes = []
    for block in range(blocks):
        gamma = jnp.zeros((1, LANES), F32)
        for part in range(block_heads):
            gamma = jnp.where(member[part], gamma_ref[block * block_heads + part], gamma)
        gamma_lanes.append(gamma * point_scale)
    chunks = stacked_rows // fold
    chunk_rows = LANES // chunks
    diagonal = iota((chunk_rows, fold), 0) // head_dim == iota((chunk_rows, fold), 1) // residues
    same = iota((residues, stacked_rows), 0) == iota((residues, stacked_rows), 1) % residues
    columns_ref[...] = jnp.zeros_like(columns_ref)

    for copy in small:
        copy.wait()
    kinds = table_ref.shape[0]
    onehot = (iota((kinds, residues), 0) == types_ref[...]).astype(F32).T.astype(BF16)
    conditional = matmul(onehot, table_ref[...])
    empty = as_row(null_ref).astype(F32)

    tiles = []
    for frame in range(frames):
        state = x_ref[frame].astype(F32)
        initial = jnp.concatenate([state + conditional, state + empty], axis=0)
        normed = layer_norm(initial, as_row(gain_ref)).astype(BF16)

        columns_ref[0:9, :] = rotation_ref[:, frame, :]
        moved = translation_ref[:, frame, :]
        columns_ref[9:12, :] = moved - jnp.mean(moved, axis=1, keepdims=True)
        columns_ref[12:13, :] = mask_ref[...].astype(F32)
        columns = columns_ref[...].T
        allowed = (columns[:, 12:13] == 1.0) | same
        factors = []
        for step in range(-2, 3):
            factor = jnp.zeros((residues, LANES), F32)
            for row in range(3):
                if 0 <= row + step < 3:
                    entry = 3 * row + row + step
                    factor = jnp.where(component == row, columns[:, entry : entry + 1], factor)
            factors.append(jnp.concatenate([factor] * BRANCHES, axis=0))
        anchor = jnp.zeros((residues, LANES), F32)
        for row in range(3):
            anchor = jnp.where(component == row, columns[:, 9 + row : 10 + row], anchor)
        anchor = jnp.concatenate([anchor] * BRANCHES, axis=0)

        if frame == 0:
            for copy in wide:
                copy.wait()
            for copy in copies[first:]:
                copy.start()
        points = lax.dot_general(normed, points_ref[...], NT, preferred_element_type=F32)
        projected = matmul(normed, proj_ref[...])

        slots = []
        for pair in range(blocks):
            lanes = points[:, pair * LANES : (pair + 1) * LANES]
            placed = anchor + factors[2] * lanes
            for step in (-2, -1, 1, 2):
                placed = placed + factors[step + 2] * pltpu.roll(lanes, (-step) % LANES, 1)
            swapped = pltpu.roll(placed, SLOT, 1)
            slots += [jnp.where(low, placed, swapped), jnp.where(low, swapped, placed)]

        query_feature, key_first, key_second = [], [], []
        nothing = jnp.zeros((BRANCHES * residues, LANES), BF16)
        ones = jnp.ones((residues, LANES), BF16)
        for block in range(blocks):
            feature = slots[block] * (2.0 * gamma_lanes[block])
            high = feature.astype(BF16)
            rest = (feature - high.astype(F32)).astype(BF16)
            query_feature.append(jnp.where(low, high, rest))

            feature = slots[blocks + block]
            high = feature.astype(BF16)
            rest = (feature - high.astype(F32)).astype(BF16)
            key_first.append([high])
            key_second.append([jnp.where(low, rest, nothing)])
            square = feature * feature * (-gamma_lanes[block])
            high = square.astype(BF16)
            rest = square - high.astype(F32)
            middle = rest.astype(BF16)
            last = (rest - middle.astype(F32)).astype(BF16)
            key_first[block].append(jnp.where(low, high, middle))
            key_second[block].append(jnp.where(low, last, nothing))

        queries = (
            projected[:, :width].astype(BF16) * jnp.asarray(WEIGHT_LOGIT / math.sqrt(head_dim), BF16)
        )
        keys = projected[:, width : 2 * width].astype(BF16)
        values = projected[:, 2 * width :].astype(BF16)
        turned, logits = [], []
        for branch in range(BRANCHES):
            rows = slice(branch * residues, (branch + 1) * residues)
            turned.append(values[rows].T)
            for block in range(blocks):
                lanes = slice(block * LANES, (block + 1) * LANES)
                left = jnp.concatenate(
                    [
                        jnp.concatenate(
                            [piece[rows] for piece in (keys[:, lanes], *key_first[block])], axis=1
                        ),
                        jnp.concatenate(
                            [piece[rows] for piece in (nothing, *key_second[block])], axis=1
                        ),
                    ],
                    axis=0,
                )
                right = jnp.concatenate(
                    [queries[rows, lanes], query_feature[block][rows], ones], axis=1
                )
                right = jnp.concatenate([right * own for own in both_member], axis=0)
                both = lax.dot_general(left, right, NT, preferred_element_type=F32)
                logits.append(both[:residues] + both[residues:])
        attends = [softmax_down(each, allowed) for each in logits]
        mixes = []
        for index, (powers, _) in enumerate(attends):
            block = index % blocks
            for chunk in range(chunks):
                start = block * LANES + chunk * chunk_rows
                mixes.append(
                    matmul(
                        turned[index // blocks][start : start + chunk_rows],
                        powers[:, chunk * fold : (chunk + 1) * fold],
                    )
                )
        contexts = []
        for branch in range(BRANCHES):
            pieces = []
            for index in range(branch * blocks, (branch + 1) * blocks):
                scale = attends[index][1]
                for chunk in range(chunks):
                    mixed = mixes[index * chunks + chunk]
                    mixed = mixed * scale[:, chunk * fold : (chunk + 1) * fold]
                    pieces.append(jnp.where(diagonal, mixed, 0.0))
            context = jnp.concatenate(pieces, axis=0).astype(BF16).T
            joined = context[:residues]
            for start in range(residues, fold, residues):
                joined = joined + context[start : start + residues]
            contexts.append(joined)
        update = matmul(jnp.concatenate(contexts, axis=0), spatial_out_ref[...])
        total = initial + update
        tiles.append(
            [
                jnp.concatenate(
                    [
                        total[start : start + share]
                        for start in range(group * share, BRANCHES * residues, residues)
                    ],
                    axis=0,
                )
                for group in range(groups)
            ]
        )
    for group in range(groups):
        out_ref[group] = jnp.concatenate([tile[group] for tile in tiles], axis=0).astype(BF16)
    for copy in copies[first:]:
        copy.wait()


def temporal_kernel(
    period,
    x_ref,
    gain_ref,
    proj_ref,
    temporal_out_ref,
    hidden_gain_ref,
    hidden_in_ref,
    hidden_out_ref,
    head_gain_ref,
    head_out_ref,
    out_ref,
):
    groups, depth, width = x_ref.shape
    rows = groups * depth
    head_dim = width // THEADS
    block_heads = LANES // head_dim
    share = period // BRANCHES

    initial = x_ref[...].astype(F32).reshape(rows, width)
    normed = layer_norm(initial, as_row(gain_ref)).astype(BF16)
    projected = matmul(normed, proj_ref[...])
    queries = projected[:, :width].astype(BF16) * jnp.asarray(1.0 / math.sqrt(head_dim), BF16)
    keys = projected[:, width : 2 * width].astype(BF16)
    turned = projected[:, 2 * width :].astype(BF16).T
    block_lane = iota((1, LANES), 1)
    allowed = (
        iota((rows, block_heads * rows), 0) % period == iota((rows, block_heads * rows), 1) % period
    )
    logits = []
    for block in range(width // LANES):
        lanes = slice(block * LANES, (block + 1) * LANES)
        stacked = []
        for part in range(block_heads):
            own = (block_lane >= part * head_dim) & (block_lane < (part + 1) * head_dim)
            stacked.append(queries[:, lanes] * own.astype(F32).astype(BF16))
        logits.append(
            lax.dot_general(
                keys[:, lanes], jnp.concatenate(stacked, axis=0), NT, preferred_element_type=F32
            )
        )
    attends = [softmax_down(each, allowed) for each in logits]
    mixes = []
    for block, (powers, _) in enumerate(attends):
        for part in range(block_heads):
            start = block * LANES + part * head_dim
            lanes = slice(part * rows, (part + 1) * rows)
            mixes.append(matmul(turned[start : start + head_dim], powers[:, lanes]))
    pieces = []
    for index, mixed in enumerate(mixes):
        part = index % block_heads
        pieces.append(mixed * attends[index // block_heads][1][:, part * rows : (part + 1) * rows])
    context = jnp.concatenate(pieces, axis=0).astype(BF16).T
    after_time = initial + matmul(context, temporal_out_ref[...])
    second = layer_norm(after_time, as_row(hidden_gain_ref)).astype(BF16)
    feed = hidden_in_ref.shape[1]
    columns = [slice(start, start + FEED) for start in range(0, feed, FEED)]
    wide = [matmul(second, hidden_in_ref[:, columns[0]])]
    result = after_time
    for index, column in enumerate(columns):
        if index + 1 < len(columns):
            wide.append(matmul(second, hidden_in_ref[:, columns[index + 1]]))
        hidden = jax.nn.gelu(wide[index]).astype(BF16)
        result = result + matmul(hidden, hidden_out_ref[column, :])
    result = result.astype(BF16).astype(F32)
    headed = layer_norm(result, as_row(head_gain_ref)).astype(BF16)
    branch_velocity = matmul(headed, head_out_ref[...]).reshape(rows // period, period, width)
    conditional = branch_velocity[:, :share]
    empty = branch_velocity[:, share:]
    out_ref[...] = (empty + GUIDE * (conditional - empty)).astype(BF16)


def whole(memory_space=pltpu.VMEM):
    return pl.BlockSpec(memory_space=memory_space)


def body(
    groups,
    x_state,
    noise_field,
    rotations,
    translations,
    residue_types,
    pocket_mask,
    type_table,
    null_embed,
    spatial_gain,
    spatial_proj,
    spatial_points,
    spatial_gamma,
    spatial_out,
    temporal_gain,
    temporal_proj,
    temporal_out,
    hidden_gain,
    hidden_in,
    hidden_out,
    head_gain,
    head_out,
):
    frames, residues, width = x_state.shape
    share = residues // groups
    period = BRANCHES * share
    sources = (
        x_state,
        type_table,
        residue_types[None],
        null_embed,
        spatial_gain,
        rotations,
        translations,
        pocket_mask[None],
        spatial_proj,
        spatial_out,
        spatial_points.T,
    )
    slots = 2 * (width // LANES)
    later = (temporal_proj, temporal_out, hidden_in, hidden_out, head_out)
    spatial, *later = pl.pallas_call(
        functools.partial(spatial_kernel, groups),
        out_shape=[pltpu.VMEM((groups, frames * period, width), BF16)]
        + [pltpu.VMEM(array.shape, array.dtype) for array in later],
        in_specs=[whole(pltpu.SMEM)] + [whole(pl.ANY)] * (len(sources) + len(later)),
        out_specs=[whole()] * (1 + len(later)),
        scratch_shapes=[pltpu.VMEM(array.shape, array.dtype) for array in sources[:-1]]
        + [
            pltpu.VMEM((slots * SLOT, width), BF16),
            pltpu.VMEM((16, residues), F32),
            pltpu.SemaphoreType.DMA((len(sources) - 1 + slots + len(later),)),
        ],
        compiler_params=pltpu.CompilerParams(vmem_limit_bytes=SPATIAL_VMEM),
        name="spatial",
    )(spatial_gamma, *sources, *later)
    arrived = lax.all_to_all(spatial, "seq", split_axis=0, concat_axis=0, tiled=True)
    proj_local, out_local, in_local, hidden_local, head_local = later
    guided = pl.pallas_call(
        functools.partial(temporal_kernel, period),
        out_shape=pltpu.VMEM((groups * frames, share, width), BF16),
        in_specs=[whole()] * 9,
        out_specs=whole(),
        compiler_params=pltpu.CompilerParams(vmem_limit_bytes=TEMPORAL_VMEM),
        name="temporal",
    )(
        arrived,
        temporal_gain,
        proj_local,
        out_local,
        hidden_gain,
        in_local,
        hidden_local,
        head_gain,
        head_local,
    )
    velocity = lax.all_to_all(guided, "seq", split_axis=0, concat_axis=1, tiled=True)
    x_next = (
        x_state.astype(F32)
        + STEP_SIZE * velocity.astype(F32)
        + NOISE_SCALE * noise_field.astype(F32)
    ).astype(BF16)
    return (x_next, velocity)


def solution(mesh):
    tokens = P(("parts", "seq"), None, None)
    geometry = P(None, ("parts", "seq"), None)
    return jax.shard_map(
        functools.partial(body, mesh.shape["seq"]),
        mesh=mesh,
        in_specs=(tokens, tokens, geometry, geometry, P("parts"), P("parts")) + (P(),) * 15,
        out_specs=(tokens, tokens),
        check_vma=False,
    )
```

```python
import functools
import math

import jax
import jax.numpy as jnp
from jax import lax
from jax.experimental import pallas as pl
from jax.experimental.pallas import tpu as pltpu
from jax.sharding import PartitionSpec as P

THEADS = 6
BRANCHES = 2

WEIGHT_LOGIT = 0.7071067811865476
WEIGHT_POINT = 0.23570226039551584
GUIDE = 2.0
STEP_SIZE = 0.25
NOISE_SCALE = 0.2
EPSILON = 1e-05

BF16 = jnp.bfloat16
F32 = jnp.float32
LANES = 128
SLOT = 64
SPATIAL_VMEM = 56 * 2**20
TEMPORAL_VMEM = 40 * 2**20
NT = (((1,), (1,)), ((), ()))


def layer_norm(values, scale_gain):
    average = jnp.mean(values, axis=-1, keepdims=True)
    centered = values - average
    spread = jnp.mean(centered * centered, axis=-1, keepdims=True)
    return centered * lax.rsqrt(spread + EPSILON) * scale_gain


def as_row(ref):
    return ref[...].reshape(1, ref.shape[0])


def matmul(left, right):
    return jnp.dot(left, right, preferred_element_type=F32)


def iota(shape, axis):
    return lax.broadcasted_iota(jnp.int32, shape, axis)


def softmax_down(logits, allowed):
    logits = jnp.where(allowed, logits, -jnp.inf)
    powers = jnp.exp(logits - jnp.max(logits, axis=0, keepdims=True))
    return powers.astype(BF16), 1.0 / jnp.sum(powers, axis=0, keepdims=True)


def spatial_kernel(groups, gamma_ref, *refs):
    sources, refs = refs[:11], refs[11:]
    later, refs = refs[:5], refs[5:]
    out_ref, later_out, refs = refs[0], refs[1:6], refs[6:]
    local, (columns_ref, sems) = refs[:11], refs[11:]
    (
        x_ref,
        table_ref,
        types_ref,
        null_ref,
        gain_ref,
        rotation_ref,
        translation_ref,
        mask_ref,
        proj_ref,
        spatial_out_ref,
        points_ref,
    ) = local
    frames, residues, width = x_ref.shape
    heads = gamma_ref.shape[0]
    head_dim = width // heads
    blocks = width // LANES
    block_heads = LANES // head_dim
    slot_rows = sources[-1].shape[0] // (2 * blocks)
    per_head = slot_rows // block_heads
    share = residues // groups
    fold = max(residues, LANES)
    stacked_rows = block_heads * residues
    point_scale = 0.5 * WEIGHT_LOGIT * WEIGHT_POINT

    pairs = list(zip(sources[:10], local[:10], strict=True))
    for slot in range(2 * blocks):
        pairs.append(
            (
                sources[-1].at[pl.ds(slot * slot_rows, slot_rows), :],
                points_ref.at[pl.ds(slot * SLOT, slot_rows), :],
            )
        )
    pairs += list(zip(later, later_out, strict=True))
    copies = [
        pltpu.make_async_copy(source, target, sems.at[index])
        for index, (source, target) in enumerate(pairs)
    ]
    first = 10 + 2 * blocks
    for copy in copies[:first]:
        copy.start()
    small, wide = copies[:8], copies[8:first]

    for slot in range(2 * blocks):
        points_ref[slot * SLOT + slot_rows : (slot + 1) * SLOT, :] = jnp.zeros(
            (SLOT - slot_rows, width), BF16
        )
    lane = iota((1, LANES), 1)
    low = lane < SLOT
    place = lane % SLOT
    component = jnp.where(place < slot_rows, place % 3, 3)
    member, block_member = [], []
    for part in range(block_heads):
        member.append((place >= part * per_head) & (place < (part + 1) * per_head))
        block_member.append((lane >= part * head_dim) & (lane < (part + 1) * head_dim))
    head_lanes = [own.astype(F32).astype(BF16) for own in block_member]
    point_lanes = [
        jnp.concatenate([own, own], axis=1).astype(F32).astype(BF16) for own in member
    ]
    gamma_lanes = []
    for block in range(blocks):
        gamma = jnp.zeros((1, LANES), F32)
        for part in range(block_heads):
            gamma = jnp.where(member[part], gamma_ref[block * block_heads + part], gamma)
        gamma_lanes.append(gamma * point_scale)
    chunks = stacked_rows // fold
    chunk_rows = LANES // chunks
    diagonal = iota((chunk_rows, fold), 0) // head_dim == iota((chunk_rows, fold), 1) // residues
    same = iota((residues, stacked_rows), 0) == iota((residues, stacked_rows), 1) % residues
    columns_ref[...] = jnp.zeros_like(columns_ref)

    for copy in small:
        copy.wait()
    kinds = table_ref.shape[0]
    onehot = (iota((kinds, residues), 0) == types_ref[...]).astype(F32).T.astype(BF16)
    conditional = matmul(onehot, table_ref[...])
    empty = as_row(null_ref).astype(F32)

    tiles = []
    for frame in range(frames):
        state = x_ref[frame].astype(F32)
        initial = jnp.concatenate([state + conditional, state + empty], axis=0)
        normed = layer_norm(initial, as_row(gain_ref)).astype(BF16)

        columns_ref[0:9, :] = rotation_ref[:, frame, :]
        moved = translation_ref[:, frame, :]
        columns_ref[9:12, :] = moved - jnp.mean(moved, axis=1, keepdims=True)
        columns_ref[12:13, :] = mask_ref[...].astype(F32)
        columns = columns_ref[...].T
        allowed = (columns[:, 12:13] == 1.0) | same
        factors = []
        for step in range(-2, 3):
            factor = jnp.zeros((residues, LANES), F32)
            for row in range(3):
                if 0 <= row + step < 3:
                    entry = 3 * row + row + step
                    factor = jnp.where(component == row, columns[:, entry : entry + 1], factor)
            factors.append(jnp.concatenate([factor] * BRANCHES, axis=0))
        anchor = jnp.zeros((residues, LANES), F32)
        for row in range(3):
            anchor = jnp.where(component == row, columns[:, 9 + row : 10 + row], anchor)
        anchor = jnp.concatenate([anchor] * BRANCHES, axis=0)

        if frame == 0:
            for copy in wide:
                copy.wait()
            for copy in copies[first:]:
                copy.start()
        points = lax.dot_general(normed, points_ref[...], NT, preferred_element_type=F32)
        projected = matmul(normed, proj_ref[...])

        queries = (
            projected[:, :width].astype(BF16) * jnp.asarray(WEIGHT_LOGIT / math.sqrt(head_dim), BF16)
        )
        keys = projected[:, width : 2 * width].astype(BF16)
        values = projected[:, 2 * width :].astype(BF16)
        turned, scalar = [], []
        for branch in range(BRANCHES):
            rows = slice(branch * residues, (branch + 1) * residues)
            turned.append(values[rows].T)
            for start in range(0, width, LANES):
                lanes = slice(start, start + LANES)
                right = jnp.concatenate([queries[rows, lanes] * own for own in head_lanes], axis=0)
                scalar.append(
                    lax.dot_general(keys[rows, lanes], right, NT, preferred_element_type=F32)
                )

        slots = []
        for pair in range(blocks):
            lanes = points[:, pair * LANES : (pair + 1) * LANES]
            placed = anchor + factors[2] * lanes
            for step in (-2, -1, 1, 2):
                placed = placed + factors[step + 2] * pltpu.roll(lanes, (-step) % LANES, 1)
            swapped = pltpu.roll(placed, SLOT, 1)
            slots += [jnp.where(low, placed, swapped), jnp.where(low, swapped, placed)]

        query_feature, key_first, key_second = [], [], []
        nothing = jnp.zeros((BRANCHES * residues, LANES), BF16)
        ones = jnp.ones((residues, LANES), BF16)
        for block in range(blocks):
            feature = slots[block] * (2.0 * gamma_lanes[block])
            high = feature.astype(BF16)
            rest = (feature - high.astype(F32)).astype(BF16)
            query_feature.append(jnp.where(low, high, rest))

            feature = slots[blocks + block]
            high = feature.astype(BF16)
            rest = (feature - high.astype(F32)).astype(BF16)
            key_first.append([high])
            key_second.append([jnp.where(low, rest, nothing)])
            square = feature * feature * (-gamma_lanes[block])
            high = square.astype(BF16)
            rest = square - high.astype(F32)
            middle = rest.astype(BF16)
            last = (rest - middle.astype(F32)).astype(BF16)
            key_first[block].append(jnp.where(low, high, middle))
            key_second[block].append(jnp.where(low, last, nothing))

        logits = []
        for branch in range(BRANCHES):
            rows = slice(branch * residues, (branch + 1) * residues)
            for block in range(blocks):
                left = jnp.concatenate(
                    [
                        jnp.concatenate([piece[rows] for piece in pieces[block]], axis=1)
                        for pieces in (key_first, key_second)
                    ],
                    axis=0,
                )
                right = jnp.concatenate([query_feature[block][rows], ones], axis=1)
                right = jnp.concatenate([right * own for own in point_lanes], axis=0)
                both = lax.dot_general(left, right, NT, preferred_element_type=F32)
                logits.append(scalar[len(logits)] + both[:residues] + both[residues:])
        attends = [softmax_down(each, allowed) for each in logits]
        mixes = []
        for index, (powers, _) in enumerate(attends):
            block = index % blocks
            for chunk in range(chunks):
                start = block * LANES + chunk * chunk_rows
                mixes.append(
                    matmul(
                        turned[index // blocks][start : start + chunk_rows],
                        powers[:, chunk * fold : (chunk + 1) * fold],
                    )
                )
        contexts = []
        for branch in range(BRANCHES):
            pieces = []
            for index in range(branch * blocks, (branch + 1) * blocks):
                scale = attends[index][1]
                for chunk in range(chunks):
                    mixed = mixes[index * chunks + chunk]
                    mixed = mixed * scale[:, chunk * fold : (chunk + 1) * fold]
                    pieces.append(jnp.where(diagonal, mixed, 0.0))
            context = jnp.concatenate(pieces, axis=0).astype(BF16).T
            joined = context[:residues]
            for start in range(residues, fold, residues):
                joined = joined + context[start : start + residues]
            contexts.append(joined)
        update = matmul(jnp.concatenate(contexts, axis=0), spatial_out_ref[...])
        total = initial + update
        tiles.append(
            [
                jnp.concatenate(
                    [
                        total[start : start + share]
                        for start in range(group * share, BRANCHES * residues, residues)
                    ],
                    axis=0,
                )
                for group in range(groups)
            ]
        )
    for group in range(groups):
        out_ref[group] = jnp.concatenate([tile[group] for tile in tiles], axis=0).astype(BF16)
    for copy in copies[first:]:
        copy.wait()


def temporal_kernel(
    period,
    x_ref,
    gain_ref,
    proj_ref,
    temporal_out_ref,
    hidden_gain_ref,
    hidden_in_ref,
    hidden_out_ref,
    head_gain_ref,
    head_out_ref,
    out_ref,
):
    groups, depth, width = x_ref.shape
    rows = groups * depth
    head_dim = width // THEADS
    block_heads = LANES // head_dim
    share = period // BRANCHES

    initial = x_ref[...].astype(F32).reshape(rows, width)
    normed = layer_norm(initial, as_row(gain_ref)).astype(BF16)
    projected = matmul(normed, proj_ref[...])
    queries = projected[:, :width].astype(BF16) * jnp.asarray(1.0 / math.sqrt(head_dim), BF16)
    keys = projected[:, width : 2 * width].astype(BF16)
    turned = projected[:, 2 * width :].astype(BF16).T
    block_lane = iota((1, LANES), 1)
    allowed = (
        iota((rows, block_heads * rows), 0) % period == iota((rows, block_heads * rows), 1) % period
    )
    logits = []
    for block in range(width // LANES):
        lanes = slice(block * LANES, (block + 1) * LANES)
        stacked = []
        for part in range(block_heads):
            own = (block_lane >= part * head_dim) & (block_lane < (part + 1) * head_dim)
            stacked.append(queries[:, lanes] * own.astype(F32).astype(BF16))
        logits.append(
            lax.dot_general(
                keys[:, lanes], jnp.concatenate(stacked, axis=0), NT, preferred_element_type=F32
            )
        )
    attends = [softmax_down(each, allowed) for each in logits]
    mixes = []
    for block, (powers, _) in enumerate(attends):
        for part in range(block_heads):
            start = block * LANES + part * head_dim
            lanes = slice(part * rows, (part + 1) * rows)
            mixes.append(matmul(turned[start : start + head_dim], powers[:, lanes]))
    pieces = []
    for index, mixed in enumerate(mixes):
        part = index % block_heads
        pieces.append(mixed * attends[index // block_heads][1][:, part * rows : (part + 1) * rows])
    context = jnp.concatenate(pieces, axis=0).astype(BF16).T
    after_time = initial + matmul(context, temporal_out_ref[...])
    second = layer_norm(after_time, as_row(hidden_gain_ref)).astype(BF16)
    hidden = jax.nn.gelu(matmul(second, hidden_in_ref[...])).astype(BF16)
    result = (after_time + matmul(hidden, hidden_out_ref[...])).astype(BF16).astype(F32)
    headed = layer_norm(result, as_row(head_gain_ref)).astype(BF16)
    branch_velocity = matmul(headed, head_out_ref[...]).reshape(rows // period, period, width)
    conditional = branch_velocity[:, :share]
    empty = branch_velocity[:, share:]
    out_ref[...] = (empty + GUIDE * (conditional - empty)).astype(BF16)


def whole(memory_space=pltpu.VMEM):
    return pl.BlockSpec(memory_space=memory_space)


def body(
    groups,
    x_state,
    noise_field,
    rotations,
    translations,
    residue_types,
    pocket_mask,
    type_table,
    null_embed,
    spatial_gain,
    spatial_proj,
    spatial_points,
    spatial_gamma,
    spatial_out,
    temporal_gain,
    temporal_proj,
    temporal_out,
    hidden_gain,
    hidden_in,
    hidden_out,
    head_gain,
    head_out,
):
    frames, residues, width = x_state.shape
    share = residues // groups
    period = BRANCHES * share
    sources = (
        x_state,
        type_table,
        residue_types[None],
        null_embed,
        spatial_gain,
        rotations,
        translations,
        pocket_mask[None],
        spatial_proj,
        spatial_out,
        spatial_points.T,
    )
    slots = 2 * (width // LANES)
    later = (temporal_proj, temporal_out, hidden_in, hidden_out, head_out)
    spatial, *later = pl.pallas_call(
        functools.partial(spatial_kernel, groups),
        out_shape=[pltpu.VMEM((groups, frames * period, width), BF16)]
        + [pltpu.VMEM(array.shape, array.dtype) for array in later],
        in_specs=[whole(pltpu.SMEM)] + [whole(pl.ANY)] * (len(sources) + len(later)),
        out_specs=[whole()] * (1 + len(later)),
        scratch_shapes=[pltpu.VMEM(array.shape, array.dtype) for array in sources[:-1]]
        + [
            pltpu.VMEM((slots * SLOT, width), BF16),
            pltpu.VMEM((16, residues), F32),
            pltpu.SemaphoreType.DMA((len(sources) - 1 + slots + len(later),)),
        ],
        compiler_params=pltpu.CompilerParams(vmem_limit_bytes=SPATIAL_VMEM),
        name="spatial",
    )(spatial_gamma, *sources, *later)
    arrived = lax.all_to_all(spatial, "seq", split_axis=0, concat_axis=0, tiled=True)
    proj_local, out_local, in_local, hidden_local, head_local = later
    guided = pl.pallas_call(
        functools.partial(temporal_kernel, period),
        out_shape=pltpu.VMEM((groups * frames, share, width), BF16),
        in_specs=[whole()] * 9,
        out_specs=whole(),
        compiler_params=pltpu.CompilerParams(vmem_limit_bytes=TEMPORAL_VMEM),
        name="temporal",
    )(
        arrived,
        temporal_gain,
        proj_local,
        out_local,
        hidden_gain,
        in_local,
        hidden_local,
        head_gain,
        head_local,
    )
    velocity = lax.all_to_all(guided, "seq", split_axis=0, concat_axis=1, tiled=True)
    x_next = (
        x_state.astype(F32)
        + STEP_SIZE * velocity.astype(F32)
        + NOISE_SCALE * noise_field.astype(F32)
    ).astype(BF16)
    return (x_next, velocity)


def solution(mesh):
    tokens = P(("parts", "seq"), None, None)
    geometry = P(None, ("parts", "seq"), None)
    return jax.shard_map(
        functools.partial(body, mesh.shape["seq"]),
        mesh=mesh,
        in_specs=(tokens, tokens, geometry, geometry, P("parts"), P("parts")) + (P(),) * 15,
        out_specs=(tokens, tokens),
        check_vma=False,
    )
```

```python
import functools
import math

import jax
import jax.numpy as jnp
from jax import lax
from jax.experimental import pallas as pl
from jax.experimental.pallas import tpu as pltpu
from jax.sharding import PartitionSpec as P

THEADS = 6
BRANCHES = 2

WEIGHT_LOGIT = 0.7071067811865476
WEIGHT_POINT = 0.23570226039551584
GUIDE = 2.0
STEP_SIZE = 0.25
NOISE_SCALE = 0.2
EPSILON = 1e-05

BF16 = jnp.bfloat16
F32 = jnp.float32
LANES = 128
SLOT = 64
SPATIAL_VMEM = 56 * 2**20
TEMPORAL_VMEM = 40 * 2**20
NT = (((1,), (1,)), ((), ()))


def layer_norm(values, scale_gain):
    average = jnp.mean(values, axis=-1, keepdims=True)
    centered = values - average
    spread = jnp.mean(centered * centered, axis=-1, keepdims=True)
    return centered * lax.rsqrt(spread + EPSILON) * scale_gain


def as_row(ref):
    return ref[...].reshape(1, ref.shape[0])


def matmul(left, right):
    return jnp.dot(left, right, preferred_element_type=F32)


def iota(shape, axis):
    return lax.broadcasted_iota(jnp.int32, shape, axis)


def softmax_down(logits, allowed):
    logits = jnp.where(allowed, logits, -jnp.inf)
    powers = jnp.exp(logits - jnp.max(logits, axis=0, keepdims=True))
    return powers.astype(BF16), 1.0 / jnp.sum(powers, axis=0, keepdims=True)


def spatial_kernel(groups, gamma_ref, *refs):
    sources, refs = refs[:11], refs[11:]
    later, refs = refs[:5], refs[5:]
    out_ref, later_out, refs = refs[0], refs[1:6], refs[6:]
    local, (columns_ref, sems) = refs[:11], refs[11:]
    (
        x_ref,
        table_ref,
        types_ref,
        null_ref,
        gain_ref,
        rotation_ref,
        translation_ref,
        mask_ref,
        proj_ref,
        spatial_out_ref,
        points_ref,
    ) = local
    frames, residues, width = x_ref.shape
    heads = gamma_ref.shape[0]
    head_dim = width // heads
    blocks = width // LANES
    block_heads = LANES // head_dim
    slot_rows = sources[-1].shape[0] // (2 * blocks)
    per_head = slot_rows // block_heads
    share = residues // groups
    fold = max(residues, LANES)
    stacked_rows = block_heads * residues
    point_scale = 0.5 * WEIGHT_LOGIT * WEIGHT_POINT

    pairs = list(zip(sources[:10], local[:10], strict=True))
    for slot in range(2 * blocks):
        pairs.append(
            (
                sources[-1].at[pl.ds(slot * slot_rows, slot_rows), :],
                points_ref.at[pl.ds(slot * SLOT, slot_rows), :],
            )
        )
    pairs += list(zip(later, later_out, strict=True))
    copies = [
        pltpu.make_async_copy(source, target, sems.at[index])
        for index, (source, target) in enumerate(pairs)
    ]
    first = 10 + 2 * blocks
    for copy in copies[:first]:
        copy.start()
    small, wide = copies[:8], copies[8:first]

    for slot in range(2 * blocks):
        points_ref[slot * SLOT + slot_rows : (slot + 1) * SLOT, :] = jnp.zeros(
            (SLOT - slot_rows, width), BF16
        )
    lane = iota((1, LANES), 1)
    low = lane < SLOT
    place = lane % SLOT
    component = jnp.where(place < slot_rows, place % 3, 3)
    member, block_member = [], []
    for part in range(block_heads):
        member.append((place >= part * per_head) & (place < (part + 1) * per_head))
        block_member.append((lane >= part * head_dim) & (lane < (part + 1) * head_dim))
    head_lanes = [own.astype(F32).astype(BF16) for own in block_member]
    point_lanes = [
        jnp.concatenate([own, own], axis=1).astype(F32).astype(BF16) for own in member
    ]
    gamma_lanes = []
    for block in range(blocks):
        gamma = jnp.zeros((1, LANES), F32)
        for part in range(block_heads):
            gamma = jnp.where(member[part], gamma_ref[block * block_heads + part], gamma)
        gamma_lanes.append(gamma * point_scale)
    chunks = stacked_rows // fold
    chunk_rows = LANES // chunks
    diagonal = iota((chunk_rows, fold), 0) // head_dim == iota((chunk_rows, fold), 1) // residues
    same = iota((residues, stacked_rows), 0) == iota((residues, stacked_rows), 1) % residues
    columns_ref[...] = jnp.zeros_like(columns_ref)

    for copy in small:
        copy.wait()
    for copy in copies[first:]:
        copy.start()
    kinds = table_ref.shape[0]
    onehot = (iota((kinds, residues), 0) == types_ref[...]).astype(F32).T.astype(BF16)
    conditional = matmul(onehot, table_ref[...])
    empty = as_row(null_ref).astype(F32)

    tiles = []
    for frame in range(frames):
        state = x_ref[frame].astype(F32)
        initial = jnp.concatenate([state + conditional, state + empty], axis=0)
        normed = layer_norm(initial, as_row(gain_ref)).astype(BF16)

        columns_ref[0:9, :] = rotation_ref[:, frame, :]
        moved = translation_ref[:, frame, :]
        columns_ref[9:12, :] = moved - jnp.mean(moved, axis=1, keepdims=True)
        columns_ref[12:13, :] = mask_ref[...].astype(F32)
        columns = columns_ref[...].T
        allowed = (columns[:, 12:13] == 1.0) | same
        factors = []
        for step in range(-2, 3):
            factor = jnp.zeros((residues, LANES), F32)
            for row in range(3):
                if 0 <= row + step < 3:
                    entry = 3 * row + row + step
                    factor = jnp.where(component == row, columns[:, entry : entry + 1], factor)
            factors.append(jnp.concatenate([factor] * BRANCHES, axis=0))
        anchor = jnp.zeros((residues, LANES), F32)
        for row in range(3):
            anchor = jnp.where(component == row, columns[:, 9 + row : 10 + row], anchor)
        anchor = jnp.concatenate([anchor] * BRANCHES, axis=0)

        if frame == 0:
            for copy in wide:
                copy.wait()
        points = lax.dot_general(normed, points_ref[...], NT, preferred_element_type=F32)
        projected = matmul(normed, proj_ref[...])

        queries = (
            projected[:, :width].astype(BF16) * jnp.asarray(WEIGHT_LOGIT / math.sqrt(head_dim), BF16)
        )
        keys = projected[:, width : 2 * width].astype(BF16)
        values = projected[:, 2 * width :].astype(BF16)
        turned, scalar = [], []
        for branch in range(BRANCHES):
            rows = slice(branch * residues, (branch + 1) * residues)
            turned.append(values[rows].T)
            for start in range(0, width, LANES):
                lanes = slice(start, start + LANES)
                right = jnp.concatenate([queries[rows, lanes] * own for own in head_lanes], axis=0)
                scalar.append(
                    lax.dot_general(keys[rows, lanes], right, NT, preferred_element_type=F32)
                )

        slots = []
        for pair in range(blocks):
            lanes = points[:, pair * LANES : (pair + 1) * LANES]
            placed = anchor + factors[2] * lanes
            for step in (-2, -1, 1, 2):
                placed = placed + factors[step + 2] * pltpu.roll(lanes, (-step) % LANES, 1)
            swapped = pltpu.roll(placed, SLOT, 1)
            slots += [jnp.where(low, placed, swapped), jnp.where(low, swapped, placed)]

        query_feature, key_first, key_second = [], [], []
        nothing = jnp.zeros((BRANCHES * residues, LANES), BF16)
        ones = jnp.ones((residues, LANES), BF16)
        for block in range(blocks):
            feature = slots[block] * (2.0 * gamma_lanes[block])
            high = feature.astype(BF16)
            rest = (feature - high.astype(F32)).astype(BF16)
            query_feature.append(jnp.where(low, high, rest))

            feature = slots[blocks + block]
            high = feature.astype(BF16)
            rest = (feature - high.astype(F32)).astype(BF16)
            key_first.append([high])
            key_second.append([jnp.where(low, rest, nothing)])
            square = feature * feature * (-gamma_lanes[block])
            high = square.astype(BF16)
            rest = square - high.astype(F32)
            middle = rest.astype(BF16)
            last = (rest - middle.astype(F32)).astype(BF16)
            key_first[block].append(jnp.where(low, high, middle))
            key_second[block].append(jnp.where(low, last, nothing))

        logits = []
        for branch in range(BRANCHES):
            rows = slice(branch * residues, (branch + 1) * residues)
            for block in range(blocks):
                left = jnp.concatenate(
                    [
                        jnp.concatenate([piece[rows] for piece in pieces[block]], axis=1)
                        for pieces in (key_first, key_second)
                    ],
                    axis=0,
                )
                right = jnp.concatenate([query_feature[block][rows], ones], axis=1)
                right = jnp.concatenate([right * own for own in point_lanes], axis=0)
                both = lax.dot_general(left, right, NT, preferred_element_type=F32)
                logits.append(scalar[len(logits)] + both[:residues] + both[residues:])
        attends = [softmax_down(each, allowed) for each in logits]
        mixes = []
        for index, (powers, _) in enumerate(attends):
            block = index % blocks
            for chunk in range(chunks):
                start = block * LANES + chunk * chunk_rows
                mixes.append(
                    matmul(
                        turned[index // blocks][start : start + chunk_rows],
                        powers[:, chunk * fold : (chunk + 1) * fold],
                    )
                )
        contexts = []
        for branch in range(BRANCHES):
            pieces = []
            for index in range(branch * blocks, (branch + 1) * blocks):
                scale = attends[index][1]
                for chunk in range(chunks):
                    mixed = mixes[index * chunks + chunk]
                    mixed = mixed * scale[:, chunk * fold : (chunk + 1) * fold]
                    pieces.append(jnp.where(diagonal, mixed, 0.0))
            context = jnp.concatenate(pieces, axis=0).astype(BF16).T
            joined = context[:residues]
            for start in range(residues, fold, residues):
                joined = joined + context[start : start + residues]
            contexts.append(joined)
        update = matmul(jnp.concatenate(contexts, axis=0), spatial_out_ref[...])
        total = initial + update
        tiles.append(
            [
                jnp.concatenate(
                    [
                        total[start : start + share]
                        for start in range(group * share, BRANCHES * residues, residues)
                    ],
                    axis=0,
                )
                for group in range(groups)
            ]
        )
    for group in range(groups):
        out_ref[group] = jnp.concatenate([tile[group] for tile in tiles], axis=0).astype(BF16)
    for copy in copies[first:]:
        copy.wait()


def temporal_kernel(
    period,
    x_ref,
    gain_ref,
    proj_ref,
    temporal_out_ref,
    hidden_gain_ref,
    hidden_in_ref,
    hidden_out_ref,
    head_gain_ref,
    head_out_ref,
    out_ref,
):
    groups, depth, width = x_ref.shape
    rows = groups * depth
    head_dim = width // THEADS
    block_heads = LANES // head_dim
    share = period // BRANCHES

    initial = x_ref[...].astype(F32).reshape(rows, width)
    normed = layer_norm(initial, as_row(gain_ref)).astype(BF16)
    projected = matmul(normed, proj_ref[...])
    queries = projected[:, :width].astype(BF16) * jnp.asarray(1.0 / math.sqrt(head_dim), BF16)
    keys = projected[:, width : 2 * width].astype(BF16)
    turned = projected[:, 2 * width :].astype(BF16).T
    block_lane = iota((1, LANES), 1)
    allowed = (
        iota((rows, block_heads * rows), 0) % period == iota((rows, block_heads * rows), 1) % period
    )
    logits = []
    for block in range(width // LANES):
        lanes = slice(block * LANES, (block + 1) * LANES)
        stacked = []
        for part in range(block_heads):
            own = (block_lane >= part * head_dim) & (block_lane < (part + 1) * head_dim)
            stacked.append(queries[:, lanes] * own.astype(F32).astype(BF16))
        logits.append(
            lax.dot_general(
                keys[:, lanes], jnp.concatenate(stacked, axis=0), NT, preferred_element_type=F32
            )
        )
    attends = [softmax_down(each, allowed) for each in logits]
    mixes = []
    for block, (powers, _) in enumerate(attends):
        for part in range(block_heads):
            start = block * LANES + part * head_dim
            lanes = slice(part * rows, (part + 1) * rows)
            mixes.append(matmul(turned[start : start + head_dim], powers[:, lanes]))
    pieces = []
    for index, mixed in enumerate(mixes):
        part = index % block_heads
        pieces.append(mixed * attends[index // block_heads][1][:, part * rows : (part + 1) * rows])
    context = jnp.concatenate(pieces, axis=0).astype(BF16).T
    after_time = initial + matmul(context, temporal_out_ref[...])
    second = layer_norm(after_time, as_row(hidden_gain_ref)).astype(BF16)
    hidden = jax.nn.gelu(matmul(second, hidden_in_ref[...])).astype(BF16)
    result = (after_time + matmul(hidden, hidden_out_ref[...])).astype(BF16).astype(F32)
    headed = layer_norm(result, as_row(head_gain_ref)).astype(BF16)
    branch_velocity = matmul(headed, head_out_ref[...]).reshape(rows // period, period, width)
    conditional = branch_velocity[:, :share]
    empty = branch_velocity[:, share:]
    out_ref[...] = (empty + GUIDE * (conditional - empty)).astype(BF16)


def whole(memory_space=pltpu.VMEM):
    return pl.BlockSpec(memory_space=memory_space)


def body(
    groups,
    x_state,
    noise_field,
    rotations,
    translations,
    residue_types,
    pocket_mask,
    type_table,
    null_embed,
    spatial_gain,
    spatial_proj,
    spatial_points,
    spatial_gamma,
    spatial_out,
    temporal_gain,
    temporal_proj,
    temporal_out,
    hidden_gain,
    hidden_in,
    hidden_out,
    head_gain,
    head_out,
):
    frames, residues, width = x_state.shape
    share = residues // groups
    period = BRANCHES * share
    sources = (
        x_state,
        type_table,
        residue_types[None],
        null_embed,
        spatial_gain,
        rotations,
        translations,
        pocket_mask[None],
        spatial_proj,
        spatial_out,
        spatial_points.T,
    )
    slots = 2 * (width // LANES)
    later = (temporal_proj, temporal_out, hidden_in, hidden_out, head_out)
    spatial, *later = pl.pallas_call(
        functools.partial(spatial_kernel, groups),
        out_shape=[pltpu.VMEM((groups, frames * period, width), BF16)]
        + [pltpu.VMEM(array.shape, array.dtype) for array in later],
        in_specs=[whole(pltpu.SMEM)] + [whole(pl.ANY)] * (len(sources) + len(later)),
        out_specs=[whole()] * (1 + len(later)),
        scratch_shapes=[pltpu.VMEM(array.shape, array.dtype) for array in sources[:-1]]
        + [
            pltpu.VMEM((slots * SLOT, width), BF16),
            pltpu.VMEM((16, residues), F32),
            pltpu.SemaphoreType.DMA((len(sources) - 1 + slots + len(later),)),
        ],
        compiler_params=pltpu.CompilerParams(vmem_limit_bytes=SPATIAL_VMEM),
        name="spatial",
    )(spatial_gamma, *sources, *later)
    arrived = lax.all_to_all(spatial, "seq", split_axis=0, concat_axis=0, tiled=True)
    proj_local, out_local, in_local, hidden_local, head_local = later
    guided = pl.pallas_call(
        functools.partial(temporal_kernel, period),
        out_shape=pltpu.VMEM((groups * frames, share, width), BF16),
        in_specs=[whole()] * 9,
        out_specs=whole(),
        compiler_params=pltpu.CompilerParams(vmem_limit_bytes=TEMPORAL_VMEM),
        name="temporal",
    )(
        arrived,
        temporal_gain,
        proj_local,
        out_local,
        hidden_gain,
        in_local,
        hidden_local,
        head_gain,
        head_local,
    )
    velocity = lax.all_to_all(guided, "seq", split_axis=0, concat_axis=1, tiled=True)
    x_next = (
        x_state.astype(F32)
        + STEP_SIZE * velocity.astype(F32)
        + NOISE_SCALE * noise_field.astype(F32)
    ).astype(BF16)
    return (x_next, velocity)


def solution(mesh):
    tokens = P(("parts", "seq"), None, None)
    geometry = P(None, ("parts", "seq"), None)
    return jax.shard_map(
        functools.partial(body, mesh.shape["seq"]),
        mesh=mesh,
        in_specs=(tokens, tokens, geometry, geometry, P("parts"), P("parts")) + (P(),) * 15,
        out_specs=(tokens, tokens),
        check_vma=False,
    )
```

```python
import functools
import math

import jax
import jax.numpy as jnp
from jax import lax
from jax.experimental import pallas as pl
from jax.experimental.pallas import tpu as pltpu
from jax.sharding import PartitionSpec as P

THEADS = 6
BRANCHES = 2

WEIGHT_LOGIT = 0.7071067811865476
WEIGHT_POINT = 0.23570226039551584
GUIDE = 2.0
STEP_SIZE = 0.25
NOISE_SCALE = 0.2
EPSILON = 1e-05

BF16 = jnp.bfloat16
F32 = jnp.float32
LANES = 128
SLOT = 64
PIECE = 384 * 512
MOST_PIECES = 16
SPATIAL_VMEM = 56 * 2**20
TEMPORAL_VMEM = 40 * 2**20
NT = (((1,), (1,)), ((), ()))


def layer_norm(values, scale_gain):
    average = jnp.mean(values, axis=-1, keepdims=True)
    centered = values - average
    spread = jnp.mean(centered * centered, axis=-1, keepdims=True)
    return centered * lax.rsqrt(spread + EPSILON) * scale_gain


def as_row(ref):
    return ref[...].reshape(1, ref.shape[0])


def matmul(left, right):
    return jnp.dot(left, right, preferred_element_type=F32)


def iota(shape, axis):
    return lax.broadcasted_iota(jnp.int32, shape, axis)


def softmax_down(logits, allowed):
    logits = jnp.where(allowed, logits, -jnp.inf)
    powers = jnp.exp(logits - jnp.max(logits, axis=0, keepdims=True))
    return powers.astype(BF16), 1.0 / jnp.sum(powers, axis=0, keepdims=True)


def spatial_kernel(groups, gamma_ref, *refs):
    sources, refs = refs[:11], refs[11:]
    later, refs = refs[:5], refs[5:]
    out_ref, later_out, refs = refs[0], refs[1:6], refs[6:]
    local, (columns_ref, sems) = refs[:11], refs[11:]
    (
        x_ref,
        table_ref,
        types_ref,
        null_ref,
        gain_ref,
        rotation_ref,
        translation_ref,
        mask_ref,
        proj_ref,
        spatial_out_ref,
        points_ref,
    ) = local
    frames, residues, width = x_ref.shape
    heads = gamma_ref.shape[0]
    head_dim = width // heads
    blocks = width // LANES
    block_heads = LANES // head_dim
    slot_rows = sources[-1].shape[0] // (2 * blocks)
    per_head = slot_rows // block_heads
    share = residues // groups
    fold = max(residues, LANES)
    stacked_rows = block_heads * residues
    point_scale = 0.5 * WEIGHT_LOGIT * WEIGHT_POINT

    pairs = list(zip(sources[:10], local[:10], strict=True))
    for slot in range(2 * blocks):
        pairs.append(
            (
                sources[-1].at[pl.ds(slot * slot_rows, slot_rows), :],
                points_ref.at[pl.ds(slot * SLOT, slot_rows), :],
            )
        )
    for source, target in zip(later, later_out, strict=True):
        rows = source.shape[0] // max(1, source.shape[0] * source.shape[1] // PIECE)
        for start in range(0, source.shape[0], rows):
            taken = pl.ds(start, rows)
            pairs.append((source.at[taken, :], target.at[taken, :]))
    copies = [
        pltpu.make_async_copy(source, target, sems.at[index])
        for index, (source, target) in enumerate(pairs)
    ]
    first = 10 + 2 * blocks
    for copy in copies:
        copy.start()
    small, wide = copies[:8], copies[8:first]

    for slot in range(2 * blocks):
        points_ref[slot * SLOT + slot_rows : (slot + 1) * SLOT, :] = jnp.zeros(
            (SLOT - slot_rows, width), BF16
        )
    lane = iota((1, LANES), 1)
    low = lane < SLOT
    place = lane % SLOT
    component = jnp.where(place < slot_rows, place % 3, 3)
    member, block_member = [], []
    for part in range(block_heads):
        member.append((place >= part * per_head) & (place < (part + 1) * per_head))
        block_member.append((lane >= part * head_dim) & (lane < (part + 1) * head_dim))
    head_lanes = [own.astype(F32).astype(BF16) for own in block_member]
    point_lanes = [
        jnp.concatenate([own, own], axis=1).astype(F32).astype(BF16) for own in member
    ]
    gamma_lanes = []
    for block in range(blocks):
        gamma = jnp.zeros((1, LANES), F32)
        for part in range(block_heads):
            gamma = jnp.where(member[part], gamma_ref[block * block_heads + part], gamma)
        gamma_lanes.append(gamma * point_scale)
    chunks = stacked_rows // fold
    chunk_rows = LANES // chunks
    diagonal = iota((chunk_rows, fold), 0) // head_dim == iota((chunk_rows, fold), 1) // residues
    same = iota((residues, stacked_rows), 0) == iota((residues, stacked_rows), 1) % residues
    columns_ref[...] = jnp.zeros_like(columns_ref)

    for copy in small:
        copy.wait()
    kinds = table_ref.shape[0]
    onehot = (iota((kinds, residues), 0) == types_ref[...]).astype(F32).T.astype(BF16)
    conditional = matmul(onehot, table_ref[...])
    empty = as_row(null_ref).astype(F32)

    tiles = []
    for frame in range(frames):
        state = x_ref[frame].astype(F32)
        initial = jnp.concatenate([state + conditional, state + empty], axis=0)
        normed = layer_norm(initial, as_row(gain_ref)).astype(BF16)

        columns_ref[0:9, :] = rotation_ref[:, frame, :]
        moved = translation_ref[:, frame, :]
        columns_ref[9:12, :] = moved - jnp.mean(moved, axis=1, keepdims=True)
        columns_ref[12:13, :] = mask_ref[...].astype(F32)
        columns = columns_ref[...].T
        allowed = (columns[:, 12:13] == 1.0) | same
        factors = []
        for step in range(-2, 3):
            factor = jnp.zeros((residues, LANES), F32)
            for row in range(3):
                if 0 <= row + step < 3:
                    entry = 3 * row + row + step
                    factor = jnp.where(component == row, columns[:, entry : entry + 1], factor)
            factors.append(jnp.concatenate([factor] * BRANCHES, axis=0))
        anchor = jnp.zeros((residues, LANES), F32)
        for row in range(3):
            anchor = jnp.where(component == row, columns[:, 9 + row : 10 + row], anchor)
        anchor = jnp.concatenate([anchor] * BRANCHES, axis=0)

        if frame == 0:
            for copy in wide:
                copy.wait()
        points = lax.dot_general(normed, points_ref[...], NT, preferred_element_type=F32)
        projected = matmul(normed, proj_ref[...])

        queries = (
            projected[:, :width].astype(BF16) * jnp.asarray(WEIGHT_LOGIT / math.sqrt(head_dim), BF16)
        )
        keys = projected[:, width : 2 * width].astype(BF16)
        values = projected[:, 2 * width :].astype(BF16)
        turned, scalar = [], []
        for branch in range(BRANCHES):
            rows = slice(branch * residues, (branch + 1) * residues)
            turned.append(values[rows].T)
            for start in range(0, width, LANES):
                lanes = slice(start, start + LANES)
                right = jnp.concatenate([queries[rows, lanes] * own for own in head_lanes], axis=0)
                scalar.append(
                    lax.dot_general(keys[rows, lanes], right, NT, preferred_element_type=F32)
                )

        slots = []
        for pair in range(blocks):
            lanes = points[:, pair * LANES : (pair + 1) * LANES]
            placed = anchor + factors[2] * lanes
            for step in (-2, -1, 1, 2):
                placed = placed + factors[step + 2] * pltpu.roll(lanes, (-step) % LANES, 1)
            swapped = pltpu.roll(placed, SLOT, 1)
            slots += [jnp.where(low, placed, swapped), jnp.where(low, swapped, placed)]

        query_feature, key_first, key_second = [], [], []
        nothing = jnp.zeros((BRANCHES * residues, LANES), BF16)
        ones = jnp.ones((residues, LANES), BF16)
        for block in range(blocks):
            feature = slots[block] * (2.0 * gamma_lanes[block])
            high = feature.astype(BF16)
            rest = (feature - high.astype(F32)).astype(BF16)
            query_feature.append(jnp.where(low, high, rest))

            feature = slots[blocks + block]
            high = feature.astype(BF16)
            rest = (feature - high.astype(F32)).astype(BF16)
            key_first.append([high])
            key_second.append([jnp.where(low, rest, nothing)])
            square = feature * feature * (-gamma_lanes[block])
            high = square.astype(BF16)
            rest = square - high.astype(F32)
            middle = rest.astype(BF16)
            last = (rest - middle.astype(F32)).astype(BF16)
            key_first[block].append(jnp.where(low, high, middle))
            key_second[block].append(jnp.where(low, last, nothing))

        logits = []
        for branch in range(BRANCHES):
            rows = slice(branch * residues, (branch + 1) * residues)
            for block in range(blocks):
                left = jnp.concatenate(
                    [
                        jnp.concatenate([piece[rows] for piece in pieces[block]], axis=1)
                        for pieces in (key_first, key_second)
                    ],
                    axis=0,
                )
                right = jnp.concatenate([query_feature[block][rows], ones], axis=1)
                right = jnp.concatenate([right * own for own in point_lanes], axis=0)
                both = lax.dot_general(left, right, NT, preferred_element_type=F32)
                logits.append(scalar[len(logits)] + both[:residues] + both[residues:])
        attends = [softmax_down(each, allowed) for each in logits]
        mixes = []
        for index, (powers, _) in enumerate(attends):
            block = index % blocks
            for chunk in range(chunks):
                start = block * LANES + chunk * chunk_rows
                mixes.append(
                    matmul(
                        turned[index // blocks][start : start + chunk_rows],
                        powers[:, chunk * fold : (chunk + 1) * fold],
                    )
                )
        contexts = []
        for branch in range(BRANCHES):
            pieces = []
            for index in range(branch * blocks, (branch + 1) * blocks):
                scale = attends[index][1]
                for chunk in range(chunks):
                    mixed = mixes[index * chunks + chunk]
                    mixed = mixed * scale[:, chunk * fold : (chunk + 1) * fold]
                    pieces.append(jnp.where(diagonal, mixed, 0.0))
            context = jnp.concatenate(pieces, axis=0).astype(BF16).T
            joined = context[:residues]
            for start in range(residues, fold, residues):
                joined = joined + context[start : start + residues]
            contexts.append(joined)
        update = matmul(jnp.concatenate(contexts, axis=0), spatial_out_ref[...])
        total = initial + update
        tiles.append(
            [
                jnp.concatenate(
                    [
                        total[start : start + share]
                        for start in range(group * share, BRANCHES * residues, residues)
                    ],
                    axis=0,
                )
                for group in range(groups)
            ]
        )
    for group in range(groups):
        out_ref[group] = jnp.concatenate([tile[group] for tile in tiles], axis=0).astype(BF16)
    for copy in copies[first:]:
        copy.wait()


def temporal_kernel(
    period,
    x_ref,
    gain_ref,
    proj_ref,
    temporal_out_ref,
    hidden_gain_ref,
    hidden_in_ref,
    hidden_out_ref,
    head_gain_ref,
    head_out_ref,
    out_ref,
):
    groups, depth, width = x_ref.shape
    rows = groups * depth
    head_dim = width // THEADS
    block_heads = LANES // head_dim
    share = period // BRANCHES

    initial = x_ref[...].astype(F32).reshape(rows, width)
    normed = layer_norm(initial, as_row(gain_ref)).astype(BF16)
    projected = matmul(normed, proj_ref[...])
    queries = projected[:, :width].astype(BF16) * jnp.asarray(1.0 / math.sqrt(head_dim), BF16)
    keys = projected[:, width : 2 * width].astype(BF16)
    turned = projected[:, 2 * width :].astype(BF16).T
    block_lane = iota((1, LANES), 1)
    allowed = (
        iota((rows, block_heads * rows), 0) % period == iota((rows, block_heads * rows), 1) % period
    )
    logits = []
    for block in range(width // LANES):
        lanes = slice(block * LANES, (block + 1) * LANES)
        stacked = []
        for part in range(block_heads):
            own = (block_lane >= part * head_dim) & (block_lane < (part + 1) * head_dim)
            stacked.append(queries[:, lanes] * own.astype(F32).astype(BF16))
        logits.append(
            lax.dot_general(
                keys[:, lanes], jnp.concatenate(stacked, axis=0), NT, preferred_element_type=F32
            )
        )
    attends = [softmax_down(each, allowed) for each in logits]
    mixes = []
    for block, (powers, _) in enumerate(attends):
        for part in range(block_heads):
            start = block * LANES + part * head_dim
            lanes = slice(part * rows, (part + 1) * rows)
            mixes.append(matmul(turned[start : start + head_dim], powers[:, lanes]))
    pieces = []
    for index, mixed in enumerate(mixes):
        part = index % block_heads
        pieces.append(mixed * attends[index // block_heads][1][:, part * rows : (part + 1) * rows])
    context = jnp.concatenate(pieces, axis=0).astype(BF16).T
    after_time = initial + matmul(context, temporal_out_ref[...])
    second = layer_norm(after_time, as_row(hidden_gain_ref)).astype(BF16)
    hidden = jax.nn.gelu(matmul(second, hidden_in_ref[...])).astype(BF16)
    result = (after_time + matmul(hidden, hidden_out_ref[...])).astype(BF16).astype(F32)
    headed = layer_norm(result, as_row(head_gain_ref)).astype(BF16)
    branch_velocity = matmul(headed, head_out_ref[...]).reshape(rows // period, period, width)
    conditional = branch_velocity[:, :share]
    empty = branch_velocity[:, share:]
    out_ref[...] = (empty + GUIDE * (conditional - empty)).astype(BF16)


def whole(memory_space=pltpu.VMEM):
    return pl.BlockSpec(memory_space=memory_space)


def body(
    groups,
    x_state,
    noise_field,
    rotations,
    translations,
    residue_types,
    pocket_mask,
    type_table,
    null_embed,
    spatial_gain,
    spatial_proj,
    spatial_points,
    spatial_gamma,
    spatial_out,
    temporal_gain,
    temporal_proj,
    temporal_out,
    hidden_gain,
    hidden_in,
    hidden_out,
    head_gain,
    head_out,
):
    frames, residues, width = x_state.shape
    share = residues // groups
    period = BRANCHES * share
    sources = (
        x_state,
        type_table,
        residue_types[None],
        null_embed,
        spatial_gain,
        rotations,
        translations,
        pocket_mask[None],
        spatial_proj,
        spatial_out,
        spatial_points.T,
    )
    slots = 2 * (width // LANES)
    later = (temporal_proj, temporal_out, hidden_in, hidden_out, head_out)
    spatial, *later = pl.pallas_call(
        functools.partial(spatial_kernel, groups),
        out_shape=[pltpu.VMEM((groups, frames * period, width), BF16)]
        + [pltpu.VMEM(array.shape, array.dtype) for array in later],
        in_specs=[whole(pltpu.SMEM)] + [whole(pl.ANY)] * (len(sources) + len(later)),
        out_specs=[whole()] * (1 + len(later)),
        scratch_shapes=[pltpu.VMEM(array.shape, array.dtype) for array in sources[:-1]]
        + [
            pltpu.VMEM((slots * SLOT, width), BF16),
            pltpu.VMEM((16, residues), F32),
            pltpu.SemaphoreType.DMA((len(sources) - 1 + slots + MOST_PIECES,)),
        ],
        compiler_params=pltpu.CompilerParams(vmem_limit_bytes=SPATIAL_VMEM),
        name="spatial",
    )(spatial_gamma, *sources, *later)
    arrived = lax.all_to_all(spatial, "seq", split_axis=0, concat_axis=0, tiled=True)
    proj_local, out_local, in_local, hidden_local, head_local = later
    guided = pl.pallas_call(
        functools.partial(temporal_kernel, period),
        out_shape=pltpu.VMEM((groups * frames, share, width), BF16),
        in_specs=[whole()] * 9,
        out_specs=whole(),
        compiler_params=pltpu.CompilerParams(vmem_limit_bytes=TEMPORAL_VMEM),
        name="temporal",
    )(
        arrived,
        temporal_gain,
        proj_local,
        out_local,
        hidden_gain,
        in_local,
        hidden_local,
        head_gain,
        head_local,
    )
    velocity = lax.all_to_all(guided, "seq", split_axis=0, concat_axis=1, tiled=True)
    x_next = (
        x_state.astype(F32)
        + STEP_SIZE * velocity.astype(F32)
        + NOISE_SCALE * noise_field.astype(F32)
    ).astype(BF16)
    return (x_next, velocity)


def solution(mesh):
    tokens = P(("parts", "seq"), None, None)
    geometry = P(None, ("parts", "seq"), None)
    return jax.shard_map(
        functools.partial(body, mesh.shape["seq"]),
        mesh=mesh,
        in_specs=(tokens, tokens, geometry, geometry, P("parts"), P("parts")) + (P(),) * 15,
        out_specs=(tokens, tokens),
        check_vma=False,
    )
```

```python
import functools
import math

import jax
import jax.numpy as jnp
from jax import lax
from jax.experimental import pallas as pl
from jax.experimental.pallas import tpu as pltpu
from jax.sharding import PartitionSpec as P

THEADS = 6
BRANCHES = 2

WEIGHT_LOGIT = 0.7071067811865476
WEIGHT_POINT = 0.23570226039551584
GUIDE = 2.0
STEP_SIZE = 0.25
NOISE_SCALE = 0.2
EPSILON = 1e-05

BF16 = jnp.bfloat16
F32 = jnp.float32
LANES = 128
SLOT = 64
SPATIAL_VMEM = 56 * 2**20
TEMPORAL_VMEM = 40 * 2**20
NT = (((1,), (1,)), ((), ()))


def layer_norm(values, scale_gain):
    average = jnp.mean(values, axis=-1, keepdims=True)
    centered = values - average
    spread = jnp.mean(centered * centered, axis=-1, keepdims=True)
    return centered * lax.rsqrt(spread + EPSILON) * scale_gain


def as_row(ref):
    return ref[...].reshape(1, ref.shape[0])


def matmul(left, right):
    return jnp.dot(left, right, preferred_element_type=F32)


def iota(shape, axis):
    return lax.broadcasted_iota(jnp.int32, shape, axis)


def softmax_down(logits, allowed):
    logits = jnp.where(allowed, logits, -jnp.inf)
    powers = jnp.exp(logits - jnp.max(logits, axis=0, keepdims=True))
    return powers.astype(BF16), 1.0 / jnp.sum(powers, axis=0, keepdims=True)


def spatial_kernel(groups, gamma_ref, *refs):
    sources, refs = refs[:11], refs[11:]
    later, refs = refs[:5], refs[5:]
    out_ref, later_out, refs = refs[0], refs[1:6], refs[6:]
    local, (columns_ref, sems) = refs[:11], refs[11:]
    (
        x_ref,
        table_ref,
        types_ref,
        null_ref,
        gain_ref,
        rotation_ref,
        translation_ref,
        mask_ref,
        proj_ref,
        spatial_out_ref,
        points_ref,
    ) = local
    frames, residues, width = x_ref.shape
    heads = gamma_ref.shape[0]
    head_dim = width // heads
    blocks = width // LANES
    block_heads = LANES // head_dim
    slot_rows = sources[-1].shape[0] // (2 * blocks)
    per_head = slot_rows // block_heads
    share = residues // groups
    fold = max(residues, LANES)
    stacked_rows = block_heads * residues
    point_scale = 0.5 * WEIGHT_LOGIT * WEIGHT_POINT

    pairs = list(zip(sources[:8], local[:8], strict=True))
    for slot in range(2 * blocks):
        pairs.append(
            (
                sources[-1].at[pl.ds(slot * slot_rows, slot_rows), :],
                points_ref.at[pl.ds(slot * SLOT, slot_rows), :],
            )
        )
    pairs += list(zip(sources[8:10] + later, local[8:10] + tuple(later_out), strict=True))
    copies = [
        pltpu.make_async_copy(source, target, sems.at[index])
        for index, (source, target) in enumerate(pairs)
    ]
    first = 10 + 2 * blocks
    for copy in copies[:first]:
        copy.start()
    small, wide, after = copies[:8], copies[8 : first - 1], copies[first - 1]

    for slot in range(2 * blocks):
        points_ref[slot * SLOT + slot_rows : (slot + 1) * SLOT, :] = jnp.zeros(
            (SLOT - slot_rows, width), BF16
        )
    lane = iota((1, LANES), 1)
    low = lane < SLOT
    place = lane % SLOT
    component = jnp.where(place < slot_rows, place % 3, 3)
    member, block_member = [], []
    for part in range(block_heads):
        member.append((place >= part * per_head) & (place < (part + 1) * per_head))
        block_member.append((lane >= part * head_dim) & (lane < (part + 1) * head_dim))
    head_lanes = [own.astype(F32).astype(BF16) for own in block_member]
    point_lanes = [
        jnp.concatenate([own, own], axis=1).astype(F32).astype(BF16) for own in member
    ]
    gamma_lanes = []
    for block in range(blocks):
        gamma = jnp.zeros((1, LANES), F32)
        for part in range(block_heads):
            gamma = jnp.where(member[part], gamma_ref[block * block_heads + part], gamma)
        gamma_lanes.append(gamma * point_scale)
    chunks = stacked_rows // fold
    chunk_rows = LANES // chunks
    diagonal = iota((chunk_rows, fold), 0) // head_dim == iota((chunk_rows, fold), 1) // residues
    same = iota((residues, stacked_rows), 0) == iota((residues, stacked_rows), 1) % residues
    columns_ref[...] = jnp.zeros_like(columns_ref)

    for copy in small:
        copy.wait()
    for copy in copies[first:]:
        copy.start()
    kinds = table_ref.shape[0]
    onehot = (iota((kinds, residues), 0) == types_ref[...]).astype(F32).T.astype(BF16)
    conditional = matmul(onehot, table_ref[...])
    empty = as_row(null_ref).astype(F32)

    tiles = []
    for frame in range(frames):
        state = x_ref[frame].astype(F32)
        initial = jnp.concatenate([state + conditional, state + empty], axis=0)
        normed = layer_norm(initial, as_row(gain_ref)).astype(BF16)

        columns_ref[0:9, :] = rotation_ref[:, frame, :]
        moved = translation_ref[:, frame, :]
        columns_ref[9:12, :] = moved - jnp.mean(moved, axis=1, keepdims=True)
        columns_ref[12:13, :] = mask_ref[...].astype(F32)
        columns = columns_ref[...].T
        allowed = (columns[:, 12:13] == 1.0) | same
        factors = []
        for step in range(-2, 3):
            factor = jnp.zeros((residues, LANES), F32)
            for row in range(3):
                if 0 <= row + step < 3:
                    entry = 3 * row + row + step
                    factor = jnp.where(component == row, columns[:, entry : entry + 1], factor)
            factors.append(jnp.concatenate([factor] * BRANCHES, axis=0))
        anchor = jnp.zeros((residues, LANES), F32)
        for row in range(3):
            anchor = jnp.where(component == row, columns[:, 9 + row : 10 + row], anchor)
        anchor = jnp.concatenate([anchor] * BRANCHES, axis=0)

        if frame == 0:
            for copy in wide:
                copy.wait()
        points = lax.dot_general(normed, points_ref[...], NT, preferred_element_type=F32)
        projected = matmul(normed, proj_ref[...])

        queries = (
            projected[:, :width].astype(BF16) * jnp.asarray(WEIGHT_LOGIT / math.sqrt(head_dim), BF16)
        )
        keys = projected[:, width : 2 * width].astype(BF16)
        values = projected[:, 2 * width :].astype(BF16)
        turned, scalar = [], []
        for branch in range(BRANCHES):
            rows = slice(branch * residues, (branch + 1) * residues)
            turned.append(values[rows].T)
            for start in range(0, width, LANES):
                lanes = slice(start, start + LANES)
                right = jnp.concatenate([queries[rows, lanes] * own for own in head_lanes], axis=0)
                scalar.append(
                    lax.dot_general(keys[rows, lanes], right, NT, preferred_element_type=F32)
                )

        slots = []
        for pair in range(blocks):
            lanes = points[:, pair * LANES : (pair + 1) * LANES]
            placed = anchor + factors[2] * lanes
            for step in (-2, -1, 1, 2):
                placed = placed + factors[step + 2] * pltpu.roll(lanes, (-step) % LANES, 1)
            swapped = pltpu.roll(placed, SLOT, 1)
            slots += [jnp.where(low, placed, swapped), jnp.where(low, swapped, placed)]

        query_feature, key_first, key_second = [], [], []
        nothing = jnp.zeros((BRANCHES * residues, LANES), BF16)
        ones = jnp.ones((residues, LANES), BF16)
        for block in range(blocks):
            feature = slots[block] * (2.0 * gamma_lanes[block])
            high = feature.astype(BF16)
            rest = (feature - high.astype(F32)).astype(BF16)
            query_feature.append(jnp.where(low, high, rest))

            feature = slots[blocks + block]
            high = feature.astype(BF16)
            rest = (feature - high.astype(F32)).astype(BF16)
            key_first.append([high])
            key_second.append([jnp.where(low, rest, nothing)])
            square = feature * feature * (-gamma_lanes[block])
            high = square.astype(BF16)
            rest = square - high.astype(F32)
            middle = rest.astype(BF16)
            last = (rest - middle.astype(F32)).astype(BF16)
            key_first[block].append(jnp.where(low, high, middle))
            key_second[block].append(jnp.where(low, last, nothing))

        logits = []
        for branch in range(BRANCHES):
            rows = slice(branch * residues, (branch + 1) * residues)
            for block in range(blocks):
                left = jnp.concatenate(
                    [
                        jnp.concatenate([piece[rows] for piece in pieces[block]], axis=1)
                        for pieces in (key_first, key_second)
                    ],
                    axis=0,
                )
                right = jnp.concatenate([query_feature[block][rows], ones], axis=1)
                right = jnp.concatenate([right * own for own in point_lanes], axis=0)
                both = lax.dot_general(left, right, NT, preferred_element_type=F32)
                logits.append(scalar[len(logits)] + both[:residues] + both[residues:])
        attends = [softmax_down(each, allowed) for each in logits]
        mixes = []
        for index, (powers, _) in enumerate(attends):
            block = index % blocks
            for chunk in range(chunks):
                start = block * LANES + chunk * chunk_rows
                mixes.append(
                    matmul(
                        turned[index // blocks][start : start + chunk_rows],
                        powers[:, chunk * fold : (chunk + 1) * fold],
                    )
                )
        contexts = []
        for branch in range(BRANCHES):
            pieces = []
            for index in range(branch * blocks, (branch + 1) * blocks):
                scale = attends[index][1]
                for chunk in range(chunks):
                    mixed = mixes[index * chunks + chunk]
                    mixed = mixed * scale[:, chunk * fold : (chunk + 1) * fold]
                    pieces.append(jnp.where(diagonal, mixed, 0.0))
            context = jnp.concatenate(pieces, axis=0).astype(BF16).T
            joined = context[:residues]
            for start in range(residues, fold, residues):
                joined = joined + context[start : start + residues]
            contexts.append(joined)
        if frame == 0:
            after.wait()
        update = matmul(jnp.concatenate(contexts, axis=0), spatial_out_ref[...])
        total = initial + update
        tiles.append(
            [
                jnp.concatenate(
                    [
                        total[start : start + share]
                        for start in range(group * share, BRANCHES * residues, residues)
                    ],
                    axis=0,
                )
                for group in range(groups)
            ]
        )
    for group in range(groups):
        out_ref[group] = jnp.concatenate([tile[group] for tile in tiles], axis=0).astype(BF16)
    for copy in copies[first:]:
        copy.wait()


def temporal_kernel(
    period,
    x_ref,
    gain_ref,
    proj_ref,
    temporal_out_ref,
    hidden_gain_ref,
    hidden_in_ref,
    hidden_out_ref,
    head_gain_ref,
    head_out_ref,
    out_ref,
):
    groups, depth, width = x_ref.shape
    rows = groups * depth
    head_dim = width // THEADS
    block_heads = LANES // head_dim
    share = period // BRANCHES

    initial = x_ref[...].astype(F32).reshape(rows, width)
    normed = layer_norm(initial, as_row(gain_ref)).astype(BF16)
    projected = matmul(normed, proj_ref[...])
    queries = projected[:, :width].astype(BF16) * jnp.asarray(1.0 / math.sqrt(head_dim), BF16)
    keys = projected[:, width : 2 * width].astype(BF16)
    turned = projected[:, 2 * width :].astype(BF16).T
    block_lane = iota((1, LANES), 1)
    allowed = (
        iota((rows, block_heads * rows), 0) % period == iota((rows, block_heads * rows), 1) % period
    )
    logits = []
    for block in range(width // LANES):
        lanes = slice(block * LANES, (block + 1) * LANES)
        stacked = []
        for part in range(block_heads):
            own = (block_lane >= part * head_dim) & (block_lane < (part + 1) * head_dim)
            stacked.append(queries[:, lanes] * own.astype(F32).astype(BF16))
        logits.append(
            lax.dot_general(
                keys[:, lanes], jnp.concatenate(stacked, axis=0), NT, preferred_element_type=F32
            )
        )
    attends = [softmax_down(each, allowed) for each in logits]
    mixes = []
    for block, (powers, _) in enumerate(attends):
        for part in range(block_heads):
            start = block * LANES + part * head_dim
            lanes = slice(part * rows, (part + 1) * rows)
            mixes.append(matmul(turned[start : start + head_dim], powers[:, lanes]))
    pieces = []
    for index, mixed in enumerate(mixes):
        part = index % block_heads
        pieces.append(mixed * attends[index // block_heads][1][:, part * rows : (part + 1) * rows])
    context = jnp.concatenate(pieces, axis=0).astype(BF16).T
    after_time = initial + matmul(context, temporal_out_ref[...])
    second = layer_norm(after_time, as_row(hidden_gain_ref)).astype(BF16)
    hidden = jax.nn.gelu(matmul(second, hidden_in_ref[...])).astype(BF16)
    result = (after_time + matmul(hidden, hidden_out_ref[...])).astype(BF16).astype(F32)
    headed = layer_norm(result, as_row(head_gain_ref)).astype(BF16)
    branch_velocity = matmul(headed, head_out_ref[...]).reshape(rows // period, period, width)
    conditional = branch_velocity[:, :share]
    empty = branch_velocity[:, share:]
    out_ref[...] = (empty + GUIDE * (conditional - empty)).astype(BF16)


def whole(memory_space=pltpu.VMEM):
    return pl.BlockSpec(memory_space=memory_space)


def body(
    groups,
    x_state,
    noise_field,
    rotations,
    translations,
    residue_types,
    pocket_mask,
    type_table,
    null_embed,
    spatial_gain,
    spatial_proj,
    spatial_points,
    spatial_gamma,
    spatial_out,
    temporal_gain,
    temporal_proj,
    temporal_out,
    hidden_gain,
    hidden_in,
    hidden_out,
    head_gain,
    head_out,
):
    frames, residues, width = x_state.shape
    share = residues // groups
    period = BRANCHES * share
    sources = (
        x_state,
        type_table,
        residue_types[None],
        null_embed,
        spatial_gain,
        rotations,
        translations,
        pocket_mask[None],
        spatial_proj,
        spatial_out,
        spatial_points.T,
    )
    slots = 2 * (width // LANES)
    later = (temporal_proj, temporal_out, hidden_in, hidden_out, head_out)
    spatial, *later = pl.pallas_call(
        functools.partial(spatial_kernel, groups),
        out_shape=[pltpu.VMEM((groups, frames * period, width), BF16)]
        + [pltpu.VMEM(array.shape, array.dtype) for array in later],
        in_specs=[whole(pltpu.SMEM)] + [whole(pl.ANY)] * (len(sources) + len(later)),
        out_specs=[whole()] * (1 + len(later)),
        scratch_shapes=[pltpu.VMEM(array.shape, array.dtype) for array in sources[:-1]]
        + [
            pltpu.VMEM((slots * SLOT, width), BF16),
            pltpu.VMEM((16, residues), F32),
            pltpu.SemaphoreType.DMA((len(sources) - 1 + slots + len(later),)),
        ],
        compiler_params=pltpu.CompilerParams(vmem_limit_bytes=SPATIAL_VMEM),
        name="spatial",
    )(spatial_gamma, *sources, *later)
    arrived = lax.all_to_all(spatial, "seq", split_axis=0, concat_axis=0, tiled=True)
    proj_local, out_local, in_local, hidden_local, head_local = later
    guided = pl.pallas_call(
        functools.partial(temporal_kernel, period),
        out_shape=pltpu.VMEM((groups * frames, share, width), BF16),
        in_specs=[whole()] * 9,
        out_specs=whole(),
        compiler_params=pltpu.CompilerParams(vmem_limit_bytes=TEMPORAL_VMEM),
        name="temporal",
    )(
        arrived,
        temporal_gain,
        proj_local,
        out_local,
        hidden_gain,
        in_local,
        hidden_local,
        head_gain,
        head_local,
    )
    velocity = lax.all_to_all(guided, "seq", split_axis=0, concat_axis=1, tiled=True)
    x_next = (
        x_state.astype(F32)
        + STEP_SIZE * velocity.astype(F32)
        + NOISE_SCALE * noise_field.astype(F32)
    ).astype(BF16)
    return (x_next, velocity)


def solution(mesh):
    tokens = P(("parts", "seq"), None, None)
    geometry = P(None, ("parts", "seq"), None)
    return jax.shard_map(
        functools.partial(body, mesh.shape["seq"]),
        mesh=mesh,
        in_specs=(tokens, tokens, geometry, geometry, P("parts"), P("parts")) + (P(),) * 15,
        out_specs=(tokens, tokens),
        check_vma=False,
    )
```

```python
import functools
import math

import jax
import jax.numpy as jnp
from jax import lax
from jax.experimental import pallas as pl
from jax.experimental.pallas import tpu as pltpu
from jax.sharding import PartitionSpec as P

THEADS = 6
BRANCHES = 2

WEIGHT_LOGIT = 0.7071067811865476
WEIGHT_POINT = 0.23570226039551584
GUIDE = 2.0
STEP_SIZE = 0.25
NOISE_SCALE = 0.2
EPSILON = 1e-05

BF16 = jnp.bfloat16
F32 = jnp.float32
LANES = 128
SLOT = 64
SPATIAL_VMEM = 56 * 2**20
TEMPORAL_VMEM = 40 * 2**20
NT = (((1,), (1,)), ((), ()))


def layer_norm(values, scale_gain):
    average = jnp.mean(values, axis=-1, keepdims=True)
    centered = values - average
    spread = jnp.mean(centered * centered, axis=-1, keepdims=True)
    return centered * lax.rsqrt(spread + EPSILON) * scale_gain


def as_row(ref):
    return ref[...].reshape(1, ref.shape[0])


def matmul(left, right):
    return jnp.dot(left, right, preferred_element_type=F32)


def iota(shape, axis):
    return lax.broadcasted_iota(jnp.int32, shape, axis)


def softmax_down(logits, allowed):
    logits = jnp.where(allowed, logits, -jnp.inf)
    powers = jnp.exp(logits - jnp.max(logits, axis=0, keepdims=True))
    return powers.astype(BF16), 1.0 / jnp.sum(powers, axis=0, keepdims=True)


def spatial_kernel(groups, gamma_ref, *refs):
    sources, refs = refs[:11], refs[11:]
    later, refs = refs[:3], refs[3:]
    out_ref, later_out, refs = refs[0], refs[1:4], refs[4:]
    local, (columns_ref, sems) = refs[:11], refs[11:]
    (
        x_ref,
        table_ref,
        types_ref,
        null_ref,
        gain_ref,
        rotation_ref,
        translation_ref,
        mask_ref,
        proj_ref,
        spatial_out_ref,
        points_ref,
    ) = local
    frames, residues, width = x_ref.shape
    heads = gamma_ref.shape[0]
    head_dim = width // heads
    blocks = width // LANES
    block_heads = LANES // head_dim
    slot_rows = sources[-1].shape[0] // (2 * blocks)
    per_head = slot_rows // block_heads
    share = residues // groups
    fold = max(residues, LANES)
    stacked_rows = block_heads * residues
    point_scale = 0.5 * WEIGHT_LOGIT * WEIGHT_POINT

    pairs = list(zip(sources[:8], local[:8], strict=True))
    for slot in range(2 * blocks):
        pairs.append(
            (
                sources[-1].at[pl.ds(slot * slot_rows, slot_rows), :],
                points_ref.at[pl.ds(slot * SLOT, slot_rows), :],
            )
        )
    pairs += list(zip(sources[8:10] + later, local[8:10] + tuple(later_out), strict=True))
    copies = [
        pltpu.make_async_copy(source, target, sems.at[index])
        for index, (source, target) in enumerate(pairs)
    ]
    first = 10 + 2 * blocks
    for copy in copies[:first]:
        copy.start()
    small, wide, after = copies[:8], copies[8 : first - 1], copies[first - 1]

    for slot in range(2 * blocks):
        points_ref[slot * SLOT + slot_rows : (slot + 1) * SLOT, :] = jnp.zeros(
            (SLOT - slot_rows, width), BF16
        )
    lane = iota((1, LANES), 1)
    low = lane < SLOT
    place = lane % SLOT
    component = jnp.where(place < slot_rows, place % 3, 3)
    member, block_member = [], []
    for part in range(block_heads):
        member.append((place >= part * per_head) & (place < (part + 1) * per_head))
        block_member.append((lane >= part * head_dim) & (lane < (part + 1) * head_dim))
    head_lanes = [own.astype(F32).astype(BF16) for own in block_member]
    point_lanes = [
        jnp.concatenate([own, own], axis=1).astype(F32).astype(BF16) for own in member
    ]
    gamma_lanes = []
    for block in range(blocks):
        gamma = jnp.zeros((1, LANES), F32)
        for part in range(block_heads):
            gamma = jnp.where(member[part], gamma_ref[block * block_heads + part], gamma)
        gamma_lanes.append(gamma * point_scale)
    chunks = stacked_rows // fold
    chunk_rows = LANES // chunks
    diagonal = iota((chunk_rows, fold), 0) // head_dim == iota((chunk_rows, fold), 1) // residues
    same = iota((residues, stacked_rows), 0) == iota((residues, stacked_rows), 1) % residues
    columns_ref[...] = jnp.zeros_like(columns_ref)

    for copy in small:
        copy.wait()
    for copy in copies[first:]:
        copy.start()
    kinds = table_ref.shape[0]
    onehot = (iota((kinds, residues), 0) == types_ref[...]).astype(F32).T.astype(BF16)
    conditional = matmul(onehot, table_ref[...])
    empty = as_row(null_ref).astype(F32)

    tiles = []
    for frame in range(frames):
        state = x_ref[frame].astype(F32)
        initial = jnp.concatenate([state + conditional, state + empty], axis=0)
        normed = layer_norm(initial, as_row(gain_ref)).astype(BF16)

        columns_ref[0:9, :] = rotation_ref[:, frame, :]
        moved = translation_ref[:, frame, :]
        columns_ref[9:12, :] = moved - jnp.mean(moved, axis=1, keepdims=True)
        columns_ref[12:13, :] = mask_ref[...].astype(F32)
        columns = columns_ref[...].T
        allowed = (columns[:, 12:13] == 1.0) | same
        factors = []
        for step in range(-2, 3):
            factor = jnp.zeros((residues, LANES), F32)
            for row in range(3):
                if 0 <= row + step < 3:
                    entry = 3 * row + row + step
                    factor = jnp.where(component == row, columns[:, entry : entry + 1], factor)
            factors.append(jnp.concatenate([factor] * BRANCHES, axis=0))
        anchor = jnp.zeros((residues, LANES), F32)
        for row in range(3):
            anchor = jnp.where(component == row, columns[:, 9 + row : 10 + row], anchor)
        anchor = jnp.concatenate([anchor] * BRANCHES, axis=0)

        if frame == 0:
            for copy in wide:
                copy.wait()
        points = lax.dot_general(normed, points_ref[...], NT, preferred_element_type=F32)
        projected = matmul(normed, proj_ref[...])

        queries = (
            projected[:, :width].astype(BF16) * jnp.asarray(WEIGHT_LOGIT / math.sqrt(head_dim), BF16)
        )
        keys = projected[:, width : 2 * width].astype(BF16)
        values = projected[:, 2 * width :].astype(BF16)
        turned, scalar = [], []
        for branch in range(BRANCHES):
            rows = slice(branch * residues, (branch + 1) * residues)
            turned.append(values[rows].T)
            for start in range(0, width, LANES):
                lanes = slice(start, start + LANES)
                right = jnp.concatenate([queries[rows, lanes] * own for own in head_lanes], axis=0)
                scalar.append(
                    lax.dot_general(keys[rows, lanes], right, NT, preferred_element_type=F32)
                )

        slots = []
        for pair in range(blocks):
            lanes = points[:, pair * LANES : (pair + 1) * LANES]
            placed = anchor + factors[2] * lanes
            for step in (-2, -1, 1, 2):
                placed = placed + factors[step + 2] * pltpu.roll(lanes, (-step) % LANES, 1)
            swapped = pltpu.roll(placed, SLOT, 1)
            slots += [jnp.where(low, placed, swapped), jnp.where(low, swapped, placed)]

        query_feature, key_first, key_second = [], [], []
        nothing = jnp.zeros((BRANCHES * residues, LANES), BF16)
        ones = jnp.ones((residues, LANES), BF16)
        for block in range(blocks):
            feature = slots[block] * (2.0 * gamma_lanes[block])
            high = feature.astype(BF16)
            rest = (feature - high.astype(F32)).astype(BF16)
            query_feature.append(jnp.where(low, high, rest))

            feature = slots[blocks + block]
            high = feature.astype(BF16)
            rest = (feature - high.astype(F32)).astype(BF16)
            key_first.append([high])
            key_second.append([jnp.where(low, rest, nothing)])
            square = feature * feature * (-gamma_lanes[block])
            high = square.astype(BF16)
            rest = square - high.astype(F32)
            middle = rest.astype(BF16)
            last = (rest - middle.astype(F32)).astype(BF16)
            key_first[block].append(jnp.where(low, high, middle))
            key_second[block].append(jnp.where(low, last, nothing))

        logits = []
        for branch in range(BRANCHES):
            rows = slice(branch * residues, (branch + 1) * residues)
            for block in range(blocks):
                left = jnp.concatenate(
                    [
                        jnp.concatenate([piece[rows] for piece in pieces[block]], axis=1)
                        for pieces in (key_first, key_second)
                    ],
                    axis=0,
                )
                right = jnp.concatenate([query_feature[block][rows], ones], axis=1)
                right = jnp.concatenate([right * own for own in point_lanes], axis=0)
                both = lax.dot_general(left, right, NT, preferred_element_type=F32)
                logits.append(scalar[len(logits)] + both[:residues] + both[residues:])
        attends = [softmax_down(each, allowed) for each in logits]
        mixes = []
        for index, (powers, _) in enumerate(attends):
            block = index % blocks
            for chunk in range(chunks):
                start = block * LANES + chunk * chunk_rows
                mixes.append(
                    matmul(
                        turned[index // blocks][start : start + chunk_rows],
                        powers[:, chunk * fold : (chunk + 1) * fold],
                    )
                )
        contexts = []
        for branch in range(BRANCHES):
            pieces = []
            for index in range(branch * blocks, (branch + 1) * blocks):
                scale = attends[index][1]
                for chunk in range(chunks):
                    mixed = mixes[index * chunks + chunk]
                    mixed = mixed * scale[:, chunk * fold : (chunk + 1) * fold]
                    pieces.append(jnp.where(diagonal, mixed, 0.0))
            context = jnp.concatenate(pieces, axis=0).astype(BF16).T
            joined = context[:residues]
            for start in range(residues, fold, residues):
                joined = joined + context[start : start + residues]
            contexts.append(joined)
        if frame == 0:
            after.wait()
        update = matmul(jnp.concatenate(contexts, axis=0), spatial_out_ref[...])
        total = initial + update
        tiles.append(
            [
                jnp.concatenate(
                    [
                        total[start : start + share]
                        for start in range(group * share, BRANCHES * residues, residues)
                    ],
                    axis=0,
                )
                for group in range(groups)
            ]
        )
    for group in range(groups):
        out_ref[group] = jnp.concatenate([tile[group] for tile in tiles], axis=0).astype(BF16)
    for copy in copies[first:]:
        copy.wait()


def temporal_kernel(
    period,
    x_ref,
    gain_ref,
    proj_ref,
    temporal_out_ref,
    hidden_gain_ref,
    hidden_in_ref,
    hidden_source,
    head_gain_ref,
    head_source,
    out_ref,
    hidden_out_ref,
    head_out_ref,
    sems,
):
    copies = [
        pltpu.make_async_copy(hidden_source, hidden_out_ref, sems.at[0]),
        pltpu.make_async_copy(head_source, head_out_ref, sems.at[1]),
    ]
    for copy in copies:
        copy.start()
    groups, depth, width = x_ref.shape
    rows = groups * depth
    head_dim = width // THEADS
    block_heads = LANES // head_dim
    share = period // BRANCHES

    initial = x_ref[...].astype(F32).reshape(rows, width)
    normed = layer_norm(initial, as_row(gain_ref)).astype(BF16)
    projected = matmul(normed, proj_ref[...])
    queries = projected[:, :width].astype(BF16) * jnp.asarray(1.0 / math.sqrt(head_dim), BF16)
    keys = projected[:, width : 2 * width].astype(BF16)
    turned = projected[:, 2 * width :].astype(BF16).T
    block_lane = iota((1, LANES), 1)
    allowed = (
        iota((rows, block_heads * rows), 0) % period == iota((rows, block_heads * rows), 1) % period
    )
    logits = []
    for block in range(width // LANES):
        lanes = slice(block * LANES, (block + 1) * LANES)
        stacked = []
        for part in range(block_heads):
            own = (block_lane >= part * head_dim) & (block_lane < (part + 1) * head_dim)
            stacked.append(queries[:, lanes] * own.astype(F32).astype(BF16))
        logits.append(
            lax.dot_general(
                keys[:, lanes], jnp.concatenate(stacked, axis=0), NT, preferred_element_type=F32
            )
        )
    attends = [softmax_down(each, allowed) for each in logits]
    mixes = []
    for block, (powers, _) in enumerate(attends):
        for part in range(block_heads):
            start = block * LANES + part * head_dim
            lanes = slice(part * rows, (part + 1) * rows)
            mixes.append(matmul(turned[start : start + head_dim], powers[:, lanes]))
    pieces = []
    for index, mixed in enumerate(mixes):
        part = index % block_heads
        pieces.append(mixed * attends[index // block_heads][1][:, part * rows : (part + 1) * rows])
    context = jnp.concatenate(pieces, axis=0).astype(BF16).T
    after_time = initial + matmul(context, temporal_out_ref[...])
    for copy in copies:
        copy.wait()
    second = layer_norm(after_time, as_row(hidden_gain_ref)).astype(BF16)
    hidden = jax.nn.gelu(matmul(second, hidden_in_ref[...])).astype(BF16)
    result = (after_time + matmul(hidden, hidden_out_ref[...])).astype(BF16).astype(F32)
    headed = layer_norm(result, as_row(head_gain_ref)).astype(BF16)
    branch_velocity = matmul(headed, head_out_ref[...]).reshape(rows // period, period, width)
    conditional = branch_velocity[:, :share]
    empty = branch_velocity[:, share:]
    out_ref[...] = (empty + GUIDE * (conditional - empty)).astype(BF16)


def whole(memory_space=pltpu.VMEM):
    return pl.BlockSpec(memory_space=memory_space)


def body(
    groups,
    x_state,
    noise_field,
    rotations,
    translations,
    residue_types,
    pocket_mask,
    type_table,
    null_embed,
    spatial_gain,
    spatial_proj,
    spatial_points,
    spatial_gamma,
    spatial_out,
    temporal_gain,
    temporal_proj,
    temporal_out,
    hidden_gain,
    hidden_in,
    hidden_out,
    head_gain,
    head_out,
):
    frames, residues, width = x_state.shape
    share = residues // groups
    period = BRANCHES * share
    sources = (
        x_state,
        type_table,
        residue_types[None],
        null_embed,
        spatial_gain,
        rotations,
        translations,
        pocket_mask[None],
        spatial_proj,
        spatial_out,
        spatial_points.T,
    )
    slots = 2 * (width // LANES)
    later = (temporal_proj, temporal_out, hidden_in)
    spatial, *later = pl.pallas_call(
        functools.partial(spatial_kernel, groups),
        out_shape=[pltpu.VMEM((groups, frames * period, width), BF16)]
        + [pltpu.VMEM(array.shape, array.dtype) for array in later],
        in_specs=[whole(pltpu.SMEM)] + [whole(pl.ANY)] * (len(sources) + len(later)),
        out_specs=[whole()] * (1 + len(later)),
        scratch_shapes=[pltpu.VMEM(array.shape, array.dtype) for array in sources[:-1]]
        + [
            pltpu.VMEM((slots * SLOT, width), BF16),
            pltpu.VMEM((16, residues), F32),
            pltpu.SemaphoreType.DMA((len(sources) - 1 + slots + len(later),)),
        ],
        compiler_params=pltpu.CompilerParams(vmem_limit_bytes=SPATIAL_VMEM),
        name="spatial",
    )(spatial_gamma, *sources, *later)
    arrived = lax.all_to_all(spatial, "seq", split_axis=0, concat_axis=0, tiled=True)
    proj_local, out_local, in_local = later
    guided = pl.pallas_call(
        functools.partial(temporal_kernel, period),
        out_shape=pltpu.VMEM((groups * frames, share, width), BF16),
        in_specs=[whole()] * 6 + [whole(pl.ANY), whole(), whole(pl.ANY)],
        out_specs=whole(),
        scratch_shapes=[
            pltpu.VMEM(hidden_out.shape, BF16),
            pltpu.VMEM(head_out.shape, BF16),
            pltpu.SemaphoreType.DMA((2,)),
        ],
        compiler_params=pltpu.CompilerParams(vmem_limit_bytes=TEMPORAL_VMEM),
        name="temporal",
    )(
        arrived,
        temporal_gain,
        proj_local,
        out_local,
        hidden_gain,
        in_local,
        hidden_out,
        head_gain,
        head_out,
    )
    velocity = lax.all_to_all(guided, "seq", split_axis=0, concat_axis=1, tiled=True)
    x_next = (
        x_state.astype(F32)
        + STEP_SIZE * velocity.astype(F32)
        + NOISE_SCALE * noise_field.astype(F32)
    ).astype(BF16)
    return (x_next, velocity)


def solution(mesh):
    tokens = P(("parts", "seq"), None, None)
    geometry = P(None, ("parts", "seq"), None)
    return jax.shard_map(
        functools.partial(body, mesh.shape["seq"]),
        mesh=mesh,
        in_specs=(tokens, tokens, geometry, geometry, P("parts"), P("parts")) + (P(),) * 15,
        out_specs=(tokens, tokens),
        check_vma=False,
    )
```

```python
import functools
import math

import jax
import jax.numpy as jnp
from jax import lax
from jax.experimental import pallas as pl
from jax.experimental.pallas import tpu as pltpu
from jax.sharding import PartitionSpec as P

THEADS = 6
BRANCHES = 2

WEIGHT_LOGIT = 0.7071067811865476
WEIGHT_POINT = 0.23570226039551584
GUIDE = 2.0
STEP_SIZE = 0.25
NOISE_SCALE = 0.2
EPSILON = 1e-05

BF16 = jnp.bfloat16
F32 = jnp.float32
LANES = 128
SLOT = 64
SPATIAL_VMEM = 56 * 2**20
TEMPORAL_VMEM = 40 * 2**20
NT = (((1,), (1,)), ((), ()))


def layer_norm(values, scale_gain):
    average = jnp.mean(values, axis=-1, keepdims=True)
    centered = values - average
    spread = jnp.mean(centered * centered, axis=-1, keepdims=True)
    return centered * lax.rsqrt(spread + EPSILON) * scale_gain


def as_row(ref):
    return ref[...].reshape(1, ref.shape[0])


def matmul(left, right):
    return jnp.dot(left, right, preferred_element_type=F32)


def iota(shape, axis):
    return lax.broadcasted_iota(jnp.int32, shape, axis)


def softmax_down(logits, allowed):
    logits = jnp.where(allowed, logits, -jnp.inf)
    powers = jnp.exp(logits - jnp.max(logits, axis=0, keepdims=True))
    return powers.astype(BF16), 1.0 / jnp.sum(powers, axis=0, keepdims=True)


def spatial_kernel(groups, gamma_ref, *refs):
    sources, refs = refs[:11], refs[11:]
    later, refs = refs[:5], refs[5:]
    out_ref, later_out, refs = refs[0], refs[1:6], refs[6:]
    local, (columns_ref, sems) = refs[:11], refs[11:]
    (
        x_ref,
        table_ref,
        types_ref,
        null_ref,
        gain_ref,
        rotation_ref,
        translation_ref,
        mask_ref,
        proj_ref,
        spatial_out_ref,
        points_ref,
    ) = local
    frames, residues, width = x_ref.shape
    heads = gamma_ref.shape[0]
    head_dim = width // heads
    blocks = width // LANES
    block_heads = LANES // head_dim
    slot_rows = sources[-1].shape[0] // (2 * blocks)
    per_head = slot_rows // block_heads
    share = residues // groups
    fold = max(residues, LANES)
    stacked_rows = block_heads * residues
    point_scale = 0.5 * WEIGHT_LOGIT * WEIGHT_POINT

    whole_pairs = list(zip(sources[:10], local[:10], strict=True))
    slot_pairs = [
        (
            sources[-1].at[pl.ds(slot * slot_rows, slot_rows), :],
            points_ref.at[pl.ds(slot * SLOT, slot_rows), :],
        )
        for slot in range(2 * blocks)
    ]
    stages = [
        [whole_pairs[2], whole_pairs[1]],
        [whole_pairs[0], whole_pairs[3], whole_pairs[4]],
        slot_pairs + [whole_pairs[8]] + whole_pairs[5:8],
        [whole_pairs[9]],
        list(zip(later, later_out, strict=True)),
    ]
    copies, index = [], 0
    for stage in stages:
        copies.append([])
        for source, target in stage:
            copies[-1].append(pltpu.make_async_copy(source, target, sems.at[index]))
            index += 1
    for_embed, for_norm, for_points, for_update, for_later = copies
    for copy in for_embed + for_norm + for_points + for_update:
        copy.start()

    for slot in range(2 * blocks):
        points_ref[slot * SLOT + slot_rows : (slot + 1) * SLOT, :] = jnp.zeros(
            (SLOT - slot_rows, width), BF16
        )
    lane = iota((1, LANES), 1)
    low = lane < SLOT
    place = lane % SLOT
    component = jnp.where(place < slot_rows, place % 3, 3)
    member, block_member = [], []
    for part in range(block_heads):
        member.append((place >= part * per_head) & (place < (part + 1) * per_head))
        block_member.append((lane >= part * head_dim) & (lane < (part + 1) * head_dim))
    head_lanes = [own.astype(F32).astype(BF16) for own in block_member]
    point_lanes = [
        jnp.concatenate([own, own], axis=1).astype(F32).astype(BF16) for own in member
    ]
    gamma_lanes = []
    for block in range(blocks):
        gamma = jnp.zeros((1, LANES), F32)
        for part in range(block_heads):
            gamma = jnp.where(member[part], gamma_ref[block * block_heads + part], gamma)
        gamma_lanes.append(gamma * point_scale)
    chunks = stacked_rows // fold
    chunk_rows = LANES // chunks
    diagonal = iota((chunk_rows, fold), 0) // head_dim == iota((chunk_rows, fold), 1) // residues
    same = iota((residues, stacked_rows), 0) == iota((residues, stacked_rows), 1) % residues
    columns_ref[...] = jnp.zeros_like(columns_ref)

    for copy in for_embed:
        copy.wait()
    kinds = table_ref.shape[0]
    onehot = (iota((kinds, residues), 0) == types_ref[...]).astype(F32).T.astype(BF16)
    conditional = matmul(onehot, table_ref[...])
    for copy in for_norm:
        copy.wait()
    for copy in for_later:
        copy.start()
    empty = as_row(null_ref).astype(F32)

    tiles = []
    for frame in range(frames):
        state = x_ref[frame].astype(F32)
        initial = jnp.concatenate([state + conditional, state + empty], axis=0)
        normed = layer_norm(initial, as_row(gain_ref)).astype(BF16)

        if frame == 0:
            for copy in for_points:
                copy.wait()
        points = lax.dot_general(normed, points_ref[...], NT, preferred_element_type=F32)
        projected = matmul(normed, proj_ref[...])
        columns_ref[0:9, :] = rotation_ref[:, frame, :]
        moved = translation_ref[:, frame, :]
        columns_ref[9:12, :] = moved - jnp.mean(moved, axis=1, keepdims=True)
        columns_ref[12:13, :] = mask_ref[...].astype(F32)
        columns = columns_ref[...].T
        allowed = (columns[:, 12:13] == 1.0) | same
        factors = []
        for step in range(-2, 3):
            factor = jnp.zeros((residues, LANES), F32)
            for row in range(3):
                if 0 <= row + step < 3:
                    entry = 3 * row + row + step
                    factor = jnp.where(component == row, columns[:, entry : entry + 1], factor)
            factors.append(jnp.concatenate([factor] * BRANCHES, axis=0))
        anchor = jnp.zeros((residues, LANES), F32)
        for row in range(3):
            anchor = jnp.where(component == row, columns[:, 9 + row : 10 + row], anchor)
        anchor = jnp.concatenate([anchor] * BRANCHES, axis=0)

        queries = (
            projected[:, :width].astype(BF16) * jnp.asarray(WEIGHT_LOGIT / math.sqrt(head_dim), BF16)
        )
        keys = projected[:, width : 2 * width].astype(BF16)
        values = projected[:, 2 * width :].astype(BF16)
        turned, scalar = [], []
        for branch in range(BRANCHES):
            rows = slice(branch * residues, (branch + 1) * residues)
            turned.append(values[rows].T)
            for start in range(0, width, LANES):
                lanes = slice(start, start + LANES)
                right = jnp.concatenate([queries[rows, lanes] * own for own in head_lanes], axis=0)
                scalar.append(
                    lax.dot_general(keys[rows, lanes], right, NT, preferred_element_type=F32)
                )

        slots = []
        for pair in range(blocks):
            lanes = points[:, pair * LANES : (pair + 1) * LANES]
            placed = anchor + factors[2] * lanes
            for step in (-2, -1, 1, 2):
                placed = placed + factors[step + 2] * pltpu.roll(lanes, (-step) % LANES, 1)
            swapped = pltpu.roll(placed, SLOT, 1)
            slots += [jnp.where(low, placed, swapped), jnp.where(low, swapped, placed)]

        query_feature, key_first, key_second = [], [], []
        nothing = jnp.zeros((BRANCHES * residues, LANES), BF16)
        ones = jnp.ones((residues, LANES), BF16)
        for block in range(blocks):
            feature = slots[block] * (2.0 * gamma_lanes[block])
            high = feature.astype(BF16)
            rest = (feature - high.astype(F32)).astype(BF16)
            query_feature.append(jnp.where(low, high, rest))

            feature = slots[blocks + block]
            high = feature.astype(BF16)
            rest = (feature - high.astype(F32)).astype(BF16)
            key_first.append([high])
            key_second.append([jnp.where(low, rest, nothing)])
            square = feature * feature * (-gamma_lanes[block])
            high = square.astype(BF16)
            rest = square - high.astype(F32)
            middle = rest.astype(BF16)
            last = (rest - middle.astype(F32)).astype(BF16)
            key_first[block].append(jnp.where(low, high, middle))
            key_second[block].append(jnp.where(low, last, nothing))

        logits = []
        for branch in range(BRANCHES):
            rows = slice(branch * residues, (branch + 1) * residues)
            for block in range(blocks):
                left = jnp.concatenate(
                    [
                        jnp.concatenate([piece[rows] for piece in pieces[block]], axis=1)
                        for pieces in (key_first, key_second)
                    ],
                    axis=0,
                )
                right = jnp.concatenate([query_feature[block][rows], ones], axis=1)
                right = jnp.concatenate([right * own for own in point_lanes], axis=0)
                both = lax.dot_general(left, right, NT, preferred_element_type=F32)
                logits.append(scalar[len(logits)] + both[:residues] + both[residues:])
        attends = [softmax_down(each, allowed) for each in logits]
        mixes = []
        for index, (powers, _) in enumerate(attends):
            block = index % blocks
            for chunk in range(chunks):
                start = block * LANES + chunk * chunk_rows
                mixes.append(
                    matmul(
                        turned[index // blocks][start : start + chunk_rows],
                        powers[:, chunk * fold : (chunk + 1) * fold],
                    )
                )
        contexts = []
        for branch in range(BRANCHES):
            pieces = []
            for index in range(branch * blocks, (branch + 1) * blocks):
                scale = attends[index][1]
                for chunk in range(chunks):
                    mixed = mixes[index * chunks + chunk]
                    mixed = mixed * scale[:, chunk * fold : (chunk + 1) * fold]
                    pieces.append(jnp.where(diagonal, mixed, 0.0))
            context = jnp.concatenate(pieces, axis=0).astype(BF16).T
            joined = context[:residues]
            for start in range(residues, fold, residues):
                joined = joined + context[start : start + residues]
            contexts.append(joined)
        if frame == 0:
            for copy in for_update:
                copy.wait()
        update = matmul(jnp.concatenate(contexts, axis=0), spatial_out_ref[...])
        total = initial + update
        tiles.append(
            [
                jnp.concatenate(
                    [
                        total[start : start + share]
                        for start in range(group * share, BRANCHES * residues, residues)
                    ],
                    axis=0,
                )
                for group in range(groups)
            ]
        )
    for group in range(groups):
        out_ref[group] = jnp.concatenate([tile[group] for tile in tiles], axis=0).astype(BF16)
    for copy in for_later:
        copy.wait()


def temporal_kernel(
    period,
    x_ref,
    gain_ref,
    proj_ref,
    temporal_out_ref,
    hidden_gain_ref,
    hidden_in_ref,
    hidden_out_ref,
    head_gain_ref,
    head_out_ref,
    out_ref,
):
    groups, depth, width = x_ref.shape
    rows = groups * depth
    head_dim = width // THEADS
    block_heads = LANES // head_dim
    share = period // BRANCHES

    initial = x_ref[...].astype(F32).reshape(rows, width)
    normed = layer_norm(initial, as_row(gain_ref)).astype(BF16)
    projected = matmul(normed, proj_ref[...])
    queries = projected[:, :width].astype(BF16) * jnp.asarray(1.0 / math.sqrt(head_dim), BF16)
    keys = projected[:, width : 2 * width].astype(BF16)
    turned = projected[:, 2 * width :].astype(BF16).T
    block_lane = iota((1, LANES), 1)
    allowed = (
        iota((rows, block_heads * rows), 0) % period == iota((rows, block_heads * rows), 1) % period
    )
    logits = []
    for block in range(width // LANES):
        lanes = slice(block * LANES, (block + 1) * LANES)
        stacked = []
        for part in range(block_heads):
            own = (block_lane >= part * head_dim) & (block_lane < (part + 1) * head_dim)
            stacked.append(queries[:, lanes] * own.astype(F32).astype(BF16))
        logits.append(
            lax.dot_general(
                keys[:, lanes], jnp.concatenate(stacked, axis=0), NT, preferred_element_type=F32
            )
        )
    attends = [softmax_down(each, allowed) for each in logits]
    mixes = []
    for block, (powers, _) in enumerate(attends):
        for part in range(block_heads):
            start = block * LANES + part * head_dim
            lanes = slice(part * rows, (part + 1) * rows)
            mixes.append(matmul(turned[start : start + head_dim], powers[:, lanes]))
    pieces = []
    for index, mixed in enumerate(mixes):
        part = index % block_heads
        pieces.append(mixed * attends[index // block_heads][1][:, part * rows : (part + 1) * rows])
    context = jnp.concatenate(pieces, axis=0).astype(BF16).T
    after_time = initial + matmul(context, temporal_out_ref[...])
    second = layer_norm(after_time, as_row(hidden_gain_ref)).astype(BF16)
    hidden = jax.nn.gelu(matmul(second, hidden_in_ref[...])).astype(BF16)
    result = (after_time + matmul(hidden, hidden_out_ref[...])).astype(BF16).astype(F32)
    headed = layer_norm(result, as_row(head_gain_ref)).astype(BF16)
    branch_velocity = matmul(headed, head_out_ref[...]).reshape(rows // period, period, width)
    conditional = branch_velocity[:, :share]
    empty = branch_velocity[:, share:]
    out_ref[...] = (empty + GUIDE * (conditional - empty)).astype(BF16)


def whole(memory_space=pltpu.VMEM):
    return pl.BlockSpec(memory_space=memory_space)


def body(
    groups,
    x_state,
    noise_field,
    rotations,
    translations,
    residue_types,
    pocket_mask,
    type_table,
    null_embed,
    spatial_gain,
    spatial_proj,
    spatial_points,
    spatial_gamma,
    spatial_out,
    temporal_gain,
    temporal_proj,
    temporal_out,
    hidden_gain,
    hidden_in,
    hidden_out,
    head_gain,
    head_out,
):
    frames, residues, width = x_state.shape
    share = residues // groups
    period = BRANCHES * share
    sources = (
        x_state,
        type_table,
        residue_types[None],
        null_embed,
        spatial_gain,
        rotations,
        translations,
        pocket_mask[None],
        spatial_proj,
        spatial_out,
        spatial_points.T,
    )
    slots = 2 * (width // LANES)
    later = (temporal_proj, temporal_out, hidden_in, hidden_out, head_out)
    spatial, *later = pl.pallas_call(
        functools.partial(spatial_kernel, groups),
        out_shape=[pltpu.VMEM((groups, frames * period, width), BF16)]
        + [pltpu.VMEM(array.shape, array.dtype) for array in later],
        in_specs=[whole(pltpu.SMEM)] + [whole(pl.ANY)] * (len(sources) + len(later)),
        out_specs=[whole()] * (1 + len(later)),
        scratch_shapes=[pltpu.VMEM(array.shape, array.dtype) for array in sources[:-1]]
        + [
            pltpu.VMEM((slots * SLOT, width), BF16),
            pltpu.VMEM((16, residues), F32),
            pltpu.SemaphoreType.DMA((len(sources) - 1 + slots + len(later),)),
        ],
        compiler_params=pltpu.CompilerParams(vmem_limit_bytes=SPATIAL_VMEM),
        name="spatial",
    )(spatial_gamma, *sources, *later)
    arrived = lax.all_to_all(spatial, "seq", split_axis=0, concat_axis=0, tiled=True)
    proj_local, out_local, in_local, hidden_local, head_local = later
    guided = pl.pallas_call(
        functools.partial(temporal_kernel, period),
        out_shape=pltpu.VMEM((groups * frames, share, width), BF16),
        in_specs=[whole()] * 9,
        out_specs=whole(),
        compiler_params=pltpu.CompilerParams(vmem_limit_bytes=TEMPORAL_VMEM),
        name="temporal",
    )(
        arrived,
        temporal_gain,
        proj_local,
        out_local,
        hidden_gain,
        in_local,
        hidden_local,
        head_gain,
        head_local,
    )
    velocity = lax.all_to_all(guided, "seq", split_axis=0, concat_axis=1, tiled=True)
    x_next = (
        x_state.astype(F32)
        + STEP_SIZE * velocity.astype(F32)
        + NOISE_SCALE * noise_field.astype(F32)
    ).astype(BF16)
    return (x_next, velocity)


def solution(mesh):
    tokens = P(("parts", "seq"), None, None)
    geometry = P(None, ("parts", "seq"), None)
    return jax.shard_map(
        functools.partial(body, mesh.shape["seq"]),
        mesh=mesh,
        in_specs=(tokens, tokens, geometry, geometry, P("parts"), P("parts")) + (P(),) * 15,
        out_specs=(tokens, tokens),
        check_vma=False,
    )
```

```python
import functools
import math

import jax
import jax.numpy as jnp
from jax import lax
from jax.experimental import pallas as pl
from jax.experimental.pallas import tpu as pltpu
from jax.sharding import PartitionSpec as P

THEADS = 6
BRANCHES = 2

WEIGHT_LOGIT = 0.7071067811865476
WEIGHT_POINT = 0.23570226039551584
GUIDE = 2.0
STEP_SIZE = 0.25
NOISE_SCALE = 0.2
EPSILON = 1e-05

BF16 = jnp.bfloat16
F32 = jnp.float32
LANES = 128
SLOT = 64
SPATIAL_VMEM = 56 * 2**20
TEMPORAL_VMEM = 40 * 2**20
NT = (((1,), (1,)), ((), ()))


def layer_norm(values, scale_gain):
    average = jnp.mean(values, axis=-1, keepdims=True)
    centered = values - average
    spread = jnp.mean(centered * centered, axis=-1, keepdims=True)
    return centered * lax.rsqrt(spread + EPSILON) * scale_gain


def as_row(ref):
    return ref[...].reshape(1, ref.shape[0])


def matmul(left, right):
    return jnp.dot(left, right, preferred_element_type=F32)


def iota(shape, axis):
    return lax.broadcasted_iota(jnp.int32, shape, axis)


def softmax_down(logits, allowed):
    logits = jnp.where(allowed, logits, -jnp.inf)
    powers = jnp.exp(logits - jnp.max(logits, axis=0, keepdims=True))
    return powers.astype(BF16), 1.0 / jnp.sum(powers, axis=0, keepdims=True)


def spatial_kernel(groups, gamma_ref, *refs):
    sources, refs = refs[:11], refs[11:]
    later, refs = refs[:5], refs[5:]
    out_ref, later_out, refs = refs[0], refs[1:6], refs[6:]
    local, (columns_ref, sems) = refs[:11], refs[11:]
    (
        x_ref,
        table_ref,
        types_ref,
        null_ref,
        gain_ref,
        rotation_ref,
        translation_ref,
        mask_ref,
        proj_ref,
        spatial_out_ref,
        points_ref,
    ) = local
    frames, residues, width = x_ref.shape
    heads = gamma_ref.shape[0]
    head_dim = width // heads
    blocks = width // LANES
    block_heads = LANES // head_dim
    slot_rows = sources[-1].shape[0] // (2 * blocks)
    per_head = slot_rows // block_heads
    share = residues // groups
    fold = max(residues, LANES)
    stacked_rows = block_heads * residues
    point_scale = 0.5 * WEIGHT_LOGIT * WEIGHT_POINT

    pairs = list(zip(sources[:10], local[:10], strict=True))
    for slot in range(2 * blocks):
        pairs.append(
            (
                sources[-1].at[pl.ds(slot * slot_rows, slot_rows), :],
                points_ref.at[pl.ds(slot * SLOT, slot_rows), :],
            )
        )
    pairs += list(zip(later, later_out, strict=True))
    copies = [
        pltpu.make_async_copy(source, target, sems.at[index])
        for index, (source, target) in enumerate(pairs)
    ]
    first = 10 + 2 * blocks
    for copy in copies[:first]:
        copy.start()
    small, wide = copies[:8], copies[8:first]

    for slot in range(2 * blocks):
        points_ref[slot * SLOT + slot_rows : (slot + 1) * SLOT, :] = jnp.zeros(
            (SLOT - slot_rows, width), BF16
        )
    lane = iota((1, LANES), 1)
    low = lane < SLOT
    place = lane % SLOT
    component = jnp.where(place < slot_rows, place % 3, 3)
    member, block_member = [], []
    for part in range(block_heads):
        member.append((place >= part * per_head) & (place < (part + 1) * per_head))
        block_member.append((lane >= part * head_dim) & (lane < (part + 1) * head_dim))
    both_member = [
        jnp.concatenate([left, right, right], axis=1).astype(F32).astype(BF16)
        for left, right in zip(block_member, member, strict=True)
    ]
    gamma_lanes = []
    for block in range(blocks):
        gamma = jnp.zeros((1, LANES), F32)
        for part in range(block_heads):
            gamma = jnp.where(member[part], gamma_ref[block * block_heads + part], gamma)
        gamma_lanes.append(gamma * point_scale)
    chunks = stacked_rows // fold
    chunk_rows = LANES // chunks
    diagonal = iota((chunk_rows, fold), 0) // head_dim == iota((chunk_rows, fold), 1) // residues
    same = iota((residues, stacked_rows), 0) == iota((residues, stacked_rows), 1) % residues
    columns_ref[...] = jnp.zeros_like(columns_ref)

    for copy in small:
        copy.wait()
    for copy in copies[first:]:
        copy.start()
    kinds = table_ref.shape[0]
    onehot = (iota((kinds, residues), 0) == types_ref[...]).astype(F32).T.astype(BF16)
    conditional = matmul(onehot, table_ref[...])
    empty = as_row(null_ref).astype(F32)

    tiles = []
    for frame in range(frames):
        state = x_ref[frame].astype(F32)
        initial = jnp.concatenate([state + conditional, state + empty], axis=0)
        normed = layer_norm(initial, as_row(gain_ref)).astype(BF16)

        columns_ref[0:9, :] = rotation_ref[:, frame, :]
        moved = translation_ref[:, frame, :]
        columns_ref[9:12, :] = moved - jnp.mean(moved, axis=1, keepdims=True)
        columns_ref[12:13, :] = mask_ref[...].astype(F32)
        columns = columns_ref[...].T
        allowed = (columns[:, 12:13] == 1.0) | same
        factors = []
        for step in range(-2, 3):
            factor = jnp.zeros((residues, LANES), F32)
            for row in range(3):
                if 0 <= row + step < 3:
                    entry = 3 * row + row + step
                    factor = jnp.where(component == row, columns[:, entry : entry + 1], factor)
            factors.append(jnp.concatenate([factor] * BRANCHES, axis=0))
        anchor = jnp.zeros((residues, LANES), F32)
        for row in range(3):
            anchor = jnp.where(component == row, columns[:, 9 + row : 10 + row], anchor)
        anchor = jnp.concatenate([anchor] * BRANCHES, axis=0)

        if frame == 0:
            for copy in wide:
                copy.wait()
        points = lax.dot_general(normed, points_ref[...], NT, preferred_element_type=F32)
        projected = matmul(normed, proj_ref[...])

        slots = []
        for pair in range(blocks):
            lanes = points[:, pair * LANES : (pair + 1) * LANES]
            placed = anchor + factors[2] * lanes
            for step in (-2, -1, 1, 2):
                placed = placed + factors[step + 2] * pltpu.roll(lanes, (-step) % LANES, 1)
            swapped = pltpu.roll(placed, SLOT, 1)
            slots += [jnp.where(low, placed, swapped), jnp.where(low, swapped, placed)]

        query_feature, key_first, key_second = [], [], []
        nothing = jnp.zeros((BRANCHES * residues, LANES), BF16)
        ones = jnp.ones((residues, LANES), BF16)
        for block in range(blocks):
            feature = slots[block] * (2.0 * gamma_lanes[block])
            high = feature.astype(BF16)
            rest = (feature - high.astype(F32)).astype(BF16)
            query_feature.append(jnp.where(low, high, rest))

            feature = slots[blocks + block]
            high = feature.astype(BF16)
            rest = (feature - high.astype(F32)).astype(BF16)
            key_first.append([high])
            key_second.append([jnp.where(low, rest, nothing)])
            square = feature * feature * (-gamma_lanes[block])
            high = square.astype(BF16)
            rest = square - high.astype(F32)
            middle = rest.astype(BF16)
            last = (rest - middle.astype(F32)).astype(BF16)
            key_first[block].append(jnp.where(low, high, middle))
            key_second[block].append(jnp.where(low, last, nothing))

        queries = (
            projected[:, :width].astype(BF16) * jnp.asarray(WEIGHT_LOGIT / math.sqrt(head_dim), BF16)
        )
        keys = projected[:, width : 2 * width].astype(BF16)
        values = projected[:, 2 * width :].astype(BF16)
        turned, logits = [], []
        for branch in range(BRANCHES):
            rows = slice(branch * residues, (branch + 1) * residues)
            turned.append(values[rows].T)
            for block in range(blocks):
                lanes = slice(block * LANES, (block + 1) * LANES)
                left = jnp.concatenate(
                    [
                        jnp.concatenate(
                            [piece[rows] for piece in (keys[:, lanes], *key_first[block])], axis=1
                        ),
                        jnp.concatenate(
                            [piece[rows] for piece in (nothing, *key_second[block])], axis=1
                        ),
                    ],
                    axis=0,
                )
                right = jnp.concatenate(
                    [queries[rows, lanes], query_feature[block][rows], ones], axis=1
                )
                right = jnp.concatenate([right * own for own in both_member], axis=0)
                both = lax.dot_general(left, right, NT, preferred_element_type=F32)
                logits.append(both[:residues] + both[residues:])
        attends = [softmax_down(each, allowed) for each in logits]
        mixes = []
        for index, (powers, _) in enumerate(attends):
            block = index % blocks
            for chunk in range(chunks):
                start = block * LANES + chunk * chunk_rows
                mixes.append(
                    matmul(
                        turned[index // blocks][start : start + chunk_rows],
                        powers[:, chunk * fold : (chunk + 1) * fold],
                    )
                )
        contexts = []
        for branch in range(BRANCHES):
            pieces = []
            for index in range(branch * blocks, (branch + 1) * blocks):
                scale = attends[index][1]
                for chunk in range(chunks):
                    mixed = mixes[index * chunks + chunk]
                    mixed = mixed * scale[:, chunk * fold : (chunk + 1) * fold]
                    pieces.append(jnp.where(diagonal, mixed, 0.0))
            context = jnp.concatenate(pieces, axis=0).astype(BF16).T
            joined = context[:residues]
            for start in range(residues, fold, residues):
                joined = joined + context[start : start + residues]
            contexts.append(joined)
        update = matmul(jnp.concatenate(contexts, axis=0), spatial_out_ref[...])
        total = initial + update
        tiles.append(
            [
                jnp.concatenate(
                    [
                        total[start : start + share]
                        for start in range(group * share, BRANCHES * residues, residues)
                    ],
                    axis=0,
                )
                for group in range(groups)
            ]
        )
    for group in range(groups):
        out_ref[group] = jnp.concatenate([tile[group] for tile in tiles], axis=0).astype(BF16)
    for copy in copies[first:]:
        copy.wait()


def temporal_kernel(
    period,
    x_ref,
    gain_ref,
    proj_ref,
    temporal_out_ref,
    hidden_gain_ref,
    hidden_in_ref,
    hidden_out_ref,
    head_gain_ref,
    head_out_ref,
    out_ref,
):
    groups, depth, width = x_ref.shape
    rows = groups * depth
    head_dim = width // THEADS
    block_heads = LANES // head_dim
    share = period // BRANCHES

    initial = x_ref[...].astype(F32).reshape(rows, width)
    normed = layer_norm(initial, as_row(gain_ref)).astype(BF16)
    projected = matmul(normed, proj_ref[...])
    queries = projected[:, :width].astype(BF16) * jnp.asarray(1.0 / math.sqrt(head_dim), BF16)
    keys = projected[:, width : 2 * width].astype(BF16)
    turned = projected[:, 2 * width :].astype(BF16).T
    block_lane = iota((1, LANES), 1)
    allowed = (
        iota((rows, block_heads * rows), 0) % period == iota((rows, block_heads * rows), 1) % period
    )
    logits = []
    for block in range(width // LANES):
        lanes = slice(block * LANES, (block + 1) * LANES)
        stacked = []
        for part in range(block_heads):
            own = (block_lane >= part * head_dim) & (block_lane < (part + 1) * head_dim)
            stacked.append(queries[:, lanes] * own.astype(F32).astype(BF16))
        logits.append(
            lax.dot_general(
                keys[:, lanes], jnp.concatenate(stacked, axis=0), NT, preferred_element_type=F32
            )
        )
    attends = [softmax_down(each, allowed) for each in logits]
    mixes = []
    for block, (powers, _) in enumerate(attends):
        for part in range(block_heads):
            start = block * LANES + part * head_dim
            lanes = slice(part * rows, (part + 1) * rows)
            mixes.append(matmul(turned[start : start + head_dim], powers[:, lanes]))
    pieces = []
    for index, mixed in enumerate(mixes):
        part = index % block_heads
        pieces.append(mixed * attends[index // block_heads][1][:, part * rows : (part + 1) * rows])
    context = jnp.concatenate(pieces, axis=0).astype(BF16).T
    after_time = initial + matmul(context, temporal_out_ref[...])
    second = layer_norm(after_time, as_row(hidden_gain_ref)).astype(BF16)
    hidden = jax.nn.gelu(matmul(second, hidden_in_ref[...])).astype(BF16)
    result = (after_time + matmul(hidden, hidden_out_ref[...])).astype(BF16).astype(F32)
    headed = layer_norm(result, as_row(head_gain_ref)).astype(BF16)
    branch_velocity = matmul(headed, head_out_ref[...]).reshape(rows // period, period, width)
    conditional = branch_velocity[:, :share]
    empty = branch_velocity[:, share:]
    out_ref[...] = (empty + GUIDE * (conditional - empty)).astype(BF16)


def whole(memory_space=pltpu.VMEM):
    return pl.BlockSpec(memory_space=memory_space)


def body(
    groups,
    x_state,
    noise_field,
    rotations,
    translations,
    residue_types,
    pocket_mask,
    type_table,
    null_embed,
    spatial_gain,
    spatial_proj,
    spatial_points,
    spatial_gamma,
    spatial_out,
    temporal_gain,
    temporal_proj,
    temporal_out,
    hidden_gain,
    hidden_in,
    hidden_out,
    head_gain,
    head_out,
):
    frames, residues, width = x_state.shape
    share = residues // groups
    period = BRANCHES * share
    sources = (
        x_state,
        type_table,
        residue_types[None],
        null_embed,
        spatial_gain,
        rotations,
        translations,
        pocket_mask[None],
        spatial_proj,
        spatial_out,
        spatial_points.T,
    )
    slots = 2 * (width // LANES)
    later = (temporal_proj, temporal_out, hidden_in, hidden_out, head_out)
    spatial, *later = pl.pallas_call(
        functools.partial(spatial_kernel, groups),
        out_shape=[pltpu.VMEM((groups, frames * period, width), BF16)]
        + [pltpu.VMEM(array.shape, array.dtype) for array in later],
        in_specs=[whole(pltpu.SMEM)] + [whole(pl.ANY)] * (len(sources) + len(later)),
        out_specs=[whole()] * (1 + len(later)),
        scratch_shapes=[pltpu.VMEM(array.shape, array.dtype) for array in sources[:-1]]
        + [
            pltpu.VMEM((slots * SLOT, width), BF16),
            pltpu.VMEM((16, residues), F32),
            pltpu.SemaphoreType.DMA((len(sources) - 1 + slots + len(later),)),
        ],
        compiler_params=pltpu.CompilerParams(vmem_limit_bytes=SPATIAL_VMEM),
        name="spatial",
    )(spatial_gamma, *sources, *later)
    arrived = lax.all_to_all(spatial, "seq", split_axis=0, concat_axis=0, tiled=True)
    proj_local, out_local, in_local, hidden_local, head_local = later
    guided = pl.pallas_call(
        functools.partial(temporal_kernel, period),
        out_shape=pltpu.VMEM((groups * frames, share, width), BF16),
        in_specs=[whole()] * 9,
        out_specs=whole(),
        compiler_params=pltpu.CompilerParams(vmem_limit_bytes=TEMPORAL_VMEM),
        name="temporal",
    )(
        arrived,
        temporal_gain,
        proj_local,
        out_local,
        hidden_gain,
        in_local,
        hidden_local,
        head_gain,
        head_local,
    )
    velocity = lax.all_to_all(guided, "seq", split_axis=0, concat_axis=1, tiled=True)
    x_next = (
        x_state.astype(F32)
        + STEP_SIZE * velocity.astype(F32)
        + NOISE_SCALE * noise_field.astype(F32)
    ).astype(BF16)
    return (x_next, velocity)


def solution(mesh):
    tokens = P(("parts", "seq"), None, None)
    geometry = P(None, ("parts", "seq"), None)
    return jax.shard_map(
        functools.partial(body, mesh.shape["seq"]),
        mesh=mesh,
        in_specs=(tokens, tokens, geometry, geometry, P("parts"), P("parts")) + (P(),) * 15,
        out_specs=(tokens, tokens),
        check_vma=False,
    )
```

```python
import functools
import math

import jax
import jax.numpy as jnp
from jax import lax
from jax.experimental import pallas as pl
from jax.experimental.pallas import tpu as pltpu
from jax.sharding import PartitionSpec as P

THEADS = 6
BRANCHES = 2

WEIGHT_LOGIT = 0.7071067811865476
WEIGHT_POINT = 0.23570226039551584
GUIDE = 2.0
STEP_SIZE = 0.25
NOISE_SCALE = 0.2
EPSILON = 1e-05

BF16 = jnp.bfloat16
F32 = jnp.float32
LANES = 128
SLOT = 64
SPATIAL_VMEM = 56 * 2**20
TEMPORAL_VMEM = 40 * 2**20
NT = (((1,), (1,)), ((), ()))


def layer_norm(values, scale_gain):
    average = jnp.mean(values, axis=-1, keepdims=True)
    centered = values - average
    spread = jnp.mean(centered * centered, axis=-1, keepdims=True)
    return centered * lax.rsqrt(spread + EPSILON) * scale_gain


def as_row(ref):
    return ref[...].reshape(1, ref.shape[0])


def matmul(left, right):
    return jnp.dot(left, right, preferred_element_type=F32)


def iota(shape, axis):
    return lax.broadcasted_iota(jnp.int32, shape, axis)


def softmax_down(logits, allowed):
    logits = jnp.where(allowed, logits, -jnp.inf)
    powers = jnp.exp(logits - jnp.max(logits, axis=0, keepdims=True))
    return powers.astype(BF16), 1.0 / jnp.sum(powers, axis=0, keepdims=True)


def spatial_kernel(groups, gamma_ref, *refs):
    sources, refs = refs[:11], refs[11:]
    later, refs = refs[:5], refs[5:]
    out_ref, later_out, refs = refs[0], refs[1:6], refs[6:]
    local, (columns_ref, sems) = refs[:11], refs[11:]
    (
        x_ref,
        table_ref,
        types_ref,
        null_ref,
        gain_ref,
        rotation_ref,
        translation_ref,
        mask_ref,
        proj_ref,
        spatial_out_ref,
        points_ref,
    ) = local
    frames, residues, width = x_ref.shape
    heads = gamma_ref.shape[0]
    head_dim = width // heads
    blocks = width // LANES
    block_heads = LANES // head_dim
    slot_rows = sources[-1].shape[0] // (2 * blocks)
    per_head = slot_rows // block_heads
    share = residues // groups
    fold = max(residues, LANES)
    stacked_rows = block_heads * residues
    point_scale = 0.5 * WEIGHT_LOGIT * WEIGHT_POINT

    pairs = list(zip(sources[:10], local[:10], strict=True))
    for slot in range(2 * blocks):
        pairs.append(
            (
                sources[-1].at[pl.ds(slot * slot_rows, slot_rows), :],
                points_ref.at[pl.ds(slot * SLOT, slot_rows), :],
            )
        )
    pairs += list(zip(later, later_out, strict=True))
    copies = [
        pltpu.make_async_copy(source, target, sems.at[index])
        for index, (source, target) in enumerate(pairs)
    ]
    first = 10 + 2 * blocks
    for copy in copies[:first]:
        copy.start()
    small, wide = copies[:8], copies[8:first]

    for slot in range(2 * blocks):
        points_ref[slot * SLOT + slot_rows : (slot + 1) * SLOT, :] = jnp.zeros(
            (SLOT - slot_rows, width), BF16
        )
    lane = iota((1, LANES), 1)
    low = lane < SLOT
    place = lane % SLOT
    component = jnp.where(place < slot_rows, place % 3, 3)
    member, block_member = [], []
    for part in range(block_heads):
        member.append((place >= part * per_head) & (place < (part + 1) * per_head))
        block_member.append((lane >= part * head_dim) & (lane < (part + 1) * head_dim))
    both_member = [
        jnp.concatenate([left, right, right], axis=1).astype(F32).astype(BF16)
        for left, right in zip(block_member, member, strict=True)
    ]
    gamma_lanes = []
    for block in range(blocks):
        gamma = jnp.zeros((1, LANES), F32)
        for part in range(block_heads):
            gamma = jnp.where(member[part], gamma_ref[block * block_heads + part], gamma)
        gamma_lanes.append(gamma * point_scale)
    chunks = stacked_rows // fold
    chunk_rows = LANES // chunks
    diagonal = iota((chunk_rows, fold), 0) // head_dim == iota((chunk_rows, fold), 1) // residues
    same = iota((residues, stacked_rows), 0) == iota((residues, stacked_rows), 1) % residues
    columns_ref[...] = jnp.zeros_like(columns_ref)

    for copy in small:
        copy.wait()
    for copy in copies[first:]:
        copy.start()
    kinds = table_ref.shape[0]
    onehot = (iota((kinds, residues), 0) == types_ref[...]).astype(F32).astype(BF16)
    conditional = lax.dot_general(
        onehot, table_ref[...], (((0,), (0,)), ((), ())), preferred_element_type=F32
    )
    empty = as_row(null_ref).astype(F32)

    tiles = []
    for frame in range(frames):
        state = x_ref[frame].astype(F32)
        initial = jnp.concatenate([state + conditional, state + empty], axis=0)
        normed = layer_norm(initial, as_row(gain_ref)).astype(BF16)

        columns_ref[0:9, :] = rotation_ref[:, frame, :]
        moved = translation_ref[:, frame, :]
        columns_ref[9:12, :] = moved - jnp.mean(moved, axis=1, keepdims=True)
        columns_ref[12:13, :] = mask_ref[...].astype(F32)
        columns = columns_ref[...].T
        allowed = (columns[:, 12:13] == 1.0) | same
        factors = []
        for step in range(-2, 3):
            factor = jnp.zeros((residues, LANES), F32)
            for row in range(3):
                if 0 <= row + step < 3:
                    entry = 3 * row + row + step
                    factor = jnp.where(component == row, columns[:, entry : entry + 1], factor)
            factors.append(jnp.concatenate([factor] * BRANCHES, axis=0))
        anchor = jnp.zeros((residues, LANES), F32)
        for row in range(3):
            anchor = jnp.where(component == row, columns[:, 9 + row : 10 + row], anchor)
        anchor = jnp.concatenate([anchor] * BRANCHES, axis=0)

        if frame == 0:
            for copy in wide:
                copy.wait()
        points = lax.dot_general(normed, points_ref[...], NT, preferred_element_type=F32)
        projected = matmul(normed, proj_ref[...])

        slots = []
        for pair in range(blocks):
            lanes = points[:, pair * LANES : (pair + 1) * LANES]
            placed = anchor + factors[2] * lanes
            for step in (-2, -1, 1, 2):
                placed = placed + factors[step + 2] * pltpu.roll(lanes, (-step) % LANES, 1)
            swapped = pltpu.roll(placed, SLOT, 1)
            slots += [jnp.where(low, placed, swapped), jnp.where(low, swapped, placed)]

        query_feature, key_first, key_second = [], [], []
        nothing = jnp.zeros((BRANCHES * residues, LANES), BF16)
        ones = jnp.ones((residues, LANES), BF16)
        for block in range(blocks):
            feature = slots[block] * (2.0 * gamma_lanes[block])
            high = feature.astype(BF16)
            rest = (feature - high.astype(F32)).astype(BF16)
            query_feature.append(jnp.where(low, high, rest))

            feature = slots[blocks + block]
            high = feature.astype(BF16)
            rest = (feature - high.astype(F32)).astype(BF16)
            key_first.append([high])
            key_second.append([jnp.where(low, rest, nothing)])
            square = feature * feature * (-gamma_lanes[block])
            high = square.astype(BF16)
            rest = square - high.astype(F32)
            middle = rest.astype(BF16)
            last = (rest - middle.astype(F32)).astype(BF16)
            key_first[block].append(jnp.where(low, high, middle))
            key_second[block].append(jnp.where(low, last, nothing))

        queries = (
            projected[:, :width].astype(BF16) * jnp.asarray(WEIGHT_LOGIT / math.sqrt(head_dim), BF16)
        )
        keys = projected[:, width : 2 * width].astype(BF16)
        values = projected[:, 2 * width :].astype(BF16)
        turned, logits = [], []
        for branch in range(BRANCHES):
            rows = slice(branch * residues, (branch + 1) * residues)
            turned.append(values[rows].T)
            for block in range(blocks):
                lanes = slice(block * LANES, (block + 1) * LANES)
                left = jnp.concatenate(
                    [
                        jnp.concatenate(
                            [piece[rows] for piece in (keys[:, lanes], *key_first[block])], axis=1
                        ),
                        jnp.concatenate(
                            [piece[rows] for piece in (nothing, *key_second[block])], axis=1
                        ),
                    ],
                    axis=0,
                )
                right = jnp.concatenate(
                    [queries[rows, lanes], query_feature[block][rows], ones], axis=1
                )
                right = jnp.concatenate([right * own for own in both_member], axis=0)
                both = lax.dot_general(left, right, NT, preferred_element_type=F32)
                logits.append(both[:residues] + both[residues:])
        attends = [softmax_down(each, allowed) for each in logits]
        mixes = []
        for index, (powers, _) in enumerate(attends):
            block = index % blocks
            for chunk in range(chunks):
                start = block * LANES + chunk * chunk_rows
                mixes.append(
                    matmul(
                        turned[index // blocks][start : start + chunk_rows],
                        powers[:, chunk * fold : (chunk + 1) * fold],
                    )
                )
        contexts = []
        for branch in range(BRANCHES):
            pieces = []
            for index in range(branch * blocks, (branch + 1) * blocks):
                scale = attends[index][1]
                for chunk in range(chunks):
                    mixed = mixes[index * chunks + chunk]
                    mixed = mixed * scale[:, chunk * fold : (chunk + 1) * fold]
                    pieces.append(jnp.where(diagonal, mixed, 0.0))
            context = jnp.concatenate(pieces, axis=0).astype(BF16).T
            joined = context[:residues]
            for start in range(residues, fold, residues):
                joined = joined + context[start : start + residues]
            contexts.append(joined)
        update = matmul(jnp.concatenate(contexts, axis=0), spatial_out_ref[...])
        total = initial + update
        tiles.append(
            [
                jnp.concatenate(
                    [
                        total[start : start + share]
                        for start in range(group * share, BRANCHES * residues, residues)
                    ],
                    axis=0,
                )
                for group in range(groups)
            ]
        )
    for group in range(groups):
        out_ref[group] = jnp.concatenate([tile[group] for tile in tiles], axis=0).astype(BF16)
    for copy in copies[first:]:
        copy.wait()


def temporal_kernel(
    period,
    x_ref,
    gain_ref,
    proj_ref,
    temporal_out_ref,
    hidden_gain_ref,
    hidden_in_ref,
    hidden_out_ref,
    head_gain_ref,
    head_out_ref,
    out_ref,
):
    groups, depth, width = x_ref.shape
    rows = groups * depth
    head_dim = width // THEADS
    block_heads = LANES // head_dim
    share = period // BRANCHES

    initial = x_ref[...].astype(F32).reshape(rows, width)
    normed = layer_norm(initial, as_row(gain_ref)).astype(BF16)
    projected = matmul(normed, proj_ref[...])
    queries = projected[:, :width].astype(BF16) * jnp.asarray(1.0 / math.sqrt(head_dim), BF16)
    keys = projected[:, width : 2 * width].astype(BF16)
    turned = projected[:, 2 * width :].astype(BF16).T
    block_lane = iota((1, LANES), 1)
    allowed = (
        iota((rows, block_heads * rows), 0) % period == iota((rows, block_heads * rows), 1) % period
    )
    logits = []
    for block in range(width // LANES):
        lanes = slice(block * LANES, (block + 1) * LANES)
        stacked = []
        for part in range(block_heads):
            own = (block_lane >= part * head_dim) & (block_lane < (part + 1) * head_dim)
            stacked.append(queries[:, lanes] * own.astype(F32).astype(BF16))
        logits.append(
            lax.dot_general(
                keys[:, lanes], jnp.concatenate(stacked, axis=0), NT, preferred_element_type=F32
            )
        )
    attends = [softmax_down(each, allowed) for each in logits]
    mixes = []
    for block, (powers, _) in enumerate(attends):
        for part in range(block_heads):
            start = block * LANES + part * head_dim
            lanes = slice(part * rows, (part + 1) * rows)
            mixes.append(matmul(turned[start : start + head_dim], powers[:, lanes]))
    pieces = []
    for index, mixed in enumerate(mixes):
        part = index % block_heads
        pieces.append(mixed * attends[index // block_heads][1][:, part * rows : (part + 1) * rows])
    context = jnp.concatenate(pieces, axis=0).astype(BF16).T
    after_time = initial + matmul(context, temporal_out_ref[...])
    second = layer_norm(after_time, as_row(hidden_gain_ref)).astype(BF16)
    hidden = jax.nn.gelu(matmul(second, hidden_in_ref[...])).astype(BF16)
    result = (after_time + matmul(hidden, hidden_out_ref[...])).astype(BF16).astype(F32)
    headed = layer_norm(result, as_row(head_gain_ref)).astype(BF16)
    branch_velocity = matmul(headed, head_out_ref[...]).reshape(rows // period, period, width)
    conditional = branch_velocity[:, :share]
    empty = branch_velocity[:, share:]
    out_ref[...] = (empty + GUIDE * (conditional - empty)).astype(BF16)


def whole(memory_space=pltpu.VMEM):
    return pl.BlockSpec(memory_space=memory_space)


def body(
    groups,
    x_state,
    noise_field,
    rotations,
    translations,
    residue_types,
    pocket_mask,
    type_table,
    null_embed,
    spatial_gain,
    spatial_proj,
    spatial_points,
    spatial_gamma,
    spatial_out,
    temporal_gain,
    temporal_proj,
    temporal_out,
    hidden_gain,
    hidden_in,
    hidden_out,
    head_gain,
    head_out,
):
    frames, residues, width = x_state.shape
    share = residues // groups
    period = BRANCHES * share
    sources = (
        x_state,
        type_table,
        residue_types[None],
        null_embed,
        spatial_gain,
        rotations,
        translations,
        pocket_mask[None],
        spatial_proj,
        spatial_out,
        spatial_points.T,
    )
    slots = 2 * (width // LANES)
    later = (temporal_proj, temporal_out, hidden_in, hidden_out, head_out)
    spatial, *later = pl.pallas_call(
        functools.partial(spatial_kernel, groups),
        out_shape=[pltpu.VMEM((groups, frames * period, width), BF16)]
        + [pltpu.VMEM(array.shape, array.dtype) for array in later],
        in_specs=[whole(pltpu.SMEM)] + [whole(pl.ANY)] * (len(sources) + len(later)),
        out_specs=[whole()] * (1 + len(later)),
        scratch_shapes=[pltpu.VMEM(array.shape, array.dtype) for array in sources[:-1]]
        + [
            pltpu.VMEM((slots * SLOT, width), BF16),
            pltpu.VMEM((16, residues), F32),
            pltpu.SemaphoreType.DMA((len(sources) - 1 + slots + len(later),)),
        ],
        compiler_params=pltpu.CompilerParams(vmem_limit_bytes=SPATIAL_VMEM),
        name="spatial",
    )(spatial_gamma, *sources, *later)
    arrived = lax.all_to_all(spatial, "seq", split_axis=0, concat_axis=0, tiled=True)
    proj_local, out_local, in_local, hidden_local, head_local = later
    guided = pl.pallas_call(
        functools.partial(temporal_kernel, period),
        out_shape=pltpu.VMEM((groups * frames, share, width), BF16),
        in_specs=[whole()] * 9,
        out_specs=whole(),
        compiler_params=pltpu.CompilerParams(vmem_limit_bytes=TEMPORAL_VMEM),
        name="temporal",
    )(
        arrived,
        temporal_gain,
        proj_local,
        out_local,
        hidden_gain,
        in_local,
        hidden_local,
        head_gain,
        head_local,
    )
    velocity = lax.all_to_all(guided, "seq", split_axis=0, concat_axis=1, tiled=True)
    x_next = (
        x_state.astype(F32)
        + STEP_SIZE * velocity.astype(F32)
        + NOISE_SCALE * noise_field.astype(F32)
    ).astype(BF16)
    return (x_next, velocity)


def solution(mesh):
    tokens = P(("parts", "seq"), None, None)
    geometry = P(None, ("parts", "seq"), None)
    return jax.shard_map(
        functools.partial(body, mesh.shape["seq"]),
        mesh=mesh,
        in_specs=(tokens, tokens, geometry, geometry, P("parts"), P("parts")) + (P(),) * 15,
        out_specs=(tokens, tokens),
        check_vma=False,
    )
```
